32 devices in a mesh: node: 8 (over y, x, core), local: 4 (over z).
Axes of the slice: x: 2, y: 2, z: 4, core: 2. Of those that a mesh axis runs over, the one named last changes fastest.
Arguments:
- tokens: bfloat16 [4096, 4096], P(('node', 'local')), may hold values from -8 to 8
- norm_gain: bfloat16 [4096], replicated, may hold values from 0.25 to 1.75
- routes: int32 [4096, 8], P(('node', 'local')), may hold values from 0 to 31, as said below
- route_gates: float32 [4096, 8], P(('node', 'local')), may hold values from 0.35 to 1
- placement: int32 [32], replicated, may hold values from 0 to 31, each once
- gate_weight: bfloat16 [32, 4096, 768], P(('node', 'local')), may hold values from -0.09375 to 0.09375
- up_weight: bfloat16 [32, 4096, 768], P(('node', 'local')), may hold values from -0.09375 to 0.09375
- down_weight: bfloat16 [32, 768, 4096], P(('node', 'local')), may hold values from -0.21875 to 0.21875
Outputs:
- moe_output: bfloat16 [4096, 4096], P(('node', 'local'))
The draws below stay inside these ranges and needn't reach their ends.
Inputs may be any that keep to these rules, and one draw needn't show every extreme that they name: `routes`: each token names 8 different experts. In every aligned block of 32 tokens of one device, each expert is named at most 12 times; at every block position some expert is named exactly 12 times by that block of every device.
All inputs are finite; a program needn't handle non-finite values.
Results may differ from the reference program's by a relative error of at most 0.0076.
Values may be sent and summed in bfloat16 or wider, within the bound.
No kernel may reach another device: no remote copies, remote signals or barrier semaphores. Data moves between devices by JAX's collectives and lax.ppermute only.
A program may use at most 128 MiB of HBM per device.

```python
import math
import jax
import jax.numpy as jnp
from jax import lax

D = 4096
TOPK = 8
HID = 768
BLOCKS = 4
BLOCK_TOK = 32
TOKENS = 4096
EXPERTS = 32
CAP = 12


def draw_tokens(key, part):
    key = jax.random.fold_in(key, 5)
    first_key, second_key, third_key = jax.random.split(key, 3)
    basic = jax.random.normal(first_key, (TOKENS, D), jnp.float32)
    columns = jnp.exp(jax.random.uniform(second_key, (D,), jnp.float32, math.log(0.5), math.log(5.0)))
    row_scale = jnp.exp(jax.random.uniform(third_key, (TOKENS, 1), jnp.float32, math.log(0.5), math.log(2.0)))
    return jnp.clip(basic * columns[None, :] * row_scale, -8.0, 8.0).astype(jnp.bfloat16)


def draw_routes(key, part):
    key = jax.random.fold_in(key, 11)
    groups = TOKENS // BLOCK_TOK
    per_expert = BLOCK_TOK * TOPK // EXPERTS
    spare = CAP - per_expert
    hot_base = jax.random.fold_in(key, 7)
    expert_ids = jnp.arange(EXPERTS, dtype=jnp.int32)
    list_pos = jnp.arange(BLOCK_TOK * TOPK, dtype=jnp.int32)

    def one_block(group):
        block_key = jax.random.fold_in(key, group)
        hot_key = jax.random.fold_in(hot_base, group % BLOCKS)
        hot = jax.random.randint(hot_key, (), 0, EXPERTS, dtype=jnp.int32)
        raise_key, offset_key, shuffle_key = jax.random.split(block_key, 3)
        raised = jax.random.randint(raise_key, (EXPERTS,), 0, spare + 1, dtype=jnp.int32)
        offset = jax.random.randint(offset_key, (), 1, EXPERTS, dtype=jnp.int32)
        partner = (hot + offset) % EXPERTS
        raised = jnp.where(expert_ids == hot, spare, raised)
        raised = jnp.where(expert_ids == partner, 0, raised)
        counts = per_expert + raised - jnp.take(raised, (expert_ids + offset) % EXPERTS)
        shuffle = jax.random.permutation(shuffle_key, EXPERTS).astype(jnp.int32)
        bounds = jnp.cumsum(jnp.take(counts, shuffle))
        which = jnp.sum((bounds[None, :] <= list_pos[:, None]).astype(jnp.int32), axis=1)
        listed = jnp.take(shuffle, which)
        return listed.reshape(TOPK, BLOCK_TOK).T
    blocks_all = jax.vmap(one_block)(jnp.arange(groups, dtype=jnp.int32))
    return blocks_all.reshape(TOKENS, TOPK).astype(jnp.int32)


def shard_levels(key, extent, pieces, low, top_value):
    factor_of, own = 1.0, jax.random.fold_in(key, 6)
    for axis_at, shards_of in pieces:
        steps = jnp.exp(jax.random.uniform(jax.random.fold_in(own, axis_at), (shards_of,), jnp.float32, low / len(pieces), top_value / len(pieces)))
        factor_of = factor_of * jnp.repeat(steps, extent[axis_at] // shards_of).reshape([-1 if axis == axis_at else 1 for axis in range(len(extent))])
    return factor_of


def scatter_about(own_key, dims, spread, limit, cuts=(), kind=jnp.bfloat16):
    array = jax.random.normal(own_key, dims, jnp.float32) * spread
    if len(cuts) > 0:
        array = shard_levels(own_key, dims, cuts, -0.22, 0.18) * array
    return jnp.clip(array, min=-limit, max=limit).astype(kind)


def setup_inputs(seed: int = 0) -> dict:
    arg_keys = jax.random.split(jax.random.key(seed), 9)
    tokens = draw_tokens(jax.random.fold_in(arg_keys[8], 71), 0)
    norm_gain = jnp.clip(1.0 + 0.15 * jax.random.normal(arg_keys[1], (D,), jnp.float32), 0.25, 1.75).astype(jnp.bfloat16)
    routes = draw_routes(jax.random.fold_in(arg_keys[8], 71), 0)
    route_gates = jnp.clip(jnp.exp(math.log(1.0) - 1.0498221 * jax.random.uniform(arg_keys[3], (TOKENS, TOPK), jnp.float32) ** shard_levels(arg_keys[3], (TOKENS, TOPK), ((0, 32),), -0.2, 0.2)), 0.35, 1.0)
    placement = jax.random.permutation(arg_keys[4], EXPERTS).astype(jnp.int32)
    gate_weight = scatter_about(arg_keys[5], (EXPERTS, D, HID), D ** -0.5, 0.09375, ((0, 32),))
    up_weight = scatter_about(arg_keys[6], (EXPERTS, D, HID), D ** -0.5, 0.09375, ((0, 32),))
    down_weight = scatter_about(arg_keys[7], (EXPERTS, HID, D), HID ** -0.5, 0.21875, ((0, 32),))
    return dict(tokens=tokens, norm_gain=norm_gain, routes=routes, route_gates=route_gates, placement=placement, gate_weight=gate_weight, up_weight=up_weight, down_weight=down_weight)


def reference(tokens, norm_gain, routes, route_gates, placement, gate_weight, up_weight, down_weight):
    values = tokens.astype(jnp.float32)
    rescale = lax.rsqrt(lax.optimization_barrier(jnp.mean(values * values, axis=-1, keepdims=True)) + 1e-06)
    normed = (values * rescale * norm_gain.astype(jnp.float32)).astype(jnp.bfloat16)
    combine_weight = (route_gates / lax.optimization_barrier(jnp.sum(route_gates, axis=-1, keepdims=True))).astype(jnp.bfloat16)
    groups = TOKENS // BLOCK_TOK
    flat_ids = routes.reshape(groups, BLOCK_TOK * TOPK)
    expert_ids = jnp.arange(EXPERTS, dtype=jnp.int32)
    matches = (flat_ids[:, :, None] == expert_ids[None, None, :]).astype(jnp.int32)
    position = lax.optimization_barrier(jnp.sum((jnp.cumsum(matches, axis=1) - matches) * matches, axis=-1)).astype(jnp.int32)
    group_ids = jnp.arange(groups, dtype=jnp.int32)[:, None]
    token_ids = group_ids * BLOCK_TOK + jnp.arange(BLOCK_TOK * TOPK, dtype=jnp.int32)[None, :] // TOPK
    row_slots = (group_ids * CAP + position).astype(jnp.int32)
    source = jnp.full((EXPERTS, groups * CAP), TOKENS, jnp.int32).at[flat_ids, row_slots].set(token_ids)
    shares = jnp.zeros((EXPERTS, groups * CAP), jnp.float32).at[flat_ids, row_slots].set(combine_weight.reshape(groups, BLOCK_TOK * TOPK).astype(jnp.float32))
    padded = jnp.concatenate([normed, jnp.zeros((1, D), jnp.bfloat16)], axis=0)

    def apply_expert(running, stacked):
        gate_mat, up_mat, down_mat, expert = stacked
        row_index = source[expert]
        picked = padded[row_index]
        gate_pre = jnp.dot(picked, gate_mat, preferred_element_type=jnp.float32)
        up_pre = jnp.dot(picked, up_mat, preferred_element_type=jnp.float32)
        hidden = (jax.nn.silu(gate_pre) * up_pre).astype(jnp.bfloat16)
        expert_out = jnp.dot(hidden, down_mat, preferred_element_type=jnp.float32).astype(jnp.bfloat16)
        running = running.at[row_index].add(shares[expert][:, None] * expert_out.astype(jnp.float32))
        return (running, None)
    running, _ = lax.scan(apply_expert, jnp.zeros((TOKENS + 1, D), jnp.float32), (gate_weight, up_weight, down_weight, placement))
    return running[:TOKENS].astype(jnp.bfloat16)
```

```python
import jax
import jax.numpy as jnp
from jax import lax
from jax.sharding import PartitionSpec as P

BLOCK_TOK = 32
EPSILON = 1e-06
AXES = ("node", "local")


def body(tokens, norm_gain, routes, route_gates, placement, gate_weight, up_weight, down_weight):
    nodes, locals_ = lax.axis_size("node"), lax.axis_size("local")
    experts = placement.shape[0]
    tok_rows, features = tokens.shape
    top_count = routes.shape[1]
    blocks = tok_rows // BLOCK_TOK
    capacity = BLOCK_TOK * top_count // experts * 3 // 2
    slots = nodes * locals_ * capacity
    values = tokens.astype(jnp.float32)
    rescale = lax.rsqrt(jnp.mean(values * values, axis=-1, keepdims=True) + EPSILON)
    normed = (values * rescale * norm_gain.astype(jnp.float32)).astype(jnp.bfloat16)
    combine_weight = (route_gates / jnp.sum(route_gates, axis=-1, keepdims=True)).astype(
        jnp.bfloat16
    )
    held = routes[:, :, None] == placement[None, None, :]
    table = jnp.sum(
        jnp.where(held, combine_weight[:, :, None], jnp.zeros((), jnp.bfloat16)), axis=1
    )
    column = lax.all_gather(table, "local", axis=0, tiled=True)
    column = column.reshape(locals_, blocks, BLOCK_TOK, nodes, locals_)
    mine = lax.dynamic_index_in_dim(column, lax.axis_index("local"), 4, keepdims=False)
    mask = (mine > 0).astype(jnp.int32)
    rank = jnp.cumsum(mask, axis=2) - mask
    first = (
        jnp.arange(nodes, dtype=jnp.int32)[None, :] * locals_
        + jnp.arange(locals_, dtype=jnp.int32)[:, None]
    ) * capacity
    place = jnp.where(mask > 0, rank + first[:, None, None, :], -1)
    slot_ids = jnp.arange(slots, dtype=jnp.int32)
    matched = place[..., None] == slot_ids
    spread = jnp.any(matched, axis=3).astype(jnp.bfloat16)
    mixing = jnp.sum(
        jnp.where(matched, mine[..., None], jnp.zeros((), jnp.bfloat16)), axis=3
    )
    pieces = []
    for block in range(blocks):
        rows = normed[block * BLOCK_TOK : (block + 1) * BLOCK_TOK]
        gathered = lax.all_gather(rows, "local", axis=0, tiled=True)
        outbound = jnp.einsum(
            "ts,td->sd",
            spread[:, block].reshape(-1, slots),
            gathered,
            preferred_element_type=jnp.float32,
        ).astype(jnp.bfloat16)
        arrived = lax.all_to_all(outbound, "node", 0, 0, tiled=True)
        gate_pre = jnp.dot(arrived, gate_weight[0], preferred_element_type=jnp.float32)
        up_pre = jnp.dot(arrived, up_weight[0], preferred_element_type=jnp.float32)
        hidden = (jax.nn.silu(gate_pre) * up_pre).astype(jnp.bfloat16)
        out = jnp.dot(hidden, down_weight[0], preferred_element_type=jnp.float32).astype(jnp.bfloat16)
        landed = lax.all_to_all(out, "node", 0, 0, tiled=True)
        mixed = jnp.dot(
            mixing[:, block].reshape(-1, slots), landed, preferred_element_type=jnp.float32
        ).astype(jnp.bfloat16)
        pieces.append(lax.psum_scatter(mixed, "local", scatter_dimension=0, tiled=True))
    return jnp.concatenate(pieces, axis=0)


def solution(mesh):
    rows = P(AXES, None)
    stacked = P(AXES, None, None)
    in_specs = (rows, P(), rows, rows, P(), stacked, stacked, stacked)
    return jax.shard_map(body, mesh=mesh, in_specs=in_specs, out_specs=rows, check_vma=False)
```

```python
import jax
import jax.numpy as jnp
import numpy as np
from jax import lax
from jax.experimental import pallas as pl
from jax.experimental.pallas import tpu as pltpu
from jax.sharding import PartitionSpec as P

BLOCK_TOK = 32
EPSILON = 1e-06
AXES = ("node", "local")
LANES = 128
BF16, F32 = jnp.bfloat16, jnp.float32


def fence(*arrays):
    def kernel(*refs):
        pass

    anywhere = pl.BlockSpec(memory_space=pl.ANY)
    return pl.pallas_call(
        kernel,
        out_shape=[jax.ShapeDtypeStruct(a.shape, a.dtype) for a in arrays],
        in_specs=[anywhere] * len(arrays),
        out_specs=[anywhere] * len(arrays),
        input_output_aliases={i: i for i in range(len(arrays))},
    )(*arrays)


def swap(array, axis, bits):
    size = lax.axis_size(axis)
    return lax.ppermute(array, axis, [(i, i ^ bits) for i in range(size)])


def swaps(parts, axis, first, last):
    return [swap(parts[k], axis, k) for k in range(first, last)]


def bit_order(size, last_first):
    bits = [1 << i for i in range(size.bit_length() - 1)]
    return bits[:1] + bits[:0:-1] if last_first else bits


def gather_doubling(array, axis, bits):
    for bit in bits:
        array = jnp.concatenate([array, swap(array, axis, bit)])
    return array


def gathered_from(bits):
    found = [0]
    for bit in bits:
        found += [k ^ bit for k in found]
    return np.array(found)


def sum_halving(array, axis, bits):
    for bit in bits[::-1]:
        keep, give = jnp.split(array, 2)
        array = keep + swap(give.astype(BF16), axis, bit).astype(F32)
    return array.astype(BF16)


def relative(array, axis, dim):
    size = lax.axis_size(axis)
    order = jnp.arange(size, dtype=jnp.int32) ^ lax.axis_index(axis)
    pick = (order[:, None] == jnp.arange(size, dtype=jnp.int32)).astype(array.dtype)
    return jnp.moveaxis(jnp.tensordot(pick, array, ((1,), (dim,))), 0, dim)


def tables(known, capacity, gather_axis, exchange_axis, by_bits):
    group, peers = lax.axis_size(gather_axis), lax.axis_size(exchange_axis)
    experts = group * peers
    slots = experts * capacity
    known = known[:, :experts].reshape(
        group, BLOCK_TOK, lax.axis_size("node"), lax.axis_size("local")
    )
    at = 3 if gather_axis == "local" else 2
    known = lax.dynamic_index_in_dim(known, lax.axis_index(gather_axis), at, keepdims=False)
    if by_bits:
        known = relative(known, exchange_axis, 2)
    mask = (known > 0).astype(jnp.int32)
    rank = jnp.cumsum(mask, axis=1) - mask
    first = (
        jnp.arange(peers, dtype=jnp.int32)[None, :] * group
        + jnp.arange(group, dtype=jnp.int32)[:, None]
    ) * capacity
    place = jnp.where(mask > 0, rank + first[:, None, :], -1)
    matched = place[..., None] == jnp.arange(slots, dtype=jnp.int32)
    spread = jnp.any(matched, axis=2).astype(BF16)
    mixing = jnp.sum(jnp.where(matched, known[..., None], jnp.zeros((), BF16)), axis=2)
    return spread, mixing


def pick_rows(spread, rows):
    flat = spread.reshape(-1, spread.shape[-1])
    return jnp.einsum("ts,td->sd", flat, rows, preferred_element_type=F32).astype(BF16)


def mix_rows(mixing, landed):
    flat = mixing.reshape(-1, mixing.shape[-1])
    return jnp.dot(flat, landed, preferred_element_type=F32)


def expert_kernel(x_ref, gate_ref, up_ref, down_ref, out_ref, total):
    step = pl.program_id(0)
    x = x_ref[...]
    gate_pre = jnp.dot(x, gate_ref[...], preferred_element_type=F32)
    up_pre = jnp.dot(x, up_ref[...], preferred_element_type=F32)
    hidden = (gate_pre / (1 + jnp.exp(-gate_pre)) * up_pre).astype(BF16)
    part = jnp.dot(hidden, down_ref[...], preferred_element_type=F32)

    @pl.when(step == 0)
    def _():
        total[...] = part

    @pl.when(step > 0)
    def _():
        total[...] += part

    @pl.when(step == pl.num_programs(0) - 1)
    def _():
        out_ref[...] = total[...].astype(BF16)


def expert(arrived, gate_weight, up_weight, down_weight):
    rows, features = arrived.shape
    hidden = gate_weight.shape[1]
    tile = 256
    return pl.pallas_call(
        expert_kernel,
        grid=(hidden // tile,),
        out_shape=jax.ShapeDtypeStruct((rows, features), BF16),
        in_specs=[
            pl.BlockSpec((rows, features), lambda i: (0, 0)),
            pl.BlockSpec((features, tile), lambda i: (0, i)),
            pl.BlockSpec((features, tile), lambda i: (0, i)),
            pl.BlockSpec((tile, features), lambda i: (i, 0)),
        ],
        out_specs=pl.BlockSpec((rows, features), lambda i: (0, 0)),
        scratch_shapes=[pltpu.VMEM((rows, features), F32)],
        compiler_params=pltpu.CompilerParams(vmem_limit_bytes=44 * 2**20),
        cost_estimate=pl.CostEstimate(
            flops=6 * rows * features * hidden,
            bytes_accessed=6 * features * hidden + 4 * rows * features,
            transcendentals=rows * hidden,
        ),
    )(arrived, gate_weight, up_weight, down_weight)


def to_experts(rows):
    return lax.all_to_all(rows, "node", 0, 0, tiled=True)


def body(tokens, norm_gain, routes, route_gates, placement, gate_weight, up_weight, down_weight):
    experts = placement.shape[0]
    tok_rows, features = tokens.shape
    top_count = routes.shape[1]
    capacity = BLOCK_TOK * top_count // experts * 3 // 2
    half = features // 2
    values = tokens.astype(F32)
    rescale = lax.rsqrt(jnp.mean(values * values, axis=-1, keepdims=True) + EPSILON)
    normed = (values * rescale * norm_gain.astype(F32)).astype(BF16)
    combine_weight = (route_gates / jnp.sum(route_gates, axis=-1, keepdims=True)).astype(BF16)
    held = routes[:, :, None] == placement[None, None, :]
    table = jnp.sum(jnp.where(held, combine_weight[:, :, None], jnp.zeros((), BF16)), axis=1)
    weights = (gate_weight[0], up_weight[0], down_weight[0])
    sent = jnp.concatenate([normed, jnp.pad(table, ((0, 0), (0, -experts % LANES)))], axis=1)
    sent0, sent1, sent2, sent3 = jnp.split(sent, tok_rows // BLOCK_TOK)

    peers = lax.axis_size("local")
    cut = max(peers - 1, 1)

    def gather(rows, first, last):
        return swaps([rows] * peers, "local", first, last)

    def along_local(parts):
        gathered = jnp.concatenate(parts)
        spread, mixing = tables(gathered[:, features:], capacity, "local", "node", False)
        return pick_rows(spread, gathered[:, :features]), mixing

    def sums_out(mixed):
        own, *parts = jnp.split(mixed, peers)
        return own, [part.astype(BF16) for part in parts]

    def total(own, parts):
        for part in parts:
            own = own + part.astype(F32)
        return own.astype(BF16)

    nodes = lax.axis_size("node")
    bits_a, bits_b = bit_order(nodes, False), bit_order(nodes, True)
    order_a, order_b = gathered_from(bits_a), gathered_from(bits_b)
    near0 = gather(sent0, 1, peers)
    near = jnp.concatenate([sent3, swap(sent3, "node", bits_a[0])])
    rows_a = gather_doubling(near[:, :half], "node", bits_a[1:])
    rows_b = gather_doubling(near[:, half:], "node", bits_b[1:])
    back = np.argsort(order_b)
    known = rows_b[:, half:].reshape(nodes, BLOCK_TOK, -1)
    known = jnp.concatenate([known[int(k)] for k in back])
    spread3, mixing3 = tables(known, capacity, "node", "local", True)
    spread3b = jnp.stack([spread3[int(k)] for k in order_b])
    mixing3b = jnp.stack([mixing3[int(k)] for k in order_b])
    sent1, *near0 = fence(sent1, *near0)
    near1 = gather(sent1, 1, cut)
    outbound0, mixing0 = along_local([sent0] + near0)
    outbound3 = jnp.concatenate(
        [pick_rows(spread3, rows_a), pick_rows(spread3b, rows_b[:, :half])], axis=1
    )

    outbound0, outbound3, sent1, sent2, *near1 = fence(outbound0, outbound3, sent1, sent2, *near1)
    arrived0 = to_experts(outbound0)
    near1 += gather(sent1, cut, peers)
    own3, *parts = jnp.split(outbound3, peers)
    arrived3 = swaps([own3] + parts, "local", 1, cut)
    outbound1, mixing1 = along_local([sent1] + near1)

    arrived0, outbound1, sent2, last3, *arrived3 = fence(
        arrived0, outbound1, sent2, parts[-1], *arrived3
    )
    arrived1 = to_experts(outbound1)
    near2 = gather(sent2, 1, peers)
    last3 = jnp.split(last3, 2)
    arrived3.append(swap(last3[0], "local", peers - 1))
    out0 = expert(arrived0, *weights)
    out0, sent2, *near2 = fence(out0, sent2, *near2)
    outbound2, mixing2 = along_local([sent2] + near2)

    arrived1, outbound2, out0, last3, *arrived3 = fence(
        arrived1, outbound2, out0, last3[1], *arrived3
    )
    arrived2 = to_experts(outbound2)
    arrived3.append(swap(last3, "local", peers - 1))
    out1 = expert(arrived1, *weights)
    out1, *arrived3 = fence(out1, *arrived3)
    out3 = expert(jnp.concatenate([own3] + arrived3), *weights)

    arrived2, out0, out1, out3 = fence(arrived2, out0, out1, out3)
    landed0 = to_experts(out0)
    own3, *parts = jnp.split(out3, peers)
    landed3 = swaps([own3] + parts, "local", 1, cut)
    out2 = expert(arrived2, *weights)

    landed0, out1, out2, last3, *landed3 = fence(landed0, out1, out2, parts[-1], *landed3)
    landed1 = to_experts(out1)
    last3 = jnp.split(last3, 2)
    landed3.append(swap(last3[0], "local", peers - 1))
    sum0, parts0 = sums_out(mix_rows(mixing0, landed0))
    parts0 = swaps([None] + parts0, "local", 1, peers)

    landed1, out2, last3, *rest = fence(landed1, out2, last3[1], *landed3, *parts0)
    landed3, parts0 = rest[: len(landed3)], rest[len(landed3) :]
    landed2 = to_experts(out2)
    landed3.append(swap(last3, "local", peers - 1))
    piece0 = total(sum0, parts0)
    sum1, parts1 = sums_out(mix_rows(mixing1, landed1))
    parts1 = swaps([None] + parts1, "local", 1, peers)
    landed3 = jnp.concatenate([own3] + landed3)
    mixed3a = mix_rows(mixing3, landed3[:, :half])
    mixed3b = mix_rows(mixing3b, landed3[:, half:])

    landed2, mixed3a, mixed3b, piece0, *parts1 = fence(
        landed2, mixed3a, mixed3b, piece0, *parts1
    )
    sum2, parts2 = sums_out(mix_rows(mixing2, landed2))
    mixed3a, mixed3b, *parts2 = fence(mixed3a, mixed3b, *parts2)
    parts2 = swaps([None] + parts2, "local", 1, peers)
    piece1 = total(sum1, parts1)
    piece3 = jnp.concatenate(
        [sum_halving(mixed3a, "node", bits_a), sum_halving(mixed3b, "node", bits_b)], axis=1
    )
    piece2 = total(sum2, parts2)
    return jnp.concatenate([piece0, piece1, piece2, piece3], axis=0)


def solution(mesh):
    rows = P(AXES, None)
    stacked = P(AXES, None, None)
    in_specs = (rows, P(), rows, rows, P(), stacked, stacked, stacked)
    return jax.shard_map(body, mesh=mesh, in_specs=in_specs, out_specs=rows, check_vma=False)
```

```python
import functools

import jax
import jax.numpy as jnp
import numpy as np
from jax import lax
from jax.experimental import pallas as pl
from jax.experimental.pallas import tpu as pltpu
from jax.sharding import PartitionSpec as P

BLOCK_TOK = 32
EPSILON = 1e-06
AXES = ("node", "local")
LANES = 128
TILES = 4
BF16, F32, I32 = jnp.bfloat16, jnp.float32, jnp.int32
ANYWHERE = pl.BlockSpec(memory_space=pl.ANY)
PARAMS = pltpu.CompilerParams(vmem_limit_bytes=60 * 2**20)


def fence(arrays, after):
    token = sum(a[:16, :LANES].astype(F32) for a in after)

    def kernel(*refs):
        pass

    return pl.pallas_call(
        kernel,
        out_shape=[jax.ShapeDtypeStruct(a.shape, a.dtype) for a in arrays],
        in_specs=[ANYWHERE] * (len(arrays) + 1),
        out_specs=[ANYWHERE] * len(arrays),
        input_output_aliases={i: i for i in range(len(arrays))},
    )(*arrays, token)


def swap(array, axis, bits):
    size = lax.axis_size(axis)
    return lax.ppermute(array, axis, [(i, i ^ bits) for i in range(size)])


def swaps(parts, axis, first, last):
    return [swap(parts[k], axis, k) for k in range(first, last)]


def bit_order(size, last_first):
    bits = [1 << i for i in range(size.bit_length() - 1)]
    return bits[:1] + bits[:0:-1] if last_first else bits


def gather_doubling(array, axis, bits):
    for bit in bits:
        array = jnp.concatenate([array, swap(array, axis, bit)])
    return array


def gathered_from(bits):
    found = [0]
    for bit in bits:
        found += [k ^ bit for k in found]
    return found


def sum_halving(keep, give, axis, bits):
    for step, bit in enumerate(bits[::-1]):
        if step:
            keep, give = jnp.split(keep, 2)
        keep = keep + swap(give.astype(BF16), axis, bit).astype(F32)
    return keep.astype(BF16)


def below(rows):
    at = np.arange(rows)
    same = at[:, None] // BLOCK_TOK == at[None, :] // BLOCK_TOK
    return jnp.asarray((same & (at[None, :] < at[:, None])).astype(np.float32), BF16)


def choose(table, lane, own, turn, before):
    select = lax.broadcasted_iota(I32, (table.shape[1], lane.shape[1]), 0) == lane
    weight = jnp.dot(table, select.astype(BF16), preferred_element_type=F32)
    mask = jnp.where(weight > 0, own.astype(F32), 0.0)
    rank = jnp.dot(before, mask.astype(BF16), preferred_element_type=F32)
    place = jnp.where(rank == turn, mask, 0.0)
    return place.astype(BF16), (place * weight).astype(BF16)


def gather_rows(place, rows):
    return lax.dot_general(
        place, rows, (((0,), (0,)), ((), ())), preferred_element_type=F32
    ).astype(BF16)


def pick_kernel(count, *refs):
    parts, refs = refs[:count], refs[count:]
    tables, refs = refs[:count], refs[count:]
    lane, own, turn, before, out, mixing, place = refs

    @pl.when(pl.program_id(0) == 0)
    def _():
        table = jnp.concatenate([t[...] for t in tables])
        place[...], mixing[...] = choose(table, lane[...], own[...], turn[...], before[...])

    out[...] = gather_rows(place[...], jnp.concatenate([p[...] for p in parts]))


def whole_block(array):
    return pl.BlockSpec(array.shape, lambda j: (0,) * array.ndim)


def pick(parts, lane, own, turn, features):
    slots = lane.shape[1]
    rows = len(parts) * BLOCK_TOK
    tile = features // TILES
    before = below(rows)
    small = (lane, own, turn, before)
    return pl.pallas_call(
        functools.partial(pick_kernel, len(parts)),
        grid=(TILES,),
        out_shape=[
            jax.ShapeDtypeStruct((slots, features), BF16),
            jax.ShapeDtypeStruct((rows, slots), BF16),
        ],
        in_specs=[pl.BlockSpec((BLOCK_TOK, tile), lambda j: (0, j))] * len(parts)
        + [pl.BlockSpec((BLOCK_TOK, LANES), lambda j: (0, features // LANES))] * len(parts)
        + [whole_block(a) for a in small],
        out_specs=[
            pl.BlockSpec((slots, tile), lambda j: (0, j)),
            pl.BlockSpec((rows, slots), lambda j: (0, 0)),
        ],
        scratch_shapes=[pltpu.VMEM((rows, slots), BF16)],
        compiler_params=PARAMS,
        cost_estimate=pl.CostEstimate(
            flops=2 * rows * slots * features,
            bytes_accessed=2 * (rows + slots) * features,
            transcendentals=0,
        ),
    )(*parts, *parts, *small)


def pick_cross_kernel(order, cuts, a_ref, b_ref, table, lane, own_a, own_b, turn, before, *refs):
    outs, (mixing_a, mixing_b, place_a, place_b) = refs[:-4], refs[-4:]
    step = pl.program_id(0)

    @pl.when(step == 0)
    def _():
        known = table[...]
        place_b[...], mixing_b[...] = choose(known, lane[...], own_b[...], turn[...], before[...])
        back = [order.index(k) * BLOCK_TOK for k in range(len(order))]
        known = jnp.concatenate([known[at : at + BLOCK_TOK] for at in back])
        place_a[...], mixing_a[...] = choose(known, lane[...], own_a[...], turn[...], before[...])

    def store(place, rows):
        result = gather_rows(place, rows)
        for out, first, last in zip(outs, cuts[:-1], cuts[1:]):
            out[...] = result[first:last]

    @pl.when(step < TILES // 2)
    def _():
        store(place_a[...], a_ref[...])

    @pl.when(step >= TILES // 2)
    def _():
        store(place_b[...], b_ref[...])


def in_first_half(shape):
    return pl.BlockSpec(shape, lambda j: (0, jnp.minimum(j, TILES // 2 - 1)))


def in_second_half(shape):
    return pl.BlockSpec(shape, lambda j: (0, jnp.maximum(j - TILES // 2, 0)))


def pick_cross(rows_a, rows_b, order_b, lane, own_a, own_b, turn, features, cuts):
    slots = lane.shape[1]
    rows = rows_a.shape[0]
    tile = features // TILES
    small = (lane, own_a, own_b, turn, below(rows))
    sizes = [last - first for first, last in zip(cuts[:-1], cuts[1:])]
    results = pl.pallas_call(
        functools.partial(pick_cross_kernel, order_b, cuts),
        grid=(TILES,),
        out_shape=[jax.ShapeDtypeStruct((size, features), BF16) for size in sizes]
        + [jax.ShapeDtypeStruct((rows, slots), BF16)] * 2,
        in_specs=[
            in_first_half((rows, tile)),
            in_second_half((rows, tile)),
            pl.BlockSpec((rows, LANES), lambda j: (0, features // 2 // LANES)),
        ]
        + [whole_block(a) for a in small],
        out_specs=[pl.BlockSpec((size, tile), lambda j: (0, j)) for size in sizes]
        + [pl.BlockSpec((rows, slots), lambda j: (0, 0))] * 2,
        scratch_shapes=[pltpu.VMEM((rows, slots), BF16)] * 2,
        compiler_params=PARAMS,
        cost_estimate=pl.CostEstimate(
            flops=2 * rows * slots * features,
            bytes_accessed=2 * (rows + slots) * features,
            transcendentals=0,
        ),
    )(rows_a, rows_b, rows_b, *small)
    return list(results[:-2]), results[-2], results[-1]


def mix_kernel(mixing, landed, own, *outs):
    result = jnp.dot(mixing[...], landed[...], preferred_element_type=F32)
    own[...] = result[:BLOCK_TOK]
    for k, out in enumerate(outs):
        out[...] = result[(k + 1) * BLOCK_TOK : (k + 2) * BLOCK_TOK].astype(BF16)


def mix(mixing, landed):
    rows, slots = mixing.shape
    features = landed.shape[1]
    tile = features // TILES
    count = rows // BLOCK_TOK
    own, *parts = pl.pallas_call(
        mix_kernel,
        grid=(TILES,),
        out_shape=[jax.ShapeDtypeStruct((BLOCK_TOK, features), F32)]
        + [jax.ShapeDtypeStruct((BLOCK_TOK, features), BF16)] * (count - 1),
        in_specs=[whole_block(mixing), pl.BlockSpec((slots, tile), lambda j: (0, j))],
        out_specs=[pl.BlockSpec((BLOCK_TOK, tile), lambda j: (0, j))] * count,
        compiler_params=PARAMS,
        cost_estimate=pl.CostEstimate(
            flops=2 * rows * slots * features,
            bytes_accessed=2 * (rows + slots) * features,
            transcendentals=0,
        ),
    )(mixing, landed)
    return own, [None] + parts


def mix_cross_kernel(mixing_a, mixing_b, *refs):
    landed, (keep_a, give_a, keep_b, give_b) = refs[:-4], refs[-4:]
    step = pl.program_id(0)
    half = keep_a.shape[0]
    rows = jnp.concatenate([part[...] for part in landed])

    def store(mixing, keep, give):
        result = jnp.dot(mixing[...], rows, preferred_element_type=F32)
        keep[...] = result[:half]
        give[...] = result[half:].astype(BF16)

    @pl.when(step < TILES // 2)
    def _():
        store(mixing_a, keep_a, give_a)

    @pl.when(step >= TILES // 2)
    def _():
        store(mixing_b, keep_b, give_b)


def mix_cross(mixing_a, mixing_b, landed):
    rows, slots = mixing_a.shape
    features = landed[0].shape[1]
    tile = features // TILES
    shape = (rows // 2, features // 2)
    return pl.pallas_call(
        mix_cross_kernel,
        grid=(TILES,),
        out_shape=[jax.ShapeDtypeStruct(shape, F32), jax.ShapeDtypeStruct(shape, BF16)] * 2,
        in_specs=[whole_block(mixing_a), whole_block(mixing_b)]
        + [pl.BlockSpec((part.shape[0], tile), lambda j: (0, j)) for part in landed],
        out_specs=[in_first_half((rows // 2, tile))] * 2 + [in_second_half((rows // 2, tile))] * 2,
        compiler_params=PARAMS,
        cost_estimate=pl.CostEstimate(
            flops=2 * rows * slots * features,
            bytes_accessed=2 * (rows + slots) * features,
            transcendentals=0,
        ),
    )(mixing_a, mixing_b, *landed)


def expert_kernel(count, *refs):
    parts, (gate_ref, up_ref, down_ref), outs = refs[:count], refs[count : count + 3], refs[count + 3 : -2]
    x_ref, total = refs[-2:]
    step = pl.program_id(0)

    @pl.when(step == 0)
    def _():
        x_ref[...] = jnp.concatenate([part[...] for part in parts])

    x = x_ref[...]
    gate_pre = jnp.dot(x, gate_ref[...], preferred_element_type=F32)
    up_pre = jnp.dot(x, up_ref[...], preferred_element_type=F32)
    hidden = (gate_pre / (1 + jnp.exp(-gate_pre)) * up_pre).astype(BF16)
    part = jnp.dot(hidden, down_ref[...], preferred_element_type=F32)

    @pl.when(step == 0)
    def _():
        total[...] = part

    @pl.when(step > 0)
    def _():
        total[...] += part

    @pl.when(step == pl.num_programs(0) - 1)
    def _():
        at = 0
        for out in outs:
            out[...] = total[at : at + out.shape[0]].astype(BF16)
            at += out.shape[0]


def expert(parts, gate_weight, up_weight, down_weight):
    rows = sum(part.shape[0] for part in parts)
    features, hidden = gate_weight.shape
    tile = 256
    return pl.pallas_call(
        functools.partial(expert_kernel, len(parts)),
        grid=(hidden // tile,),
        out_shape=[jax.ShapeDtypeStruct(part.shape, BF16) for part in parts],
        in_specs=[whole_block(part) for part in parts]
        + [
            pl.BlockSpec((features, tile), lambda i: (0, i)),
            pl.BlockSpec((features, tile), lambda i: (0, i)),
            pl.BlockSpec((tile, features), lambda i: (i, 0)),
        ],
        out_specs=[whole_block(part) for part in parts],
        scratch_shapes=[pltpu.VMEM((rows, features), BF16), pltpu.VMEM((rows, features), F32)],
        compiler_params=PARAMS,
        cost_estimate=pl.CostEstimate(
            flops=6 * rows * features * hidden,
            bytes_accessed=6 * features * hidden + 4 * rows * features,
            transcendentals=rows * hidden,
        ),
    )(*parts, gate_weight, up_weight, down_weight)


def to_experts(rows):
    return lax.all_to_all(rows, "node", 0, 0, tiled=True)


def total(own, parts):
    for part in parts:
        own = own + part.astype(F32)
    return own.astype(BF16)


def body(tokens, norm_gain, routes, route_gates, placement, gate_weight, up_weight, down_weight):
    nodes, peers = lax.axis_size("node"), lax.axis_size("local")
    node, local = lax.axis_index("node"), lax.axis_index("local")
    experts = placement.shape[0]
    tok_rows, features = tokens.shape
    top_count = routes.shape[1]
    capacity = BLOCK_TOK * top_count // experts * 3 // 2
    slots = experts * capacity
    half = features // 2
    values = tokens.astype(F32)
    rescale = lax.rsqrt(jnp.mean(values * values, axis=-1, keepdims=True) + EPSILON)
    normed = (values * rescale * norm_gain.astype(F32)).astype(BF16)
    combine_weight = (route_gates / jnp.sum(route_gates, axis=-1, keepdims=True)).astype(BF16)
    held = routes[:, :, None] == placement[None, None, :]
    table = jnp.sum(jnp.where(held, combine_weight[:, :, None], jnp.zeros((), BF16)), axis=1)
    weights = (gate_weight[0], up_weight[0], down_weight[0])
    sent = jnp.concatenate([normed, jnp.pad(table, ((0, 0), (0, -experts % LANES)))], axis=1)
    sent0, sent1, sent2, sent3 = jnp.split(sent, tok_rows // BLOCK_TOK)

    bits_a, bits_b = bit_order(nodes, False), bit_order(nodes, True)
    order_a, order_b = gathered_from(bits_a), gathered_from(bits_b)
    slot = np.arange(slots)
    turn = jnp.asarray(slot[None, :] % capacity, F32)
    near_group = slot // capacity % peers
    near_lane = jnp.asarray(slot[None, :] // (capacity * peers) * peers, I32) + local
    near_own = (np.arange(peers * BLOCK_TOK)[:, None] // BLOCK_TOK == near_group).astype(np.float32)
    near_own = jnp.asarray(near_own, BF16)
    cross_group = slot // capacity % nodes
    cross_lane = (jnp.asarray(slot[None, :] // (capacity * nodes), I32) ^ local) + node * peers
    cross_own = [
        jnp.asarray((np.repeat(order, BLOCK_TOK)[:, None] == cross_group).astype(np.float32), BF16)
        for order in (order_a, order_b)
    ]
    cuts = [slots // peers * k for k in range(peers)] + [slots - slots // peers // 2, slots]

    def gather(rows, first, last):
        return swaps([rows] * peers, "local", first, last)

    def pick_near(rows, near):
        return pick([rows] + near, near_lane, near_own, turn, features)

    near0 = gather(sent0, 1, peers)
    pair = jnp.concatenate([sent3, swap(sent3, "node", bits_a[0])])
    rows_a = gather_doubling(pair[:, :half], "node", bits_a[1:])
    rows_b = gather_doubling(pair[:, half:], "node", bits_b[1:])
    (sent1,) = fence([sent1], near0 + [rows_a, rows_b])
    near1 = gather(sent1, 1, peers - 1)
    outbound0, mixing0 = pick_near(sent0, near0)

    outbound0, sent1, rows_a, rows_b = fence([outbound0, sent1, rows_a, rows_b], near1)
    arrived0 = to_experts(outbound0)
    near1 += gather(sent1, peers - 1, peers)
    outbound3, mixing3a, mixing3b = pick_cross(
        rows_a, rows_b, order_b, cross_lane, *cross_own, turn, features, cuts
    )
    arrived3 = outbound3[:1] + swaps(outbound3, "local", 1, peers - 1)
    outbound1, mixing1 = pick_near(sent1, near1)

    outbound1, sent2, first3, last3 = fence(
        [outbound1, sent2] + outbound3[-2:], [arrived0] + arrived3[1:]
    )
    arrived1 = to_experts(outbound1)
    near2 = gather(sent2, 1, peers)
    arrived3.append(swap(first3, "local", peers - 1))
    (out0,) = expert([arrived0], *weights)
    outbound2, mixing2 = pick_near(sent2, near2)

    outbound2, last3 = fence([outbound2, last3], [arrived1, out0, arrived3[-1]])
    arrived2 = to_experts(outbound2)
    arrived3.append(swap(last3, "local", peers - 1))
    (out1,) = expert([arrived1], *weights)
    arrived3[-1], = fence([arrived3[-1]], [out1])
    out3 = list(expert(arrived3, *weights))

    out0, *out3 = fence([out0] + out3, [arrived2, out1])
    landed0 = to_experts(out0)
    landed3 = out3[:1] + swaps(out3, "local", 1, peers - 1)
    (out2,) = expert([arrived2], *weights)

    out1, first3, last3 = fence([out1] + out3[-2:], [landed0, out2] + landed3[1:])
    landed1 = to_experts(out1)
    landed3.append(swap(first3, "local", peers - 1))
    sum0, parts0 = mix(mixing0, landed0)
    parts0 = swaps(parts0, "local", 1, peers)

    out2, last3 = fence([out2, last3], [landed1, landed3[-1]] + parts0)
    landed2 = to_experts(out2)
    landed3.append(swap(last3, "local", peers - 1))
    sum1, parts1 = mix(mixing1, landed1)
    parts1 = swaps(parts1, "local", 1, peers)
    piece0 = total(sum0, parts0)
    cross = mix_cross(mixing3a, mixing3b, landed3)

    landed2, *cross = fence([landed2] + list(cross), parts1)
    sum2, parts2 = mix(mixing2, landed2)
    cross = fence(list(cross), parts2[1:])
    parts2 = swaps(parts2, "local", 1, peers)
    piece1 = total(sum1, parts1)
    piece3 = jnp.concatenate(
        [sum_halving(*cross[:2], "node", bits_a), sum_halving(*cross[2:], "node", bits_b)], axis=1
    )
    piece2 = total(sum2, parts2)
    return jnp.concatenate([piece0, piece1, piece2, piece3], axis=0)


def solution(mesh):
    rows = P(AXES, None)
    stacked = P(AXES, None, None)
    in_specs = (rows, P(), rows, rows, P(), stacked, stacked, stacked)
    return jax.shard_map(body, mesh=mesh, in_specs=in_specs, out_specs=rows, check_vma=False)
```

```python
import functools

import jax
import jax.numpy as jnp
import numpy as np
from jax import lax
from jax.experimental import pallas as pl
from jax.experimental.pallas import tpu as pltpu
from jax.sharding import PartitionSpec as P

BLOCK_TOK = 32
EPSILON = 1e-06
AXES = ("node", "local")
LANES = 128
TILES = 4
BF16, F32, I32 = jnp.bfloat16, jnp.float32, jnp.int32
ANYWHERE = pl.BlockSpec(memory_space=pl.ANY)
PARAMS = pltpu.CompilerParams(vmem_limit_bytes=60 * 2**20)


def fence(arrays, after):
    token = sum(a[:16, :LANES].astype(F32) for a in after)

    def kernel(*refs):
        pass

    return pl.pallas_call(
        kernel,
        out_shape=[jax.ShapeDtypeStruct(a.shape, a.dtype) for a in arrays],
        in_specs=[ANYWHERE] * (len(arrays) + 1),
        out_specs=[ANYWHERE] * len(arrays),
        input_output_aliases={i: i for i in range(len(arrays))},
    )(*arrays, token)


def swap(array, axis, bits):
    size = lax.axis_size(axis)
    return lax.ppermute(array, axis, [(i, i ^ bits) for i in range(size)])


def swaps(parts, axis, first, last):
    return [swap(parts[k], axis, k) for k in range(first, last)]


def bit_order(size, last_first):
    bits = [1 << i for i in range(size.bit_length() - 1)]
    return bits[:1] + bits[:0:-1] if last_first else bits


def chain_step(arrays, axis, step):
    size = lax.axis_size(axis)
    rightward = [(i, i + 1) for i in range(step - 1, size - 1)]
    leftward = [(size - 1 - i, size - 2 - i) for i in range(step - 1, size - 1)]
    return [lax.ppermute(a, axis, way) for a, way in zip(arrays, (rightward, leftward))]


def gather_doubling(array, axis, bits):
    for bit in bits:
        array = jnp.concatenate([array, swap(array, axis, bit)])
    return array


def gathered_from(bits):
    found = [0]
    for bit in bits:
        found += [k ^ bit for k in found]
    return found


def sum_halving(keep, give, axis, bits):
    for step, bit in enumerate(bits[::-1]):
        if step:
            keep, give = jnp.split(keep, 2)
        keep = keep + swap(give.astype(BF16), axis, bit).astype(F32)
    return keep.astype(BF16)


def below(rows):
    at = np.arange(rows)
    same = at[:, None] // BLOCK_TOK == at[None, :] // BLOCK_TOK
    return jnp.asarray((same & (at[None, :] < at[:, None])).astype(np.float32), BF16)


def choose(table, lane, row_group, slot_group, turn, before):
    select = lax.broadcasted_iota(I32, (table.shape[1], lane.shape[1]), 0) == lane
    weight = jnp.dot(table, select.astype(BF16), preferred_element_type=F32)
    mask = jnp.where((weight > 0) & (row_group == slot_group), 1.0, 0.0)
    rank = jnp.dot(before, mask.astype(BF16), preferred_element_type=F32)
    place = jnp.where(rank == turn, mask, 0.0)
    return place.astype(BF16), (place * weight).astype(BF16)


def gather_rows(place, rows):
    return lax.dot_general(
        place, rows, (((0,), (0,)), ((), ())), preferred_element_type=F32
    ).astype(BF16)


def pick_kernel(count, *refs):
    parts, refs = refs[:count], refs[count:]
    tables, refs = refs[:count], refs[count:]
    lane, row_group, slot_group, turn, before, order, out, mixing, place = refs

    @pl.when(pl.program_id(0) == 0)
    def _():
        table = jnp.concatenate([t[...] for t in tables])
        place[...], weights = choose(
            table, lane[...], row_group[...], slot_group[...], turn[...], before[...]
        )
        mixing[...] = jnp.dot(order[...], weights, preferred_element_type=F32).astype(BF16)

    out[...] = gather_rows(place[...], jnp.concatenate([p[...] for p in parts]))


def whole_block(array):
    return pl.BlockSpec(array.shape, lambda j: (0,) * array.ndim)


def pick(parts, block, lane, row_group, slot_group, turn, order, features):
    slots = lane.shape[1]
    rows = len(parts) * BLOCK_TOK
    tile = features // TILES
    small = (lane, row_group, slot_group, turn, below(rows), order)
    return pl.pallas_call(
        functools.partial(pick_kernel, len(parts)),
        grid=(TILES,),
        out_shape=[
            jax.ShapeDtypeStruct((slots, features), BF16),
            jax.ShapeDtypeStruct((order.shape[0], slots), BF16),
        ],
        in_specs=[pl.BlockSpec((BLOCK_TOK, tile), lambda j: (block, j))] * len(parts)
        + [pl.BlockSpec((BLOCK_TOK, LANES), lambda j: (block, features // LANES))] * len(parts)
        + [whole_block(a) for a in small],
        out_specs=[
            pl.BlockSpec((slots, tile), lambda j: (0, j)),
            pl.BlockSpec((order.shape[0], slots), lambda j: (0, 0)),
        ],
        scratch_shapes=[pltpu.VMEM((rows, slots), BF16)],
        compiler_params=PARAMS,
        cost_estimate=pl.CostEstimate(
            flops=2 * rows * slots * features,
            bytes_accessed=2 * (rows + slots) * features,
            transcendentals=0,
        ),
    )(*parts, *parts, *small)


def pick_cross_kernel(order, cuts, a0, a1, b0, b1, t0, t1, *refs):
    lane, group_a, group_b, slot_group, turn, before = refs[:6]
    outs, (mixing_a, mixing_b, place_a, place_b) = refs[6:-4], refs[-4:]
    step = pl.program_id(0)

    @pl.when(step == 0)
    def _():
        known = jnp.concatenate([t0[...], t1[...]])
        common = slot_group[...], turn[...], before[...]
        place_b[...], mixing_b[...] = choose(known, lane[...], group_b[...], *common)
        back = [order.index(k) * BLOCK_TOK for k in range(len(order))]
        known = jnp.concatenate([known[at : at + BLOCK_TOK] for at in back])
        place_a[...], mixing_a[...] = choose(known, lane[...], group_a[...], *common)

    def store(place, first_rows, last_rows):
        result = gather_rows(place[...], jnp.concatenate([first_rows[...], last_rows[...]]))
        for out, first, last in zip(outs, cuts[:-1], cuts[1:]):
            out[...] = result[first:last]

    @pl.when(step < TILES // 2)
    def _():
        store(place_a, a0, a1)

    @pl.when(step >= TILES // 2)
    def _():
        store(place_b, b0, b1)


def in_first_half(shape):
    return pl.BlockSpec(shape, lambda j: (0, jnp.minimum(j, TILES // 2 - 1)))


def in_second_half(shape):
    return pl.BlockSpec(shape, lambda j: (0, jnp.maximum(j - TILES // 2, 0)))


def pick_cross(rows_a, rows_b, order_b, lane, group_a, group_b, slot_group, turn, features, cuts):
    slots = lane.shape[1]
    part = rows_a[0].shape[0]
    rows = 2 * part
    tile = features // TILES
    small = (lane, group_a, group_b, slot_group, turn, below(rows))
    sizes = [last - first for first, last in zip(cuts[:-1], cuts[1:])]
    results = pl.pallas_call(
        functools.partial(pick_cross_kernel, order_b, cuts),
        grid=(TILES,),
        out_shape=[jax.ShapeDtypeStruct((size, features), BF16) for size in sizes]
        + [jax.ShapeDtypeStruct((rows, slots), BF16)] * 2,
        in_specs=[in_first_half((part, tile))] * 2
        + [in_second_half((part, tile))] * 2
        + [pl.BlockSpec((part, LANES), lambda j: (0, features // 2 // LANES))] * 2
        + [whole_block(a) for a in small],
        out_specs=[pl.BlockSpec((size, tile), lambda j: (0, j)) for size in sizes]
        + [pl.BlockSpec((rows, slots), lambda j: (0, 0))] * 2,
        scratch_shapes=[pltpu.VMEM((rows, slots), BF16)] * 2,
        compiler_params=PARAMS,
        cost_estimate=pl.CostEstimate(
            flops=2 * rows * slots * features,
            bytes_accessed=2 * (rows + slots) * features,
            transcendentals=0,
        ),
    )(*rows_a, *rows_b, *rows_b, *small)
    return list(results[:-2]), results[-2], results[-1]


def mix_kernel(mixing, landed, own, *outs):
    result = jnp.dot(mixing[...], landed[...], preferred_element_type=F32)
    own[...] = result[:BLOCK_TOK]
    for k, out in enumerate(outs):
        out[...] = result[(k + 1) * BLOCK_TOK : (k + 2) * BLOCK_TOK].astype(BF16)


def mix(mixing, landed):
    rows, slots = mixing.shape
    features = landed.shape[1]
    tile = features // TILES
    count = rows // BLOCK_TOK
    own, *parts = pl.pallas_call(
        mix_kernel,
        grid=(TILES,),
        out_shape=[jax.ShapeDtypeStruct((BLOCK_TOK, features), F32)]
        + [jax.ShapeDtypeStruct((BLOCK_TOK, features), BF16)] * (count - 1),
        in_specs=[whole_block(mixing), pl.BlockSpec((slots, tile), lambda j: (0, j))],
        out_specs=[pl.BlockSpec((BLOCK_TOK, tile), lambda j: (0, j))] * count,
        compiler_params=PARAMS,
        cost_estimate=pl.CostEstimate(
            flops=2 * rows * slots * features,
            bytes_accessed=2 * (rows + slots) * features,
            transcendentals=0,
        ),
    )(mixing, landed)
    return own, [None] + parts


def mix_cross_kernel(mixing_a, mixing_b, *refs):
    landed, (keep_a, give_a, keep_b, give_b) = refs[:-4], refs[-4:]
    step = pl.program_id(0)
    half = keep_a.shape[0]
    rows = jnp.concatenate([part[...] for part in landed])

    def store(mixing, keep, give):
        result = jnp.dot(mixing[...], rows, preferred_element_type=F32)
        keep[...] = result[:half]
        give[...] = result[half:].astype(BF16)

    @pl.when(step < TILES // 2)
    def _():
        store(mixing_a, keep_a, give_a)

    @pl.when(step >= TILES // 2)
    def _():
        store(mixing_b, keep_b, give_b)


def mix_cross(mixing_a, mixing_b, landed):
    rows, slots = mixing_a.shape
    features = landed[0].shape[1]
    tile = features // TILES
    shape = (rows // 2, features // 2)
    return pl.pallas_call(
        mix_cross_kernel,
        grid=(TILES,),
        out_shape=[jax.ShapeDtypeStruct(shape, F32), jax.ShapeDtypeStruct(shape, BF16)] * 2,
        in_specs=[whole_block(mixing_a), whole_block(mixing_b)]
        + [pl.BlockSpec((part.shape[0], tile), lambda j: (0, j)) for part in landed],
        out_specs=[in_first_half((rows // 2, tile))] * 2 + [in_second_half((rows // 2, tile))] * 2,
        compiler_params=PARAMS,
        cost_estimate=pl.CostEstimate(
            flops=2 * rows * slots * features,
            bytes_accessed=2 * (rows + slots) * features,
            transcendentals=0,
        ),
    )(mixing_a, mixing_b, *landed)


def expert_kernel(count, *refs):
    parts, (gate_ref, up_ref, down_ref) = refs[:count], refs[count : count + 3]
    outs, (joined, total) = refs[count + 3 : -2], refs[-2:]
    step = pl.program_id(0)
    x_ref = parts[0] if count == 1 else joined

    if count > 1:

        @pl.when(step == 0)
        def _():
            joined[...] = jnp.concatenate([part[...] for part in parts])

    x = x_ref[...]
    gate_pre = jnp.dot(x, gate_ref[...], preferred_element_type=F32)
    up_pre = jnp.dot(x, up_ref[...], preferred_element_type=F32)
    hidden = (gate_pre / (1 + jnp.exp(-gate_pre)) * up_pre).astype(BF16)
    part = jnp.dot(hidden, down_ref[...], preferred_element_type=F32)

    @pl.when(step == 0)
    def _():
        total[...] = part

    @pl.when(step > 0)
    def _():
        total[...] += part

    @pl.when(step == pl.num_programs(0) - 1)
    def _():
        at = 0
        for out in outs:
            out[...] = total[at : at + out.shape[0]].astype(BF16)
            at += out.shape[0]


def expert(parts, gate_weight, up_weight, down_weight):
    rows = sum(part.shape[0] for part in parts)
    features, hidden = gate_weight.shape
    tile = 256
    return pl.pallas_call(
        functools.partial(expert_kernel, len(parts)),
        grid=(hidden // tile,),
        out_shape=[jax.ShapeDtypeStruct(part.shape, BF16) for part in parts],
        in_specs=[whole_block(part) for part in parts]
        + [
            pl.BlockSpec((features, tile), lambda i: (0, i)),
            pl.BlockSpec((features, tile), lambda i: (0, i)),
            pl.BlockSpec((tile, features), lambda i: (i, 0)),
        ],
        out_specs=[whole_block(part) for part in parts],
        scratch_shapes=[
            pltpu.VMEM((rows if len(parts) > 1 else 16, features), BF16),
            pltpu.VMEM((rows, features), F32),
        ],
        compiler_params=PARAMS,
        cost_estimate=pl.CostEstimate(
            flops=6 * rows * features * hidden,
            bytes_accessed=6 * features * hidden + 4 * rows * features,
            transcendentals=rows * hidden,
        ),
    )(*parts, gate_weight, up_weight, down_weight)


def prepare_kernel(tokens, gain, routes, gates, placement, *outs):
    scale = gain[...].astype(F32)
    chosen = gates[...] / jnp.sum(gates[...], axis=-1, keepdims=True)
    for block, out in enumerate(outs):
        at = slice(block * BLOCK_TOK, (block + 1) * BLOCK_TOK)
        values = tokens[at].astype(F32)
        rescale = lax.rsqrt(jnp.mean(values * values, axis=-1, keepdims=True) + EPSILON)
        out[:, : values.shape[1]] = (values * rescale * scale).astype(BF16)
        table = jnp.zeros((BLOCK_TOK, placement.shape[1]), F32)
        for k in range(routes.shape[1]):
            held = routes[at, k : k + 1] == placement[...]
            table = jnp.where(held, chosen[at, k : k + 1], table)
        out[:, values.shape[1] :] = table.astype(BF16)


def prepare(tokens, norm_gain, routes, route_gates, placement):
    rows, features = tokens.shape
    lanes = -(-placement.shape[0] // LANES) * LANES
    padded = jnp.pad(placement, (0, lanes - placement.shape[0]), constant_values=-1)
    return pl.pallas_call(
        prepare_kernel,
        out_shape=[jax.ShapeDtypeStruct((BLOCK_TOK, features + lanes), BF16)] * (rows // BLOCK_TOK),
        compiler_params=PARAMS,
    )(tokens, norm_gain[None], routes, route_gates, padded[None])


def to_experts(rows):
    return lax.all_to_all(rows, "node", 0, 0, tiled=True)


def total(own, parts):
    for part in parts:
        own = own + part.astype(F32)
    return own.astype(BF16)


def body(tokens, norm_gain, routes, route_gates, placement, gate_weight, up_weight, down_weight):
    nodes, peers = lax.axis_size("node"), lax.axis_size("local")
    node, local = lax.axis_index("node"), lax.axis_index("local")
    experts = placement.shape[0]
    features = tokens.shape[1]
    capacity = BLOCK_TOK * routes.shape[1] // experts * 3 // 2
    slots = experts * capacity
    half = features // 2
    weights = (gate_weight[0], up_weight[0], down_weight[0])
    sent0, sent1, sent2, sent3 = prepare(tokens, norm_gain, routes, route_gates, placement)

    bits_a, bits_b = bit_order(nodes, False), bit_order(nodes, True)
    order_a, order_b = gathered_from(bits_a), gathered_from(bits_b)
    slot = np.arange(slots)
    turn = jnp.asarray(slot[None, :] % capacity, F32)
    near_group = jnp.asarray(slot[None, :] // capacity % peers, I32)
    near_lane = jnp.asarray(slot[None, :] // (capacity * peers) * peers, I32) + local
    cross_group = jnp.asarray(slot[None, :] // capacity % nodes, I32)
    cross_lane = (jnp.asarray(slot[None, :] // (capacity * nodes), I32) ^ local) + node * peers

    def by_token(groups):
        return jnp.repeat(jnp.asarray(groups, I32), BLOCK_TOK)[:, None]

    bits = by_token(np.arange(peers))
    steps = np.array([0] + [s for d in range(1, peers) for s in (-d, d)])
    source = local + jnp.asarray(steps, I32)
    chain_bits = by_token(jnp.where((source >= 0) & (source < peers), source ^ local, -1))
    within = np.arange(peers * BLOCK_TOK)[:, None] % BLOCK_TOK
    chain_within = np.arange(len(steps) * BLOCK_TOK)[None, :] % BLOCK_TOK
    chain_order = (bits == chain_bits.T) & jnp.asarray(within == chain_within)
    chain_order = chain_order.astype(BF16)
    same_order = jnp.asarray(np.eye(peers * BLOCK_TOK, dtype=np.float32), BF16)
    size = slots // peers
    cuts = [size * k for k in range(peers - 1)]
    cuts += [cuts[-1] + size * 2 // 3, size * (peers - 1), slots - size // 3, slots]

    near0 = swaps([sent0] * peers, "local", 1, peers)
    pair = jnp.concatenate([sent3, swap(sent3, "node", bits_a[0])])
    rows_a = gather_doubling(pair[:, :half], "node", bits_a[1:-1])
    rows_b = gather_doubling(pair[:, half:], "node", bits_b[1:-1])
    rows_a = [rows_a, swap(rows_a, "node", bits_a[-1])]
    rows_b = [rows_b, swap(rows_b, "node", bits_b[-1])]
    sent12 = jnp.concatenate([sent1, sent2])
    (sent12,) = fence([sent12], near0 + [rows_a[1], rows_b[1]])
    chain = chain_step([sent12, sent12], "local", 1)
    outbound0, mixing0 = pick(
        [sent0] + near0, 0, near_lane, bits, near_group, turn, same_order, features
    )

    outbound0, *last_rows = fence([outbound0, rows_a[1], rows_b[1]], chain)
    arrived0 = to_experts(outbound0)
    parts12 = [sent12] + chain
    for step in range(2, peers):
        chain = chain_step(chain, "local", step)
        parts12 += chain
    outbound3, mixing3a, mixing3b = pick_cross(
        [rows_a[0], last_rows[0]],
        [rows_b[0], last_rows[1]],
        order_b,
        cross_lane,
        by_token(order_a),
        by_token(order_b),
        cross_group,
        turn,
        features,
        cuts,
    )
    arrived3 = outbound3[:1] + swaps(outbound3, "local", 1, peers - 1)
    outbound1, mixing1 = pick(
        parts12, 0, near_lane, chain_bits, near_group, turn, chain_order, features
    )

    outbound1, *later3 = fence([outbound1] + outbound3[-3:], arrived3[1:])
    arrived1 = to_experts(outbound1)
    outbound2, mixing2 = pick(
        parts12, 1, near_lane, chain_bits, near_group, turn, chain_order, features
    )
    arrived3.append(swap(later3[0], "local", peers - 2))
    arrived3 += [swap(part, "local", peers - 1) for part in later3[1:]]
    (out0,) = expert([arrived0], *weights)

    (outbound2,) = fence([outbound2], [out0])
    arrived2 = to_experts(outbound2)
    out3 = list(expert(arrived3, *weights))
    (out1,) = expert([arrived1], *weights)

    out0, *out3 = fence([out0] + out3, [out1])
    landed0 = to_experts(out0)
    landed3 = out3[:1] + swaps(out3, "local", 1, peers - 1)
    landed3.append(swap(out3[-3], "local", peers - 2))
    (out2,) = expert([arrived2], *weights)

    out1, *later3 = fence([out1] + out3[-2:], [out2] + landed3[1:])
    landed1 = to_experts(out1)
    landed3.append(swap(later3[0], "local", peers - 1))
    sum0, parts0 = mix(mixing0, landed0)
    parts0 = swaps(parts0, "local", 1, peers)

    out2, last3 = fence([out2, later3[1]], [landed3[-1]] + parts0)
    landed2 = to_experts(out2)
    landed3.append(swap(last3, "local", peers - 1))
    sum1, parts1 = mix(mixing1, landed1)
    parts1 = swaps(parts1, "local", 1, peers)
    piece0 = total(sum0, parts0)
    cross = mix_cross(mixing3a, mixing3b, landed3)

    (mixing2,) = fence([mixing2], [cross[1], cross[3]])
    sum2, parts2 = mix(mixing2, landed2)
    cross = fence(list(cross), parts2[1:])
    parts2 = swaps(parts2, "local", 1, peers)
    piece1 = total(sum1, parts1)
    piece3 = jnp.concatenate(
        [sum_halving(*cross[:2], "node", bits_a), sum_halving(*cross[2:], "node", bits_b)], axis=1
    )
    piece2 = total(sum2, parts2)
    return jnp.concatenate([piece0, piece1, piece2, piece3], axis=0)


def solution(mesh):
    rows = P(AXES, None)
    stacked = P(AXES, None, None)
    in_specs = (rows, P(), rows, rows, P(), stacked, stacked, stacked)
    return jax.shard_map(body, mesh=mesh, in_specs=in_specs, out_specs=rows, check_vma=False)
```

```python
import functools

import jax
import jax.numpy as jnp
import numpy as np
from jax import lax
from jax.experimental import pallas as pl
from jax.experimental.pallas import tpu as pltpu
from jax.sharding import PartitionSpec as P

BLOCK_TOK = 32
EPSILON = 1e-06
AXES = ("node", "local")
LANES = 128
TILES = 4
BF16, F32, I32 = jnp.bfloat16, jnp.float32, jnp.int32
ANYWHERE = pl.BlockSpec(memory_space=pl.ANY)
PARAMS = pltpu.CompilerParams(vmem_limit_bytes=60 * 2**20)


def fence(arrays, after):
    token = sum(a[:16, :LANES].astype(F32) for a in after)

    def kernel(*refs):
        pass

    return list(pl.pallas_call(
        kernel,
        out_shape=[jax.ShapeDtypeStruct(a.shape, a.dtype) for a in arrays],
        in_specs=[ANYWHERE] * (len(arrays) + 1),
        out_specs=[ANYWHERE] * len(arrays),
        input_output_aliases={i: i for i in range(len(arrays))},
    )(*arrays, token))


def swap(array, axis, bits):
    size = lax.axis_size(axis)
    return lax.ppermute(array, axis, [(i, i ^ bits) for i in range(size)])


def swaps(parts, axis, first, last):
    return [swap(parts[k], axis, k) for k in range(first, last)]


def bit_order(size, last_first):
    bits = [1 << i for i in range(size.bit_length() - 1)]
    return bits[:1] + bits[:0:-1] if last_first else bits


def chain_step(arrays, axis, step):
    size = lax.axis_size(axis)
    rightward = [(i, i + 1) for i in range(step - 1, size - 1)]
    leftward = [(size - 1 - i, size - 2 - i) for i in range(step - 1, size - 1)]
    return [lax.ppermute(a, axis, way) for a, way in zip(arrays, (rightward, leftward))]


def chain_offsets(size):
    return [0] + [offset for d in range(1, size) for offset in (-d, d)]


def chain_sum(own, parts, axis):
    size = lax.axis_size(axis)
    left, right = parts[0::2], parts[1::2]
    for step in range(1, size):
        ways = [(i, i + 1) for i in range(step)], [(size - 1 - i, size - 2 - i) for i in range(step)]
        moved = [
            lax.ppermute(side[size - 1 - step].astype(BF16), axis, way)
            for side, way in zip((right, left), ways)
        ]
        if step < size - 1:
            at = size - 2 - step
            right[at], left[at] = (
                side[at].astype(F32) + came.astype(F32) for side, came in zip((right, left), moved)
            )
    return own, moved


def gather_doubling(array, axis, bits):
    for bit in bits:
        array = jnp.concatenate([array, swap(array, axis, bit)])
    return array


def gathered_from(bits):
    found = [0]
    for bit in bits:
        found += [k ^ bit for k in found]
    return found


def sum_halving(keep, give, axis, bits):
    for step, bit in enumerate(bits[::-1]):
        if step:
            keep, give = jnp.split(keep, 2)
        keep = keep + swap(give.astype(BF16), axis, bit).astype(F32)
    return keep.astype(BF16)


def below(rows):
    at = np.arange(rows)
    same = at[:, None] // BLOCK_TOK == at[None, :] // BLOCK_TOK
    return (same & (at[None, :] < at[:, None])).astype(BF16)


def choose(table, lane, row_group, slot_group, turn, before):
    select = lax.broadcasted_iota(I32, (table.shape[1], lane.shape[1]), 0) == lane
    weight = jnp.dot(table, select.astype(BF16), preferred_element_type=F32)
    mask = jnp.where((weight > 0) & (row_group == slot_group), 1.0, 0.0)
    rank = jnp.dot(before, mask.astype(BF16), preferred_element_type=F32)
    place = jnp.where(rank == turn, mask, 0.0)
    return place.astype(BF16), (place * weight).astype(BF16)


def gather_rows(place, rows):
    return lax.dot_general(
        place, rows, (((0,), (0,)), ((), ())), preferred_element_type=F32
    ).astype(BF16)


def bits_of(labels, local, peers, chained):
    if not chained:
        return labels
    source = labels + local
    return jnp.where((source >= 0) & (source < peers), source ^ local, -1)


def pick_kernel(count, peers, chain_in, chain_out, ids, *refs):
    parts, refs = refs[:count], refs[count:]
    tables, refs = refs[:count], refs[count:]
    lane, slot_group, turn, before, in_column, in_row, out_column, out, mixing, place = refs

    @pl.when(pl.program_id(0) == 0)
    def _():
        local = ids[1]
        table = jnp.concatenate([t[...] for t in tables])
        row_group = bits_of(in_column[...], local, peers, chain_in)
        place[...], weights = choose(
            table, lane[...] + local, row_group, slot_group[...], turn[...], before[...]
        )
        if chain_in != chain_out:
            shape = mixing.shape[0], weights.shape[0]
            same = bits_of(out_column[...], local, peers, chain_out) == bits_of(
                in_row[...], local, peers, chain_in
            )
            row = lax.broadcasted_iota(I32, shape, 0) & (BLOCK_TOK - 1)
            column = lax.broadcasted_iota(I32, shape, 1) & (BLOCK_TOK - 1)
            order = jnp.where(same & (row == column), 1.0, 0.0).astype(BF16)
            weights = jnp.dot(order, weights, preferred_element_type=F32).astype(BF16)
        mixing[...] = weights

    out[...] = gather_rows(place[...], jnp.concatenate([p[...] for p in parts]))


def whole_block(array):
    return pl.BlockSpec(array.shape, lambda j: (0,) * array.ndim)


def by_token(labels):
    return np.repeat(np.array(labels, np.int32), BLOCK_TOK)


def pick(parts, block, ids, peers, capacity, features, chain_in, chain_out):
    nodes = lax.axis_size("node")
    slots = nodes * peers * capacity
    slot = np.arange(slots, dtype=np.int32)[None, :]
    labels = chain_offsets(peers), list(range(peers))
    in_labels, out_labels = by_token(labels[not chain_in]), by_token(labels[not chain_out])
    rows, tile = len(in_labels), features // TILES
    small = (
        slot // (capacity * peers) * peers,
        slot // capacity % peers,
        (slot % capacity).astype(np.float32),
        below(rows),
        in_labels[:, None],
        in_labels[None, :],
        out_labels[:, None],
    )
    return pl.pallas_call(
        functools.partial(pick_kernel, len(parts), peers, chain_in, chain_out),
        grid=(TILES,),
        out_shape=[
            jax.ShapeDtypeStruct((slots, features), BF16),
            jax.ShapeDtypeStruct((len(out_labels), slots), BF16),
        ],
        in_specs=[pl.BlockSpec(memory_space=pltpu.SMEM)]
        + [pl.BlockSpec((BLOCK_TOK, tile), lambda j: (block, j))] * len(parts)
        + [pl.BlockSpec((BLOCK_TOK, LANES), lambda j: (block, features // LANES))] * len(parts)
        + [whole_block(a) for a in small],
        out_specs=[
            pl.BlockSpec((slots, tile), lambda j: (0, j)),
            pl.BlockSpec((len(out_labels), slots), lambda j: (0, 0)),
        ],
        scratch_shapes=[pltpu.VMEM((rows, slots), BF16)],
        compiler_params=PARAMS,
        cost_estimate=pl.CostEstimate(
            flops=2 * rows * slots * features,
            bytes_accessed=2 * (rows + slots) * features,
            transcendentals=0,
        ),
    )(ids, *parts, *parts, *small)


def pick_cross_kernel(order, cuts, peers, ids, a0, a1, b0, b1, t0, t1, *refs):
    peer, group_a, group_b, slot_group, turn, before = refs[:6]
    outs, (mixing_a, mixing_b, place_a, place_b) = refs[6:-4], refs[-4:]
    step = pl.program_id(0)

    @pl.when(step == 0)
    def _():
        known = jnp.concatenate([t0[...], t1[...]])
        lane = (peer[...] ^ ids[1]) + ids[0] * peers
        common = slot_group[...], turn[...], before[...]
        place_b[...], mixing_b[...] = choose(known, lane, group_b[...], *common)
        back = [order.index(k) * BLOCK_TOK for k in range(len(order))]
        known = jnp.concatenate([known[at : at + BLOCK_TOK] for at in back])
        place_a[...], mixing_a[...] = choose(known, lane, group_a[...], *common)

    def store(place, first_rows, last_rows):
        result = gather_rows(place[...], jnp.concatenate([first_rows[...], last_rows[...]]))
        for out, first, last in zip(outs, cuts[:-1], cuts[1:]):
            out[...] = result[first:last]

    @pl.when(step < TILES // 2)
    def _():
        store(place_a, a0, a1)

    @pl.when(step >= TILES // 2)
    def _():
        store(place_b, b0, b1)


def in_first_half(shape):
    return pl.BlockSpec(shape, lambda j: (0, jnp.minimum(j, TILES // 2 - 1)))


def in_second_half(shape):
    return pl.BlockSpec(shape, lambda j: (0, jnp.maximum(j - TILES // 2, 0)))


def pick_cross(rows_a, rows_b, order_a, order_b, ids, peers, capacity, features, cuts):
    part = rows_a[0].shape[0]
    rows = 2 * part
    nodes = rows // BLOCK_TOK
    slots = cuts[-1]
    slot = np.arange(slots, dtype=np.int32)[None, :]
    tile = features // TILES
    small = (
        slot // (capacity * nodes),
        by_token(order_a)[:, None],
        by_token(order_b)[:, None],
        slot // capacity % nodes,
        (slot % capacity).astype(np.float32),
        below(rows),
    )
    sizes = [last - first for first, last in zip(cuts[:-1], cuts[1:])]
    results = pl.pallas_call(
        functools.partial(pick_cross_kernel, order_b, cuts, peers),
        grid=(TILES,),
        out_shape=[jax.ShapeDtypeStruct((size, features), BF16) for size in sizes]
        + [jax.ShapeDtypeStruct((rows, slots), BF16)] * 2,
        in_specs=[pl.BlockSpec(memory_space=pltpu.SMEM)]
        + [in_first_half((part, tile))] * 2
        + [in_second_half((part, tile))] * 2
        + [pl.BlockSpec((part, LANES), lambda j: (0, features // 2 // LANES))] * 2
        + [whole_block(a) for a in small],
        out_specs=[pl.BlockSpec((size, tile), lambda j: (0, j)) for size in sizes]
        + [pl.BlockSpec((rows, slots), lambda j: (0, 0))] * 2,
        scratch_shapes=[pltpu.VMEM((rows, slots), BF16)] * 2,
        compiler_params=PARAMS,
        cost_estimate=pl.CostEstimate(
            flops=2 * rows * slots * features,
            bytes_accessed=2 * (rows + slots) * features,
            transcendentals=0,
        ),
    )(ids, *rows_a, *rows_b, *rows_b, *small)
    return list(results[:-2]), results[-2], results[-1]


def mix_kernel(mixing, landed, own, *outs):
    result = jnp.dot(mixing[...], landed[...], preferred_element_type=F32)
    own[...] = result[:BLOCK_TOK]
    for k, out in enumerate(outs):
        out[...] = result[(k + 1) * BLOCK_TOK : (k + 2) * BLOCK_TOK].astype(BF16)


def mix(mixing, landed):
    rows, slots = mixing.shape
    features = landed.shape[1]
    tile = features // TILES
    count = rows // BLOCK_TOK
    own, *parts = pl.pallas_call(
        mix_kernel,
        grid=(TILES,),
        out_shape=[jax.ShapeDtypeStruct((BLOCK_TOK, features), F32)]
        + [jax.ShapeDtypeStruct((BLOCK_TOK, features), BF16)] * (count - 1),
        in_specs=[whole_block(mixing), pl.BlockSpec((slots, tile), lambda j: (0, j))],
        out_specs=[pl.BlockSpec((BLOCK_TOK, tile), lambda j: (0, j))] * count,
        compiler_params=PARAMS,
        cost_estimate=pl.CostEstimate(
            flops=2 * rows * slots * features,
            bytes_accessed=2 * (rows + slots) * features,
            transcendentals=0,
        ),
    )(mixing, landed)
    return own, parts


def mix_cross_kernel(mixing_a, mixing_b, *refs):
    landed, (keep_a, give_a, keep_b, give_b) = refs[:-4], refs[-4:]
    step = pl.program_id(0)
    half = keep_a.shape[0]
    rows = jnp.concatenate([part[...] for part in landed])

    def store(mixing, keep, give):
        result = jnp.dot(mixing[...], rows, preferred_element_type=F32)
        keep[...] = result[:half]
        give[...] = result[half:].astype(BF16)

    @pl.when(step < TILES // 2)
    def _():
        store(mixing_a, keep_a, give_a)

    @pl.when(step >= TILES // 2)
    def _():
        store(mixing_b, keep_b, give_b)


def mix_cross(mixing_a, mixing_b, landed):
    rows, slots = mixing_a.shape
    features = landed[0].shape[1]
    tile = features // TILES
    shape = (rows // 2, features // 2)
    return pl.pallas_call(
        mix_cross_kernel,
        grid=(TILES,),
        out_shape=[jax.ShapeDtypeStruct(shape, F32), jax.ShapeDtypeStruct(shape, BF16)] * 2,
        in_specs=[whole_block(mixing_a), whole_block(mixing_b)]
        + [pl.BlockSpec((part.shape[0], tile), lambda j: (0, j)) for part in landed],
        out_specs=[in_first_half((rows // 2, tile))] * 2 + [in_second_half((rows // 2, tile))] * 2,
        compiler_params=PARAMS,
        cost_estimate=pl.CostEstimate(
            flops=2 * rows * slots * features,
            bytes_accessed=2 * (rows + slots) * features,
            transcendentals=0,
        ),
    )(mixing_a, mixing_b, *landed)


def expert_kernel(count, first_tiles, *refs):
    parts, (gate_ref, up_ref, down_ref) = refs[:count], refs[count : count + 3]
    outs, (joined, hidden) = refs[count + 3 : -2], refs[-2:]
    step = pl.program_id(0)
    x_ref = parts[0] if count == 1 else joined

    if count > 1:

        @pl.when(step == 0)
        def _():
            joined[...] = jnp.concatenate([part[...] for part in parts])

    @pl.when(step < first_tiles)
    def _():
        x = x_ref[...]
        gate_pre = jnp.dot(x, gate_ref[...], preferred_element_type=F32)
        up_pre = jnp.dot(x, up_ref[...], preferred_element_type=F32)
        hidden[step] = (gate_pre / (1 + jnp.exp(-gate_pre)) * up_pre).astype(BF16)

    @pl.when(step >= first_tiles)
    def _():
        rows = jnp.concatenate([hidden[i] for i in range(first_tiles)], axis=1)
        result = jnp.dot(rows, down_ref[...], preferred_element_type=F32).astype(BF16)
        at = 0
        for out in outs:
            out[...] = result[at : at + out.shape[0]]
            at += out.shape[0]


def expert(parts, gate_weight, up_weight, down_weight):
    rows = sum(part.shape[0] for part in parts)
    features, hidden = gate_weight.shape
    tile = 256
    first_tiles = hidden // tile
    out_tile = features // TILES

    def first(i):
        return jnp.minimum(i, first_tiles - 1)

    def second(i):
        return jnp.maximum(i - first_tiles, 0)

    return pl.pallas_call(
        functools.partial(expert_kernel, len(parts), first_tiles),
        grid=(first_tiles + TILES,),
        out_shape=[jax.ShapeDtypeStruct(part.shape, BF16) for part in parts],
        in_specs=[whole_block(part) for part in parts]
        + [
            pl.BlockSpec((features, tile), lambda i: (0, first(i))),
            pl.BlockSpec((features, tile), lambda i: (0, first(i))),
            pl.BlockSpec((hidden, out_tile), lambda i: (0, second(i))),
        ],
        out_specs=[
            pl.BlockSpec((part.shape[0], out_tile), lambda i: (0, second(i))) for part in parts
        ],
        scratch_shapes=[
            pltpu.VMEM((rows if len(parts) > 1 else 16, features), BF16),
            pltpu.VMEM((first_tiles, rows, tile), BF16),
        ],
        compiler_params=PARAMS,
        cost_estimate=pl.CostEstimate(
            flops=6 * rows * features * hidden,
            bytes_accessed=6 * features * hidden + 4 * rows * features,
            transcendentals=rows * hidden,
        ),
    )(*parts, gate_weight, up_weight, down_weight)


def prepare_kernel(tokens, gain, routes, gates, placement, *outs):
    experts = placement.shape[0]
    features = tokens.shape[1]
    chosen = gates[...] / jnp.sum(gates[...], axis=0, keepdims=True)
    columns = jnp.concatenate([routes[...].astype(F32), chosen]).T
    count = routes.shape[0]
    lanes = outs[0].shape[1] - features
    lane = lax.broadcasted_iota(I32, (1, lanes), 1)
    named = jnp.full((1, lanes), -1.0, F32)
    for e in range(experts):
        named = jnp.where(lane == e, placement[e].astype(F32), named)
    start = 0
    for out in outs:
        rows = out.shape[0]
        at = slice(start, start + rows)
        start += rows
        values = tokens[at].astype(F32)
        rescale = lax.rsqrt(jnp.mean(values * values, axis=-1, keepdims=True) + EPSILON)
        for c in range(features // LANES):
            to = slice(c * LANES, (c + 1) * LANES)
            out[:, to] = (values[:, to] * rescale * gain[c : c + 1].astype(F32)).astype(BF16)
        table = jnp.zeros((rows, lanes), F32)
        for k in range(count):
            held = columns[at, k : k + 1] == named
            table = jnp.where(held, columns[at, count + k : count + k + 1], table)
        out[:, features:] = table.astype(BF16)


def prepare(tokens, norm_gain, routes, route_gates, placement, sizes):
    features = tokens.shape[1]
    width = features + -(-placement.shape[0] // LANES) * LANES
    vmem = pl.BlockSpec(memory_space=pltpu.VMEM)
    return pl.pallas_call(
        prepare_kernel,
        out_shape=[jax.ShapeDtypeStruct((size, width), BF16) for size in sizes],
        in_specs=[vmem] * 4 + [pl.BlockSpec(memory_space=pltpu.SMEM)],
        compiler_params=PARAMS,
    )(tokens, norm_gain.reshape(-1, LANES), routes.T, route_gates.T, placement)


def to_experts(rows):
    return lax.all_to_all(rows, "node", 0, 0, tiled=True)


def total(own, parts):
    for part in parts:
        own = own + part.astype(F32)
    return own.astype(BF16)


def body(tokens, norm_gain, routes, route_gates, placement, gate_weight, up_weight, down_weight):
    nodes, peers = lax.axis_size("node"), lax.axis_size("local")
    node, local = lax.axis_index("node"), lax.axis_index("local")
    experts = placement.shape[0]
    features = tokens.shape[1]
    capacity = BLOCK_TOK * routes.shape[1] // experts * 3 // 2
    slots = experts * capacity
    half = features // 2
    weights = (gate_weight[0], up_weight[0], down_weight[0])
    sizes = [BLOCK_TOK, 2 * BLOCK_TOK, BLOCK_TOK]
    sent0, sent12, sent3 = prepare(tokens, norm_gain, routes, route_gates, placement, sizes)

    bits_a, bits_b = bit_order(nodes, False), bit_order(nodes, True)
    ids = jnp.stack([node, local]).astype(I32)
    near = ids, peers, capacity, features
    size = slots // peers
    cuts = [size * k for k in range(peers - 1)]
    cuts += [cuts[-1] + size // 3, cuts[-1] + size // 3 * 2, size * (peers - 1)]
    cuts += [slots - size // 3, slots]

    near0 = swaps([sent0] * peers, "local", 1, peers)
    pair = jnp.concatenate([sent3, swap(sent3, "node", bits_a[0])])
    rows_a = gather_doubling(pair[:, :half], "node", bits_a[1:-1])
    rows_b = gather_doubling(pair[:, half:], "node", bits_b[1:-1])
    sent12, rows_a, rows_b = fence([sent12, rows_a, rows_b], near0)
    rows_a = [rows_a, swap(rows_a, "node", bits_a[-1])]
    rows_b = [rows_b, swap(rows_b, "node", bits_b[-1])]
    chain = chain_step([sent12, sent12], "local", 1)
    outbound0, mixing0 = pick([sent0] + near0, 0, *near, chain_in=False, chain_out=True)
    outbound3, mixing3a, mixing3b = pick_cross(
        rows_a,
        rows_b,
        gathered_from(bits_a),
        gathered_from(bits_b),
        *near,
        cuts,
    )

    outbound0, *outbound3 = fence([outbound0] + outbound3, chain)
    arrived0 = to_experts(outbound0)
    parts12 = [sent12] + chain
    for step in range(2, peers):
        chain = chain_step(chain, "local", step)
        parts12 += chain
    own3, *outbound3 = outbound3
    last2, last1 = peers - 2, peers - 1
    third = [swap(outbound3[-5], "local", last2)]
    (late_ids,) = fence([ids], third)
    third.append(swap(outbound3[-4], "local", last2))
    outbound1, mixing1 = pick(parts12, 0, late_ids, *near[1:], chain_in=True, chain_out=False)
    (third[1],) = fence([third[1]], [outbound1])

    outbound1, ids, *later3 = fence(
        [outbound1, ids] + outbound3[:-5] + outbound3[-3:], [arrived0, third[1]]
    )
    arrived1 = to_experts(outbound1)
    early = [swap(part, "local", k + 1) for k, part in enumerate(later3[:-3])]
    third.append(swap(later3[-3], "local", last2))
    third.append(swap(later3[-2], "local", last1))
    outbound2, mixing2 = pick(parts12, 1, ids, *near[1:], chain_in=True, chain_out=False)
    (out0,) = expert([arrived0], *weights)

    outbound2, last3 = fence([outbound2, later3[-1]], [arrived1, out0] + early + third[2:])
    arrived2 = to_experts(outbound2)
    last3 = swap(last3, "local", last1)
    (out1,) = expert([arrived1], *weights)
    (last3,) = fence([last3], [out1])
    out3 = list(expert([own3] + early + third + [last3], *weights))

    out0, *out3 = fence([out0] + out3, [arrived2, out1])
    landed0 = to_experts(out0)
    landed3 = out3[:1] + swaps(out3, "local", 1, last1)
    landed3 += [swap(part, "local", last2) for part in out3[-4:-2]]
    (out2,) = expert([arrived2], *weights)

    out1, later3, mixing0 = fence([out1, out3[-2], mixing0], [landed0, out2] + landed3[1:])
    landed1 = to_experts(out1)
    landed3.append(swap(later3, "local", last1))
    own0, parts0 = chain_sum(*mix(mixing0, landed0), "local")

    out2, last3, mixing1 = fence([out2, out3[-1], mixing1], [landed1, landed3[-1]] + parts0)
    landed2 = to_experts(out2)
    landed3.append(swap(last3, "local", last1))
    own1, parts1 = mix(mixing1, landed1)
    parts1 = swaps([None] + parts1, "local", 1, peers)
    cross = mix_cross(mixing3a, mixing3b, landed3)
    piece0 = total(own0, parts0)

    own2, parts2 = mix(mixing2, landed2)
    parts2 = swaps([None] + parts2, "local", 1, peers)
    piece1 = total(own1, parts1)
    piece3 = jnp.concatenate(
        [sum_halving(*cross[:2], "node", bits_a), sum_halving(*cross[2:], "node", bits_b)], axis=1
    )
    piece2 = total(own2, parts2)
    return jnp.concatenate([piece0, piece1, piece2, piece3], axis=0)


def solution(mesh):
    rows = P(AXES, None)
    stacked = P(AXES, None, None)
    in_specs = (rows, P(), rows, rows, P(), stacked, stacked, stacked)
    return jax.shard_map(body, mesh=mesh, in_specs=in_specs, out_specs=rows, check_vma=False)
```

```python
import functools

import jax
import jax.numpy as jnp
import numpy as np
from jax import lax
from jax.experimental import pallas as pl
from jax.experimental.pallas import tpu as pltpu
from jax.sharding import PartitionSpec as P

BLOCK_TOK = 32
EPSILON = 1e-06
AXES = ("node", "local")
LANES = 128
TILES = 4
BF16, F32, I32 = jnp.bfloat16, jnp.float32, jnp.int32
ANYWHERE = pl.BlockSpec(memory_space=pl.ANY)
PARAMS = pltpu.CompilerParams(vmem_limit_bytes=60 * 2**20)


def fence(arrays, after):
    token = sum(a.reshape(-1, a.shape[-1])[:16, :LANES].astype(F32) for a in after)

    def kernel(*refs):
        pass

    return list(pl.pallas_call(
        kernel,
        out_shape=[jax.ShapeDtypeStruct(a.shape, a.dtype) for a in arrays],
        in_specs=[ANYWHERE] * (len(arrays) + 1),
        out_specs=[ANYWHERE] * len(arrays),
        input_output_aliases={i: i for i in range(len(arrays))},
    )(*arrays, token))


def swap(array, axis, bits):
    size = lax.axis_size(axis)
    return lax.ppermute(array, axis, [(i, i ^ bits) for i in range(size)])


def swaps(parts, axis, first, last):
    return [swap(parts[k], axis, k) for k in range(first, last)]


def bit_order(size, last_first):
    bits = [1 << i for i in range(size.bit_length() - 1)]
    return bits[:1] + bits[:0:-1] if last_first else bits


def chain_step(arrays, axis, step):
    size = lax.axis_size(axis)
    rightward = [(i, i + 1) for i in range(step - 1, size - 1)]
    leftward = [(size - 1 - i, size - 2 - i) for i in range(step - 1, size - 1)]
    return [lax.ppermute(a, axis, way) for a, way in zip(arrays, (rightward, leftward))]


def chain_offsets(size):
    return [0] + [offset for d in range(1, size) for offset in (-d, d)]


def chain_sum(own, parts, axis):
    size = lax.axis_size(axis)
    left, right = parts[0::2], parts[1::2]
    for step in range(1, size):
        ways = [(i, i + 1) for i in range(step)], [(size - 1 - i, size - 2 - i) for i in range(step)]
        moved = [
            lax.ppermute(side[size - 1 - step].astype(BF16), axis, way)
            for side, way in zip((right, left), ways)
        ]
        if step < size - 1:
            at = size - 2 - step
            right[at], left[at] = (
                side[at].astype(F32) + came.astype(F32) for side, came in zip((right, left), moved)
            )
    return own, moved


def gather_doubling(array, axis, bits):
    for bit in bits:
        array = jnp.concatenate([array, swap(array, axis, bit)])
    return array


def gathered_from(bits):
    found = [0]
    for bit in bits:
        found += [k ^ bit for k in found]
    return found


def sum_halving(keep, give, axis, bits):
    for step, bit in enumerate(bits[::-1]):
        if step:
            keep, give = jnp.split(keep, 2)
        keep = keep + swap(give.astype(BF16), axis, bit).astype(F32)
    return keep.astype(BF16)


def below(rows):
    at = np.arange(rows)
    same = at[:, None] // BLOCK_TOK == at[None, :] // BLOCK_TOK
    return (same & (at[None, :] < at[:, None])).astype(BF16)


def choose(table, lane, row_group, slot_group, turn, before):
    select = lax.broadcasted_iota(I32, (table.shape[1], lane.shape[1]), 0) == lane
    weight = jnp.dot(table, select.astype(BF16), preferred_element_type=F32)
    mask = jnp.where((weight > 0) & (row_group == slot_group), 1.0, 0.0)
    rank = jnp.dot(before, mask.astype(BF16), preferred_element_type=F32)
    place = jnp.where(rank == turn, mask, 0.0)
    return place.astype(BF16), (place * weight).astype(BF16)


def gather_rows(place, rows):
    return lax.dot_general(
        place, rows, (((0,), (0,)), ((), ())), preferred_element_type=F32
    ).astype(BF16)


def bits_of(labels, local, peers, chained):
    if not chained:
        return labels
    source = labels + local
    return jnp.where((source >= 0) & (source < peers), source ^ local, -1)


def pick_kernel(count, blocks, peers, chain_in, chain_out, ids, *refs):
    parts, refs = refs[:count], refs[count:]
    tables, refs = refs[:count], refs[count:]
    lane, slot_group, turn, before, in_column, in_row, out_column, out = refs[:8]
    mixings, places = refs[8 : 8 + blocks], refs[8 + blocks :]

    def rows_of(refs, block):
        return jnp.concatenate([r[block * BLOCK_TOK : (block + 1) * BLOCK_TOK] for r in refs])

    @pl.when(pl.program_id(0) == 0)
    def _():
        local = ids[1]
        row_group = bits_of(in_column[...], local, peers, chain_in)
        for block, (mixing, place) in enumerate(zip(mixings, places)):
            place[...], weights = choose(
                rows_of(tables, block),
                lane[...] + local,
                row_group,
                slot_group[...],
                turn[...],
                before[...],
            )
            if chain_in != chain_out:
                shape = mixing.shape[0], weights.shape[0]
                same = bits_of(out_column[...], local, peers, chain_out) == bits_of(
                    in_row[...], local, peers, chain_in
                )
                row = lax.broadcasted_iota(I32, shape, 0) & (BLOCK_TOK - 1)
                column = lax.broadcasted_iota(I32, shape, 1) & (BLOCK_TOK - 1)
                order = jnp.where(same & (row == column), 1.0, 0.0).astype(BF16)
                weights = jnp.dot(order, weights, preferred_element_type=F32).astype(BF16)
            mixing[...] = weights

    for block, place in enumerate(places):
        rows = lax.dot_general(
            place[...],
            rows_of(parts, block),
            (((0,), (0,)), ((), ())),
            preferred_element_type=F32,
        )
        nodes, _, size, tile = out.shape
        out[:, block] = rows.reshape(nodes, size, tile).astype(BF16)


def whole_block(array):
    return pl.BlockSpec(array.shape, lambda j: (0,) * array.ndim)


def by_token(labels):
    return np.repeat(np.array(labels, np.int32), BLOCK_TOK)


def pick(parts, ids, peers, capacity, features, chain_in, chain_out):
    nodes = lax.axis_size("node")
    held = parts[0].shape[0]
    blocks = held // BLOCK_TOK
    slots = nodes * peers * capacity
    slot = np.arange(slots, dtype=np.int32)[None, :]
    labels = chain_offsets(peers), list(range(peers))
    in_labels, out_labels = by_token(labels[not chain_in]), by_token(labels[not chain_out])
    rows, tile = len(in_labels), features // TILES
    small = (
        slot // (capacity * peers) * peers,
        slot // capacity % peers,
        (slot % capacity).astype(np.float32),
        below(rows),
        in_labels[:, None],
        in_labels[None, :],
        out_labels[:, None],
    )
    return pl.pallas_call(
        functools.partial(pick_kernel, len(parts), blocks, peers, chain_in, chain_out),
        grid=(TILES,),
        out_shape=[
            jax.ShapeDtypeStruct((nodes, blocks, peers * capacity, features), BF16),
        ]
        + [jax.ShapeDtypeStruct((len(out_labels), slots), BF16)] * blocks,
        in_specs=[pl.BlockSpec(memory_space=pltpu.SMEM)]
        + [pl.BlockSpec((held, tile), lambda j: (0, j))] * len(parts)
        + [pl.BlockSpec((held, LANES), lambda j: (0, features // LANES))] * len(parts)
        + [whole_block(a) for a in small],
        out_specs=[
            pl.BlockSpec((nodes, blocks, peers * capacity, tile), lambda j: (0, 0, 0, j)),
        ]
        + [pl.BlockSpec((len(out_labels), slots), lambda j: (0, 0))] * blocks,
        scratch_shapes=[pltpu.VMEM((rows, slots), BF16)] * blocks,
        compiler_params=PARAMS,
        cost_estimate=pl.CostEstimate(
            flops=2 * blocks * rows * slots * features,
            bytes_accessed=2 * blocks * (rows + slots) * features,
            transcendentals=0,
        ),
    )(ids, *parts, *parts, *small)


def pick_cross_kernel(order, cuts, peers, ids, a0, a1, b0, b1, t0, t1, *refs):
    peer, group_a, group_b, slot_group, turn, before = refs[:6]
    outs, (mixing_a, mixing_b, place_a, place_b) = refs[6:-4], refs[-4:]
    step = pl.program_id(0)

    @pl.when(step == 0)
    def _():
        known = jnp.concatenate([t0[...], t1[...]])
        lane = (peer[...] ^ ids[1]) + ids[0] * peers
        common = slot_group[...], turn[...], before[...]
        place_b[...], mixing_b[...] = choose(known, lane, group_b[...], *common)
        back = [order.index(k) * BLOCK_TOK for k in range(len(order))]
        known = jnp.concatenate([known[at : at + BLOCK_TOK] for at in back])
        place_a[...], mixing_a[...] = choose(known, lane, group_a[...], *common)

    def store(place, first_rows, last_rows):
        result = gather_rows(place[...], jnp.concatenate([first_rows[...], last_rows[...]]))
        for out, first, last in zip(outs, cuts[:-1], cuts[1:]):
            out[...] = result[first:last]

    @pl.when(step < TILES // 2)
    def _():
        store(place_a, a0, a1)

    @pl.when(step >= TILES // 2)
    def _():
        store(place_b, b0, b1)


def in_first_half(shape):
    return pl.BlockSpec(shape, lambda j: (0, jnp.minimum(j, TILES // 2 - 1)))


def in_second_half(shape):
    return pl.BlockSpec(shape, lambda j: (0, jnp.maximum(j - TILES // 2, 0)))


def pick_cross(rows_a, rows_b, order_a, order_b, ids, peers, capacity, features, cuts):
    part = rows_a[0].shape[0]
    rows = 2 * part
    nodes = rows // BLOCK_TOK
    slots = cuts[-1]
    slot = np.arange(slots, dtype=np.int32)[None, :]
    tile = features // TILES
    small = (
        slot // (capacity * nodes),
        by_token(order_a)[:, None],
        by_token(order_b)[:, None],
        slot // capacity % nodes,
        (slot % capacity).astype(np.float32),
        below(rows),
    )
    sizes = [last - first for first, last in zip(cuts[:-1], cuts[1:])]
    results = pl.pallas_call(
        functools.partial(pick_cross_kernel, order_b, cuts, peers),
        grid=(TILES,),
        out_shape=[jax.ShapeDtypeStruct((size, features), BF16) for size in sizes]
        + [jax.ShapeDtypeStruct((rows, slots), BF16)] * 2,
        in_specs=[pl.BlockSpec(memory_space=pltpu.SMEM)]
        + [in_first_half((part, tile))] * 2
        + [in_second_half((part, tile))] * 2
        + [pl.BlockSpec((part, LANES), lambda j: (0, features // 2 // LANES))] * 2
        + [whole_block(a) for a in small],
        out_specs=[pl.BlockSpec((size, tile), lambda j: (0, j)) for size in sizes]
        + [pl.BlockSpec((rows, slots), lambda j: (0, 0))] * 2,
        scratch_shapes=[pltpu.VMEM((rows, slots), BF16)] * 2,
        compiler_params=PARAMS,
        cost_estimate=pl.CostEstimate(
            flops=2 * rows * slots * features,
            bytes_accessed=2 * (rows + slots) * features,
            transcendentals=0,
        ),
    )(ids, *rows_a, *rows_b, *rows_b, *small)
    return list(results[:-2]), results[-2], results[-1]


def mix_kernel(mixing, landed, own, *outs):
    result = jnp.dot(mixing[...], landed[...], preferred_element_type=F32)
    own[...] = result[:BLOCK_TOK]
    for k, out in enumerate(outs):
        out[...] = result[(k + 1) * BLOCK_TOK : (k + 2) * BLOCK_TOK].astype(BF16)


def mix(mixing, landed):
    rows, slots = mixing.shape
    features = landed.shape[1]
    tile = features // TILES
    count = rows // BLOCK_TOK
    own, *parts = pl.pallas_call(
        mix_kernel,
        grid=(TILES,),
        out_shape=[jax.ShapeDtypeStruct((BLOCK_TOK, features), F32)]
        + [jax.ShapeDtypeStruct((BLOCK_TOK, features), BF16)] * (count - 1),
        in_specs=[whole_block(mixing), pl.BlockSpec((slots, tile), lambda j: (0, j))],
        out_specs=[pl.BlockSpec((BLOCK_TOK, tile), lambda j: (0, j))] * count,
        compiler_params=PARAMS,
        cost_estimate=pl.CostEstimate(
            flops=2 * rows * slots * features,
            bytes_accessed=2 * (rows + slots) * features,
            transcendentals=0,
        ),
    )(mixing, landed)
    return own, parts


def mix_cross_kernel(mixing_a, mixing_b, *refs):
    landed, (keep_a, give_a, keep_b, give_b) = refs[:-4], refs[-4:]
    step = pl.program_id(0)
    half = keep_a.shape[0]
    rows = jnp.concatenate([part[...] for part in landed])

    def store(mixing, keep, give):
        result = jnp.dot(mixing[...], rows, preferred_element_type=F32)
        keep[...] = result[:half]
        give[...] = result[half:].astype(BF16)

    @pl.when(step < TILES // 2)
    def _():
        store(mixing_a, keep_a, give_a)

    @pl.when(step >= TILES // 2)
    def _():
        store(mixing_b, keep_b, give_b)


def mix_cross(mixing_a, mixing_b, landed):
    rows, slots = mixing_a.shape
    features = landed[0].shape[1]
    tile = features // TILES
    shape = (rows // 2, features // 2)
    return pl.pallas_call(
        mix_cross_kernel,
        grid=(TILES,),
        out_shape=[jax.ShapeDtypeStruct(shape, F32), jax.ShapeDtypeStruct(shape, BF16)] * 2,
        in_specs=[whole_block(mixing_a), whole_block(mixing_b)]
        + [pl.BlockSpec((part.shape[0], tile), lambda j: (0, j)) for part in landed],
        out_specs=[in_first_half((rows // 2, tile))] * 2 + [in_second_half((rows // 2, tile))] * 2,
        compiler_params=PARAMS,
        cost_estimate=pl.CostEstimate(
            flops=2 * rows * slots * features,
            bytes_accessed=2 * (rows + slots) * features,
            transcendentals=0,
        ),
    )(mixing_a, mixing_b, *landed)


def expert_kernel(count, first_tiles, split, tie, *refs):
    parts, (gate_ref, up_ref, down_ref) = refs[:count], refs[count : count + 3]
    outs, (joined, hidden) = refs[count + 3 : -2], refs[-2:]
    step = pl.program_id(0)
    x_ref = parts[0] if count == 1 else joined

    if count > 1:

        @pl.when(step == 0)
        def _():
            joined[...] = jnp.concatenate([part[...] for part in parts])

    @pl.when(step < first_tiles)
    def _():
        x = x_ref[...]
        gate_pre = jnp.dot(x, gate_ref[...], preferred_element_type=F32)
        up_pre = jnp.dot(x, up_ref[...], preferred_element_type=F32)
        hidden[step] = (gate_pre / (1 + jnp.exp(-gate_pre)) * up_pre).astype(BF16)

    @pl.when(step >= first_tiles)
    def _():
        rows = jnp.concatenate([hidden[i] for i in range(first_tiles)], axis=1)
        result = jnp.dot(rows, down_ref[...], preferred_element_type=F32)
        if split is not None:
            result = result.reshape(*split, result.shape[1])
            for block, out in enumerate(outs):
                out[...] = result[:, block].reshape(out.shape).astype(BF16)
            return
        result = result.astype(BF16)
        at = 0
        for out in outs:
            out[...] = result[at : at + out.shape[0]]
            at += out.shape[0]


def expert(parts, tie, gate_weight, up_weight, down_weight):
    split = None
    sizes = [part.shape[0] for part in parts]
    if parts[0].ndim == 4:
        (part,) = parts
        split = part.shape[:3]
        parts = [part.reshape(-1, part.shape[3])]
        sizes = [split[0] * split[2]] * split[1]
    rows = sum(part.shape[0] for part in parts)
    features, hidden = gate_weight.shape
    tile = 256
    first_tiles = hidden // tile
    out_tile = features // TILES

    def first(i):
        return jnp.minimum(i, first_tiles - 1)

    def second(i):
        return jnp.maximum(i - first_tiles, 0)

    return pl.pallas_call(
        functools.partial(expert_kernel, len(parts), first_tiles, split),
        grid=(first_tiles + TILES,),
        out_shape=[jax.ShapeDtypeStruct((size, features), BF16) for size in sizes],
        in_specs=[pl.BlockSpec(memory_space=pltpu.SMEM)]
        + [whole_block(part) for part in parts]
        + [
            pl.BlockSpec((features, tile), lambda i: (0, first(i))),
            pl.BlockSpec((features, tile), lambda i: (0, first(i))),
            pl.BlockSpec((hidden, out_tile), lambda i: (0, second(i))),
        ],
        out_specs=[
            pl.BlockSpec((size, out_tile), lambda i: (0, second(i))) for size in sizes
        ],
        scratch_shapes=[
            pltpu.VMEM((rows if len(parts) > 1 else 16, features), BF16),
            pltpu.VMEM((first_tiles, rows, tile), BF16),
        ],
        compiler_params=PARAMS,
        cost_estimate=pl.CostEstimate(
            flops=6 * rows * features * hidden,
            bytes_accessed=6 * features * hidden + 4 * rows * features,
            transcendentals=rows * hidden,
        ),
    )(tie, *parts, gate_weight, up_weight, down_weight)


def prepare_kernel(tokens, gain, routes, gates, placement, *outs):
    experts = placement.shape[0]
    features = tokens.shape[1]
    chosen = gates[...] / jnp.sum(gates[...], axis=0, keepdims=True)
    columns = jnp.concatenate([routes[...].astype(F32), chosen]).T
    count = routes.shape[0]
    lanes = outs[0].shape[1] - features
    lane = lax.broadcasted_iota(I32, (1, lanes), 1)
    named = jnp.full((1, lanes), -1.0, F32)
    for e in range(experts):
        named = jnp.where(lane == e, placement[e].astype(F32), named)
    start = 0
    for out in outs:
        rows = out.shape[0]
        at = slice(start, start + rows)
        start += rows
        values = tokens[at].astype(F32)
        rescale = lax.rsqrt(jnp.mean(values * values, axis=-1, keepdims=True) + EPSILON)
        for c in range(features // LANES):
            to = slice(c * LANES, (c + 1) * LANES)
            out[:, to] = (values[:, to] * rescale * gain[c : c + 1].astype(F32)).astype(BF16)
        table = jnp.zeros((rows, lanes), F32)
        for k in range(count):
            held = columns[at, k : k + 1] == named
            table = jnp.where(held, columns[at, count + k : count + k + 1], table)
        out[:, features:] = table.astype(BF16)


def prepare(tokens, norm_gain, routes, route_gates, placement, sizes):
    features = tokens.shape[1]
    width = features + -(-placement.shape[0] // LANES) * LANES
    vmem = pl.BlockSpec(memory_space=pltpu.VMEM)
    return pl.pallas_call(
        prepare_kernel,
        out_shape=[jax.ShapeDtypeStruct((size, width), BF16) for size in sizes],
        in_specs=[vmem] * 4 + [pl.BlockSpec(memory_space=pltpu.SMEM)],
        compiler_params=PARAMS,
    )(tokens, norm_gain.reshape(-1, LANES), routes.T, route_gates.T, placement)


def to_experts(rows):
    return lax.all_to_all(rows, "node", 0, 0, tiled=True)


def total(own, parts):
    for part in parts:
        own = own + part.astype(F32)
    return own.astype(BF16)


def body(tokens, norm_gain, routes, route_gates, placement, gate_weight, up_weight, down_weight):
    nodes, peers = lax.axis_size("node"), lax.axis_size("local")
    node, local = lax.axis_index("node"), lax.axis_index("local")
    experts = placement.shape[0]
    features = tokens.shape[1]
    capacity = BLOCK_TOK * routes.shape[1] // experts * 3 // 2
    slots = experts * capacity
    half = features // 2
    weights = (gate_weight[0], up_weight[0], down_weight[0])
    sizes = [BLOCK_TOK, 2 * BLOCK_TOK, BLOCK_TOK]
    sent0, sent12, sent3 = prepare(tokens, norm_gain, routes, route_gates, placement, sizes)

    bits_a, bits_b = bit_order(nodes, False), bit_order(nodes, True)
    ids = jnp.stack([node, local]).astype(I32)
    near = ids, peers, capacity, features
    cuts = [slots // peers * k for k in range(peers + 1)]

    near0 = swaps([sent0] * peers, "local", 1, peers)
    pair = jnp.concatenate([sent3, swap(sent3, "node", bits_a[0])])
    rows_a = gather_doubling(pair[:, :half], "node", bits_a[1:-1])
    rows_b = gather_doubling(pair[:, half:], "node", bits_b[1:-1])
    sent12, rows_a, rows_b = fence([sent12, rows_a, rows_b], near0)
    rows_a = [rows_a, swap(rows_a, "node", bits_a[-1])]
    rows_b = [rows_b, swap(rows_b, "node", bits_b[-1])]
    chain = chain_step([sent12, sent12], "local", 1)
    outbound0, mixing0 = pick([sent0] + near0, *near, chain_in=False, chain_out=True)

    outbound0, *last_rows = fence([outbound0, rows_a[1], rows_b[1]], chain)
    arrived0 = to_experts(outbound0)
    parts12 = [sent12] + chain
    for step in range(2, peers):
        chain = chain_step(chain, "local", step)
        parts12 += chain
    outbound3, mixing3a, mixing3b = pick_cross(
        [rows_a[0], last_rows[0]],
        [rows_b[0], last_rows[1]],
        gathered_from(bits_a),
        gathered_from(bits_b),
        *near,
        cuts,
    )
    outbound12, mixing1, mixing2 = pick(parts12, *near, chain_in=True, chain_out=False)

    own3, *outbound3 = outbound3
    outbound12, *outbound3 = fence([outbound12] + outbound3, [arrived0])
    arrived12 = to_experts(outbound12)
    arrived3 = swaps([None] + outbound3, "local", 1, peers)
    (out0,) = expert([arrived0.reshape(slots, features)], ids, *weights)

    out0, tie = fence([out0, ids], [arrived12] + arrived3)
    landed0 = to_experts(out0)
    out3 = list(expert([own3] + arrived3, tie, *weights))
    landed3 = out3[:1] + swaps(out3, "local", 1, peers - 1)
    out1, out2 = expert([arrived12], tie, *weights)

    (mixing0,) = fence([mixing0], [out1])
    out1, last3 = fence([out1, out3[-1]], [landed0, out2] + landed3[1:])
    landed1 = to_experts(out1)
    landed3.append(swap(last3, "local", peers - 1))
    own0, parts0 = chain_sum(*mix(mixing0, landed0), "local")

    (out2,) = fence([out2], [landed1, landed3[-1]] + parts0)
    landed2 = to_experts(out2)
    own1, parts1 = mix(mixing1, landed1)
    parts1 = swaps([None] + parts1, "local", 1, peers)
    cross = mix_cross(mixing3a, mixing3b, landed3)
    piece0 = total(own0, parts0)

    cross = fence(list(cross), [landed2])
    (mixing2,) = fence([mixing2], [cross[1]])
    own2, parts2 = mix(mixing2, landed2)
    parts2 = swaps([None] + parts2, "local", 1, peers)
    piece1 = total(own1, parts1)
    piece3 = jnp.concatenate(
        [sum_halving(*cross[:2], "node", bits_a), sum_halving(*cross[2:], "node", bits_b)], axis=1
    )
    piece2 = total(own2, parts2)
    return jnp.concatenate([piece0, piece1, piece2, piece3], axis=0)


def solution(mesh):
    rows = P(AXES, None)
    stacked = P(AXES, None, None)
    in_specs = (rows, P(), rows, rows, P(), stacked, stacked, stacked)
    return jax.shard_map(body, mesh=mesh, in_specs=in_specs, out_specs=rows, check_vma=False)
```

```python
import functools

import jax
import jax.numpy as jnp
import numpy as np
from jax import lax
from jax.experimental import pallas as pl
from jax.experimental.pallas import tpu as pltpu
from jax.sharding import PartitionSpec as P

BLOCK_TOK = 32
EPSILON = 1e-06
AXES = ("node", "local")
LANES = 128
TILES = 4
BF16, F32, I32 = jnp.bfloat16, jnp.float32, jnp.int32
ANYWHERE = pl.BlockSpec(memory_space=pl.ANY)
PARAMS = pltpu.CompilerParams(vmem_limit_bytes=60 * 2**20)


def fence(arrays, after):
    token = sum(a.reshape(-1, a.shape[-1])[:16, :LANES].astype(F32) for a in after)

    def kernel(*refs):
        pass

    return list(pl.pallas_call(
        kernel,
        out_shape=[jax.ShapeDtypeStruct(a.shape, a.dtype) for a in arrays],
        in_specs=[ANYWHERE] * (len(arrays) + 1),
        out_specs=[ANYWHERE] * len(arrays),
        input_output_aliases={i: i for i in range(len(arrays))},
    )(*arrays, token))


def swap(array, axis, bits):
    size = lax.axis_size(axis)
    return lax.ppermute(array, axis, [(i, i ^ bits) for i in range(size)])


def swaps(parts, axis, first, last):
    return [swap(parts[k], axis, k) for k in range(first, last)]


def bit_order(size, last_first):
    bits = [1 << i for i in range(size.bit_length() - 1)]
    return bits[:1] + bits[:0:-1] if last_first else bits


def chain_step(arrays, axis, step):
    size = lax.axis_size(axis)
    rightward = [(i, i + 1) for i in range(step - 1, size - 1)]
    leftward = [(size - 1 - i, size - 2 - i) for i in range(step - 1, size - 1)]
    return [lax.ppermute(a, axis, way) for a, way in zip(arrays, (rightward, leftward))]


def chain_offsets(size):
    return [0] + [offset for d in range(1, size) for offset in (-d, d)]


def chain_sum_step(parts, axis, step, moved=None):
    size = lax.axis_size(axis)
    at = size - 1 - step
    sides = parts[1::2][at], parts[0::2][at]
    if moved is not None:
        sides = [side.astype(F32) + came.astype(F32) for side, came in zip(sides, moved)]
    ways = [(i, i + 1) for i in range(step)], [(size - 1 - i, size - 2 - i) for i in range(step)]
    return [lax.ppermute(side.astype(BF16), axis, way) for side, way in zip(sides, ways)]


def gather_doubling(array, axis, bits):
    for bit in bits:
        array = jnp.concatenate([array, swap(array, axis, bit)])
    return array


def gathered_from(bits):
    found = [0]
    for bit in bits:
        found += [k ^ bit for k in found]
    return found


def halve(keep, give, axis, bit):
    return keep + swap(give.astype(BF16), axis, bit).astype(F32)


def sum_halving(array, axis, bits):
    for bit in bits[::-1]:
        array = halve(*jnp.split(array, 2), axis, bit)
    return array.astype(BF16)


def below(rows):
    at = np.arange(rows)
    same = at[:, None] // BLOCK_TOK == at[None, :] // BLOCK_TOK
    return (same & (at[None, :] < at[:, None])).astype(BF16)


def choose(table, lane, row_group, slot_group, turn, before):
    select = lax.broadcasted_iota(I32, (table.shape[1], lane.shape[1]), 0) == lane
    weight = jnp.dot(table, select.astype(BF16), preferred_element_type=F32)
    mask = jnp.where((weight > 0) & (row_group == slot_group), 1.0, 0.0)
    rank = jnp.dot(before, mask.astype(BF16), preferred_element_type=F32)
    place = jnp.where(rank == turn, mask, 0.0)
    return place.astype(BF16), (place * weight).astype(BF16)


def gather_rows(place, rows):
    return lax.dot_general(
        place, rows, (((0,), (0,)), ((), ())), preferred_element_type=F32
    ).astype(BF16)


def bits_of(labels, local, peers, chained):
    if not chained:
        return labels
    source = labels + local
    return jnp.where((source >= 0) & (source < peers), source ^ local, -1)


def pick_kernel(count, blocks, peers, chain_in, chain_out, ids, *refs):
    parts, refs = refs[:count], refs[count:]
    tables, refs = refs[:count], refs[count:]
    lane, slot_group, turn, before, in_column, in_row, out_column, out = refs[:8]
    mixings, places = refs[8 : 8 + blocks], refs[8 + blocks :]

    def rows_of(refs, block):
        return jnp.concatenate([r[block * BLOCK_TOK : (block + 1) * BLOCK_TOK] for r in refs])

    @pl.when(pl.program_id(0) == 0)
    def _():
        local = ids[1]
        row_group = bits_of(in_column[...], local, peers, chain_in)
        for block, (mixing, place) in enumerate(zip(mixings, places)):
            place[...], weights = choose(
                rows_of(tables, block),
                lane[...] + local,
                row_group,
                slot_group[...],
                turn[...],
                before[...],
            )
            if chain_in != chain_out:
                shape = mixing.shape[0], weights.shape[0]
                same = bits_of(out_column[...], local, peers, chain_out) == bits_of(
                    in_row[...], local, peers, chain_in
                )
                row = lax.broadcasted_iota(I32, shape, 0) & (BLOCK_TOK - 1)
                column = lax.broadcasted_iota(I32, shape, 1) & (BLOCK_TOK - 1)
                order = jnp.where(same & (row == column), 1.0, 0.0).astype(BF16)
                weights = jnp.dot(order, weights, preferred_element_type=F32).astype(BF16)
            mixing[...] = weights

    for block, place in enumerate(places):
        rows = lax.dot_general(
            place[...],
            rows_of(parts, block),
            (((0,), (0,)), ((), ())),
            preferred_element_type=F32,
        )
        nodes, _, size, tile = out.shape
        out[:, block] = rows.reshape(nodes, size, tile).astype(BF16)


def whole_block(array):
    return pl.BlockSpec(array.shape, lambda j: (0,) * array.ndim)


def by_token(labels):
    return np.repeat(np.array(labels, np.int32), BLOCK_TOK)


def pick(parts, ids, peers, capacity, features, chain_in, chain_out):
    nodes = lax.axis_size("node")
    held = parts[0].shape[0]
    blocks = held // BLOCK_TOK
    slots = nodes * peers * capacity
    slot = np.arange(slots, dtype=np.int32)[None, :]
    labels = chain_offsets(peers), list(range(peers))
    in_labels, out_labels = by_token(labels[not chain_in]), by_token(labels[not chain_out])
    rows, tile = len(in_labels), features // TILES
    small = (
        slot // (capacity * peers) * peers,
        slot // capacity % peers,
        (slot % capacity).astype(np.float32),
        below(rows),
        in_labels[:, None],
        in_labels[None, :],
        out_labels[:, None],
    )
    return pl.pallas_call(
        functools.partial(pick_kernel, len(parts), blocks, peers, chain_in, chain_out),
        grid=(TILES,),
        out_shape=[
            jax.ShapeDtypeStruct((nodes, blocks, peers * capacity, features), BF16),
        ]
        + [jax.ShapeDtypeStruct((len(out_labels), slots), BF16)] * blocks,
        in_specs=[pl.BlockSpec(memory_space=pltpu.SMEM)]
        + [pl.BlockSpec((held, tile), lambda j: (0, j))] * len(parts)
        + [pl.BlockSpec((held, LANES), lambda j: (0, features // LANES))] * len(parts)
        + [whole_block(a) for a in small],
        out_specs=[
            pl.BlockSpec((nodes, blocks, peers * capacity, tile), lambda j: (0, 0, 0, j)),
        ]
        + [pl.BlockSpec((len(out_labels), slots), lambda j: (0, 0))] * blocks,
        scratch_shapes=[pltpu.VMEM((rows, slots), BF16)] * blocks,
        compiler_params=PARAMS,
        cost_estimate=pl.CostEstimate(
            flops=2 * blocks * rows * slots * features,
            bytes_accessed=2 * blocks * (rows + slots) * features,
            transcendentals=0,
        ),
    )(ids, *parts, *parts, *small)


def pick_cross_kernel(order, cuts, peers, ids, a0, a1, b0, b1, t0, t1, *refs):
    peer, group_a, group_b, slot_group, turn, before = refs[:6]
    outs, (mixing_a, mixing_b, place_a, place_b) = refs[6:-4], refs[-4:]
    step = pl.program_id(0)

    @pl.when(step == 0)
    def _():
        known = jnp.concatenate([t0[...], t1[...]])
        lane = (peer[...] ^ ids[1]) + ids[0] * peers
        common = slot_group[...], turn[...], before[...]
        place_b[...], mixing_b[...] = choose(known, lane, group_b[...], *common)
        back = [order.index(k) * BLOCK_TOK for k in range(len(order))]
        known = jnp.concatenate([known[at : at + BLOCK_TOK] for at in back])
        place_a[...], mixing_a[...] = choose(known, lane, group_a[...], *common)

    def store(place, first_rows, last_rows):
        result = gather_rows(place[...], jnp.concatenate([first_rows[...], last_rows[...]]))
        for out, first, last in zip(outs, cuts[:-1], cuts[1:]):
            out[...] = result[first:last]

    @pl.when(step < TILES // 2)
    def _():
        store(place_a, a0, a1)

    @pl.when(step >= TILES // 2)
    def _():
        store(place_b, b0, b1)


def in_first_half(shape):
    return pl.BlockSpec(shape, lambda j: (0, jnp.minimum(j, TILES // 2 - 1)))


def in_second_half(shape):
    return pl.BlockSpec(shape, lambda j: (0, jnp.maximum(j - TILES // 2, 0)))


def pick_cross(rows_a, rows_b, order_a, order_b, ids, peers, capacity, features, cuts):
    part = rows_a[0].shape[0]
    rows = 2 * part
    nodes = rows // BLOCK_TOK
    slots = cuts[-1]
    slot = np.arange(slots, dtype=np.int32)[None, :]
    tile = features // TILES
    small = (
        slot // (capacity * nodes),
        by_token(order_a)[:, None],
        by_token(order_b)[:, None],
        slot // capacity % nodes,
        (slot % capacity).astype(np.float32),
        below(rows),
    )
    sizes = [last - first for first, last in zip(cuts[:-1], cuts[1:])]
    results = pl.pallas_call(
        functools.partial(pick_cross_kernel, order_b, cuts, peers),
        grid=(TILES,),
        out_shape=[jax.ShapeDtypeStruct((size, features), BF16) for size in sizes]
        + [jax.ShapeDtypeStruct((rows, slots), BF16)] * 2,
        in_specs=[pl.BlockSpec(memory_space=pltpu.SMEM)]
        + [in_first_half((part, tile))] * 2
        + [in_second_half((part, tile))] * 2
        + [pl.BlockSpec((part, LANES), lambda j: (0, features // 2 // LANES))] * 2
        + [whole_block(a) for a in small],
        out_specs=[pl.BlockSpec((size, tile), lambda j: (0, j)) for size in sizes]
        + [pl.BlockSpec((rows, slots), lambda j: (0, 0))] * 2,
        scratch_shapes=[pltpu.VMEM((rows, slots), BF16)] * 2,
        compiler_params=PARAMS,
        cost_estimate=pl.CostEstimate(
            flops=2 * rows * slots * features,
            bytes_accessed=2 * (rows + slots) * features,
            transcendentals=0,
        ),
    )(ids, *rows_a, *rows_b, *rows_b, *small)
    return list(results[:-2]), results[-2], results[-1]


def mix_kernel(mixing, landed, own, *outs):
    result = jnp.dot(mixing[...], landed[...], preferred_element_type=F32)
    own[...] = result[:BLOCK_TOK]
    for k, out in enumerate(outs):
        out[...] = result[(k + 1) * BLOCK_TOK : (k + 2) * BLOCK_TOK].astype(BF16)


def mix(mixing, landed):
    rows, slots = mixing.shape
    features = landed.shape[1]
    tile = features // TILES
    count = rows // BLOCK_TOK
    own, *parts = pl.pallas_call(
        mix_kernel,
        grid=(TILES,),
        out_shape=[jax.ShapeDtypeStruct((BLOCK_TOK, features), F32)]
        + [jax.ShapeDtypeStruct((BLOCK_TOK, features), BF16)] * (count - 1),
        in_specs=[whole_block(mixing), pl.BlockSpec((slots, tile), lambda j: (0, j))],
        out_specs=[pl.BlockSpec((BLOCK_TOK, tile), lambda j: (0, j))] * count,
        compiler_params=PARAMS,
        cost_estimate=pl.CostEstimate(
            flops=2 * rows * slots * features,
            bytes_accessed=2 * (rows + slots) * features,
            transcendentals=0,
        ),
    )(mixing, landed)
    return own, parts


def mix_cross_kernel(mixing_a, mixing_b, *refs):
    landed, (keep_a, give_a, keep_b, give_b) = refs[:-4], refs[-4:]
    step = pl.program_id(0)
    half = keep_a.shape[0]
    rows = jnp.concatenate([part[...] for part in landed])

    def store(mixing, keep, give):
        result = jnp.dot(mixing[...], rows, preferred_element_type=F32)
        keep[...] = result[:half]
        give[...] = result[half:].astype(BF16)

    @pl.when(step < TILES // 2)
    def _():
        store(mixing_a, keep_a, give_a)

    @pl.when(step >= TILES // 2)
    def _():
        store(mixing_b, keep_b, give_b)


def mix_cross(mixing_a, mixing_b, landed):
    rows, slots = mixing_a.shape
    features = landed[0].shape[1]
    tile = features // TILES
    shape = (rows // 2, features // 2)
    return pl.pallas_call(
        mix_cross_kernel,
        grid=(TILES,),
        out_shape=[jax.ShapeDtypeStruct(shape, F32), jax.ShapeDtypeStruct(shape, BF16)] * 2,
        in_specs=[whole_block(mixing_a), whole_block(mixing_b)]
        + [pl.BlockSpec((part.shape[0], tile), lambda j: (0, j)) for part in landed],
        out_specs=[in_first_half((rows // 2, tile))] * 2 + [in_second_half((rows // 2, tile))] * 2,
        compiler_params=PARAMS,
        cost_estimate=pl.CostEstimate(
            flops=2 * rows * slots * features,
            bytes_accessed=2 * (rows + slots) * features,
            transcendentals=0,
        ),
    )(mixing_a, mixing_b, *landed)


def expert_kernel(count, first_tiles, nodes, tie, *refs):
    parts, (gate_ref, up_ref, down_ref) = refs[:count], refs[count : count + 3]
    outs, (joined, hidden) = refs[count + 3 : -2], refs[-2:]
    step = pl.program_id(0)
    x_ref = parts[0] if count == 1 and not nodes else joined

    if x_ref is joined:

        @pl.when(step == 0)
        def _():
            pieces = [parts[0][n, 0] for n in range(nodes)] or [part[...] for part in parts]
            joined[...] = jnp.concatenate(pieces)

    @pl.when(step < first_tiles)
    def _():
        x = x_ref[...]
        gate_pre = jnp.dot(x, gate_ref[...], preferred_element_type=F32)
        up_pre = jnp.dot(x, up_ref[...], preferred_element_type=F32)
        hidden[step] = (gate_pre / (1 + jnp.exp(-gate_pre)) * up_pre).astype(BF16)

    @pl.when(step >= first_tiles)
    def _():
        rows = jnp.concatenate([hidden[i] for i in range(first_tiles)], axis=1)
        result = jnp.dot(rows, down_ref[...], preferred_element_type=F32)
        result = result.astype(BF16)
        at = 0
        for out in outs:
            out[...] = result[at : at + out.shape[0]]
            at += out.shape[0]


def expert(parts, tie, gate_weight, up_weight, down_weight, block=None):
    sizes = [part.shape[0] for part in parts]
    specs = [whole_block(part) for part in parts]
    nodes = 0
    if block is not None:
        nodes, _, size, features = parts[0].shape
        sizes = [nodes * size]
        specs = [pl.BlockSpec((nodes, 1, size, features), lambda i: (0, block, 0, 0))]
    rows = sum(sizes)
    features, hidden = gate_weight.shape
    tile = 256
    first_tiles = hidden // tile
    out_tile = features // TILES

    def first(i):
        return jnp.minimum(i, first_tiles - 1)

    def second(i):
        return jnp.maximum(i - first_tiles, 0)

    return pl.pallas_call(
        functools.partial(expert_kernel, len(parts), first_tiles, nodes),
        grid=(first_tiles + TILES,),
        out_shape=[jax.ShapeDtypeStruct((size, features), BF16) for size in sizes],
        in_specs=[pl.BlockSpec(memory_space=pltpu.SMEM)]
        + specs
        + [
            pl.BlockSpec((features, tile), lambda i: (0, first(i))),
            pl.BlockSpec((features, tile), lambda i: (0, first(i))),
            pl.BlockSpec((hidden, out_tile), lambda i: (0, second(i))),
        ],
        out_specs=[
            pl.BlockSpec((size, out_tile), lambda i: (0, second(i))) for size in sizes
        ],
        scratch_shapes=[
            pltpu.VMEM((rows if nodes or len(parts) > 1 else 16, features), BF16),
            pltpu.VMEM((first_tiles, rows, tile), BF16),
        ],
        compiler_params=PARAMS,
        cost_estimate=pl.CostEstimate(
            flops=6 * rows * features * hidden,
            bytes_accessed=6 * features * hidden + 4 * rows * features,
            transcendentals=rows * hidden,
        ),
    )(tie, *parts, gate_weight, up_weight, down_weight)


def prepare_kernel(tokens, gain, routes, gates, placement, *outs):
    experts = placement.shape[0]
    features = tokens.shape[1]
    chosen = gates[...] / jnp.sum(gates[...], axis=0, keepdims=True)
    columns = jnp.concatenate([routes[...].astype(F32), chosen]).T
    count = routes.shape[0]
    lanes = outs[0].shape[1] - features
    lane = lax.broadcasted_iota(I32, (1, lanes), 1)
    named = jnp.full((1, lanes), -1.0, F32)
    for e in range(experts):
        named = jnp.where(lane == e, placement[e].astype(F32), named)
    start = 0
    for out in outs:
        rows = out.shape[0]
        at = slice(start, start + rows)
        start += rows
        values = tokens[at].astype(F32)
        rescale = lax.rsqrt(jnp.mean(values * values, axis=-1, keepdims=True) + EPSILON)
        for c in range(features // LANES):
            to = slice(c * LANES, (c + 1) * LANES)
            out[:, to] = (values[:, to] * rescale * gain[c : c + 1].astype(F32)).astype(BF16)
        table = jnp.zeros((rows, lanes), F32)
        for k in range(count):
            held = columns[at, k : k + 1] == named
            table = jnp.where(held, columns[at, count + k : count + k + 1], table)
        out[:, features:] = table.astype(BF16)


def prepare(tokens, norm_gain, routes, route_gates, placement, sizes):
    features = tokens.shape[1]
    width = features + -(-placement.shape[0] // LANES) * LANES
    vmem = pl.BlockSpec(memory_space=pltpu.VMEM)
    return pl.pallas_call(
        prepare_kernel,
        out_shape=[jax.ShapeDtypeStruct((size, width), BF16) for size in sizes],
        in_specs=[vmem] * 4 + [pl.BlockSpec(memory_space=pltpu.SMEM)],
        compiler_params=PARAMS,
    )(tokens, norm_gain.reshape(-1, LANES), routes.T, route_gates.T, placement)


def to_experts(rows):
    return lax.all_to_all(rows, "node", 0, 0, tiled=True)


def total(own, parts):
    for part in parts:
        own = own + part.astype(F32)
    return own.astype(BF16)


def body(tokens, norm_gain, routes, route_gates, placement, gate_weight, up_weight, down_weight):
    nodes, peers = lax.axis_size("node"), lax.axis_size("local")
    node, local = lax.axis_index("node"), lax.axis_index("local")
    experts = placement.shape[0]
    features = tokens.shape[1]
    capacity = BLOCK_TOK * routes.shape[1] // experts * 3 // 2
    slots = experts * capacity
    half = features // 2
    weights = (gate_weight[0], up_weight[0], down_weight[0])
    sizes = [BLOCK_TOK, 2 * BLOCK_TOK, BLOCK_TOK]
    sent0, sent12, sent3 = prepare(tokens, norm_gain, routes, route_gates, placement, sizes)

    bits_a, bits_b = bit_order(nodes, False), bit_order(nodes, True)
    ids = jnp.stack([node, local]).astype(I32)
    near = ids, peers, capacity, features
    cuts = [slots // peers * k for k in range(peers + 1)]

    near0 = swaps([sent0] * peers, "local", 1, peers)
    pair = jnp.concatenate([sent3, swap(sent3, "node", bits_a[0])])
    rows_a = gather_doubling(pair[:, :half], "node", bits_a[1:-1])
    rows_b = gather_doubling(pair[:, half:], "node", bits_b[1:-1])
    sent12, rows_a, rows_b = fence([sent12, rows_a, rows_b], near0)
    rows_a = [rows_a, swap(rows_a, "node", bits_a[-1])]
    rows_b = [rows_b, swap(rows_b, "node", bits_b[-1])]
    chain = chain_step([sent12, sent12], "local", 1)
    outbound0, mixing0 = pick([sent0] + near0, *near, chain_in=False, chain_out=True)

    outbound0, *last_rows = fence([outbound0, rows_a[1], rows_b[1]], chain)
    arrived0 = to_experts(outbound0)
    parts12 = [sent12] + chain
    for step in range(2, peers):
        chain = chain_step(chain, "local", step)
        parts12 += chain
    outbound3, mixing3a, mixing3b = pick_cross(
        [rows_a[0], last_rows[0]],
        [rows_b[0], last_rows[1]],
        gathered_from(bits_a),
        gathered_from(bits_b),
        *near,
        cuts,
    )
    outbound12, mixing1, mixing2 = pick(parts12, *near, chain_in=True, chain_out=False)

    own3, *outbound3 = outbound3
    outbound12, *outbound3 = fence([outbound12] + outbound3, [arrived0])
    arrived12 = to_experts(outbound12)
    arrived3 = swaps([None] + outbound3, "local", 1, peers)
    (out0,) = expert([arrived0.reshape(slots, features)], ids, *weights)

    out0, tie = fence([out0, ids], [arrived12] + arrived3)
    landed0 = to_experts(out0)
    out3 = list(expert([own3] + arrived3, tie, *weights))
    landed3 = out3[:1] + swaps(out3, "local", 1, peers - 1)
    (out1,) = expert([arrived12], tie, *weights, block=0)

    (mixing0,) = fence([mixing0], [out1])
    out1, last3, tie = fence([out1, out3[-1], tie], [landed0] + landed3[1:])
    landed1 = to_experts(out1)
    landed3.append(swap(last3, "local", peers - 1))
    own0, sends0 = mix(mixing0, landed0)
    parts0 = chain_sum_step(sends0, "local", 1)
    (out2,) = expert([arrived12], tie, *weights, block=1)

    out2, *parts0 = fence([out2] + parts0, [landed1, landed3[-1]])
    landed2 = to_experts(out2)
    for step in range(2, peers):
        parts0 = chain_sum_step(sends0, "local", step, parts0)
    own1, parts1 = mix(mixing1, landed1)
    parts1 = swaps([None] + parts1, "local", 1, peers)
    cross = mix_cross(mixing3a, mixing3b, landed3)

    cross = fence(list(cross), parts0 + parts1)
    sums3 = halve(*cross[:2], "node", bits_a[-1]), halve(*cross[2:], "node", bits_b[-1])
    sums3 = fence(sums3, [landed2])
    (mixing2,) = fence([mixing2], sums3[:1])
    own2, parts2 = mix(mixing2, landed2)
    parts2 = swaps([None] + parts2, "local", 1, peers)
    piece0, piece1 = total(own0, parts0), total(own1, parts1)
    piece3 = [sum_halving(s, "node", bits[:-1]) for s, bits in zip(sums3, (bits_a, bits_b))]
    piece3 = jnp.concatenate(piece3, axis=1)
    piece2 = total(own2, parts2)
    return jnp.concatenate([piece0, piece1, piece2, piece3], axis=0)


def solution(mesh):
    rows = P(AXES, None)
    stacked = P(AXES, None, None)
    in_specs = (rows, P(), rows, rows, P(), stacked, stacked, stacked)
    return jax.shard_map(body, mesh=mesh, in_specs=in_specs, out_specs=rows, check_vma=False)
```

```python
import functools

import jax
import jax.numpy as jnp
import numpy as np
from jax import lax
from jax.experimental import pallas as pl
from jax.experimental.pallas import tpu as pltpu
from jax.sharding import PartitionSpec as P

BLOCK_TOK = 32
EPSILON = 1e-06
AXES = ("node", "local")
LANES = 128
TILES = 4
BF16, F32, I32 = jnp.bfloat16, jnp.float32, jnp.int32
ANYWHERE = pl.BlockSpec(memory_space=pl.ANY)
PARAMS = pltpu.CompilerParams(vmem_limit_bytes=60 * 2**20)


def fence(arrays, after):
    token = sum(a.reshape(-1, a.shape[-1])[:16, :LANES].astype(F32) for a in after)

    def kernel(*refs):
        pass

    return list(pl.pallas_call(
        kernel,
        out_shape=[jax.ShapeDtypeStruct(a.shape, a.dtype) for a in arrays],
        in_specs=[ANYWHERE] * (len(arrays) + 1),
        out_specs=[ANYWHERE] * len(arrays),
        input_output_aliases={i: i for i in range(len(arrays))},
    )(*arrays, token))


def swap(array, axis, bits):
    size = lax.axis_size(axis)
    return lax.ppermute(array, axis, [(i, i ^ bits) for i in range(size)])


def swaps(parts, axis, first, last):
    return [swap(parts[k], axis, k) for k in range(first, last)]


def bit_order(size, last_first):
    bits = [1 << i for i in range(size.bit_length() - 1)]
    return bits[:1] + bits[:0:-1] if last_first else bits


def chain_step(arrays, axis, step):
    size = lax.axis_size(axis)
    rightward = [(i, i + 1) for i in range(step - 1, size - 1)]
    leftward = [(size - 1 - i, size - 2 - i) for i in range(step - 1, size - 1)]
    return [lax.ppermute(a, axis, way) for a, way in zip(arrays, (rightward, leftward))]


def chain_offsets(size):
    return [0] + [offset for d in range(1, size) for offset in (-d, d)]


def gather_doubling(array, axis, bits):
    for bit in bits:
        array = jnp.concatenate([array, swap(array, axis, bit)])
    return array


def gathered_from(bits):
    found = [0]
    for bit in bits:
        found += [k ^ bit for k in found]
    return found


def halve(keep, give, axis, bit):
    return keep + swap(give.astype(BF16), axis, bit).astype(F32)


def sum_halving(array, axis, bits):
    for bit in bits[::-1]:
        array = halve(*jnp.split(array, 2), axis, bit)
    return array.astype(BF16)


def below(rows):
    at = np.arange(rows)
    same = at[:, None] // BLOCK_TOK == at[None, :] // BLOCK_TOK
    return (same & (at[None, :] < at[:, None])).astype(BF16)


def choose(table, lane, row_group, slot_group, turn, before):
    select = lax.broadcasted_iota(I32, (table.shape[1], lane.shape[1]), 0) == lane
    weight = jnp.dot(table, select.astype(BF16), preferred_element_type=F32)
    mask = jnp.where((weight > 0) & (row_group == slot_group), 1.0, 0.0)
    rank = jnp.dot(before, mask.astype(BF16), preferred_element_type=F32)
    place = jnp.where(rank == turn, mask, 0.0)
    return place.astype(BF16), (place * weight).astype(BF16)


def gather_rows(place, rows):
    return lax.dot_general(
        place, rows, (((0,), (0,)), ((), ())), preferred_element_type=F32
    ).astype(BF16)


def bits_of(labels, local, peers, chained):
    if not chained:
        return labels
    source = labels + local
    return jnp.where((source >= 0) & (source < peers), source ^ local, -1)


def pick_kernel(count, blocks, peers, chain_in, chain_out, ids, *refs):
    parts, refs = refs[:count], refs[count:]
    tables, refs = refs[:count], refs[count:]
    lane, slot_group, turn, before, in_column, in_row, out_column, out = refs[:8]
    mixings, places = refs[8 : 8 + blocks], refs[8 + blocks :]

    def rows_of(refs, block):
        return jnp.concatenate([r[block * BLOCK_TOK : (block + 1) * BLOCK_TOK] for r in refs])

    @pl.when(pl.program_id(0) == 0)
    def _():
        local = ids[1]
        row_group = bits_of(in_column[...], local, peers, chain_in)
        for block, (mixing, place) in enumerate(zip(mixings, places)):
            place[...], weights = choose(
                rows_of(tables, block),
                lane[...] + local,
                row_group,
                slot_group[...],
                turn[...],
                before[...],
            )
            if chain_in != chain_out:
                shape = mixing.shape[0], weights.shape[0]
                same = bits_of(out_column[...], local, peers, chain_out) == bits_of(
                    in_row[...], local, peers, chain_in
                )
                row = lax.broadcasted_iota(I32, shape, 0) & (BLOCK_TOK - 1)
                column = lax.broadcasted_iota(I32, shape, 1) & (BLOCK_TOK - 1)
                order = jnp.where(same & (row == column), 1.0, 0.0).astype(BF16)
                weights = jnp.dot(order, weights, preferred_element_type=F32).astype(BF16)
            mixing[...] = weights

    for block, place in enumerate(places):
        rows = lax.dot_general(
            place[...],
            rows_of(parts, block),
            (((0,), (0,)), ((), ())),
            preferred_element_type=F32,
        )
        nodes, _, size, tile = out.shape
        out[:, block] = rows.reshape(nodes, size, tile).astype(BF16)


def whole_block(array):
    return pl.BlockSpec(array.shape, lambda j: (0,) * array.ndim)


def by_token(labels):
    return np.repeat(np.array(labels, np.int32), BLOCK_TOK)


def pick(parts, ids, peers, capacity, features, chain_in, chain_out):
    nodes = lax.axis_size("node")
    held = parts[0].shape[0]
    blocks = held // BLOCK_TOK
    slots = nodes * peers * capacity
    slot = np.arange(slots, dtype=np.int32)[None, :]
    labels = chain_offsets(peers), list(range(peers))
    in_labels, out_labels = by_token(labels[not chain_in]), by_token(labels[not chain_out])
    rows, tile = len(in_labels), features // TILES
    small = (
        slot // (capacity * peers) * peers,
        slot // capacity % peers,
        (slot % capacity).astype(np.float32),
        below(rows),
        in_labels[:, None],
        in_labels[None, :],
        out_labels[:, None],
    )
    return pl.pallas_call(
        functools.partial(pick_kernel, len(parts), blocks, peers, chain_in, chain_out),
        grid=(TILES,),
        out_shape=[
            jax.ShapeDtypeStruct((nodes, blocks, peers * capacity, features), BF16),
        ]
        + [jax.ShapeDtypeStruct((len(out_labels), slots), BF16)] * blocks,
        in_specs=[pl.BlockSpec(memory_space=pltpu.SMEM)]
        + [pl.BlockSpec((held, tile), lambda j: (0, j))] * len(parts)
        + [pl.BlockSpec((held, LANES), lambda j: (0, features // LANES))] * len(parts)
        + [whole_block(a) for a in small],
        out_specs=[
            pl.BlockSpec((nodes, blocks, peers * capacity, tile), lambda j: (0, 0, 0, j)),
        ]
        + [pl.BlockSpec((len(out_labels), slots), lambda j: (0, 0))] * blocks,
        scratch_shapes=[pltpu.VMEM((rows, slots), BF16)] * blocks,
        compiler_params=PARAMS,
        cost_estimate=pl.CostEstimate(
            flops=2 * blocks * rows * slots * features,
            bytes_accessed=2 * blocks * (rows + slots) * features,
            transcendentals=0,
        ),
    )(ids, *parts, *parts, *small)


def pick_cross_kernel(order, cuts, peers, ids, a0, a1, b0, b1, t0, t1, *refs):
    peer, group_a, group_b, slot_group, turn, before = refs[:6]
    outs, (mixing_a, mixing_b, place_a, place_b) = refs[6:-4], refs[-4:]
    step = pl.program_id(0)

    @pl.when(step == 0)
    def _():
        known = jnp.concatenate([t0[...], t1[...]])
        lane = (peer[...] ^ ids[1]) + ids[0] * peers
        common = slot_group[...], turn[...], before[...]
        place_b[...], mixing_b[...] = choose(known, lane, group_b[...], *common)
        back = [order.index(k) * BLOCK_TOK for k in range(len(order))]
        known = jnp.concatenate([known[at : at + BLOCK_TOK] for at in back])
        place_a[...], mixing_a[...] = choose(known, lane, group_a[...], *common)

    def store(place, first_rows, last_rows):
        result = gather_rows(place[...], jnp.concatenate([first_rows[...], last_rows[...]]))
        for out, first, last in zip(outs, cuts[:-1], cuts[1:]):
            out[...] = result[first:last]

    @pl.when(step < TILES // 2)
    def _():
        store(place_a, a0, a1)

    @pl.when(step >= TILES // 2)
    def _():
        store(place_b, b0, b1)


def in_first_half(shape):
    return pl.BlockSpec(shape, lambda j: (0, jnp.minimum(j, TILES // 2 - 1)))


def in_second_half(shape):
    return pl.BlockSpec(shape, lambda j: (0, jnp.maximum(j - TILES // 2, 0)))


def pick_cross(rows_a, rows_b, order_a, order_b, ids, peers, capacity, features, cuts):
    part = rows_a[0].shape[0]
    rows = 2 * part
    nodes = rows // BLOCK_TOK
    slots = cuts[-1]
    slot = np.arange(slots, dtype=np.int32)[None, :]
    tile = features // TILES
    small = (
        slot // (capacity * nodes),
        by_token(order_a)[:, None],
        by_token(order_b)[:, None],
        slot // capacity % nodes,
        (slot % capacity).astype(np.float32),
        below(rows),
    )
    sizes = [last - first for first, last in zip(cuts[:-1], cuts[1:])]
    results = pl.pallas_call(
        functools.partial(pick_cross_kernel, order_b, cuts, peers),
        grid=(TILES,),
        out_shape=[jax.ShapeDtypeStruct((size, features), BF16) for size in sizes]
        + [jax.ShapeDtypeStruct((rows, slots), BF16)] * 2,
        in_specs=[pl.BlockSpec(memory_space=pltpu.SMEM)]
        + [in_first_half((part, tile))] * 2
        + [in_second_half((part, tile))] * 2
        + [pl.BlockSpec((part, LANES), lambda j: (0, features // 2 // LANES))] * 2
        + [whole_block(a) for a in small],
        out_specs=[pl.BlockSpec((size, tile), lambda j: (0, j)) for size in sizes]
        + [pl.BlockSpec((rows, slots), lambda j: (0, 0))] * 2,
        scratch_shapes=[pltpu.VMEM((rows, slots), BF16)] * 2,
        compiler_params=PARAMS,
        cost_estimate=pl.CostEstimate(
            flops=2 * rows * slots * features,
            bytes_accessed=2 * (rows + slots) * features,
            transcendentals=0,
        ),
    )(ids, *rows_a, *rows_b, *rows_b, *small)
    return list(results[:-2]), results[-2], results[-1]


def mix_kernel(mixing, landed, own, *outs):
    result = jnp.dot(mixing[...], landed[...], preferred_element_type=F32)
    own[...] = result[:BLOCK_TOK]
    for k, out in enumerate(outs):
        out[...] = result[(k + 1) * BLOCK_TOK : (k + 2) * BLOCK_TOK].astype(BF16)


def mix(mixing, landed):
    rows, slots = mixing.shape
    features = landed.shape[1]
    tile = features // TILES
    count = rows // BLOCK_TOK
    own, *parts = pl.pallas_call(
        mix_kernel,
        grid=(TILES,),
        out_shape=[jax.ShapeDtypeStruct((BLOCK_TOK, features), F32)]
        + [jax.ShapeDtypeStruct((BLOCK_TOK, features), BF16)] * (count - 1),
        in_specs=[whole_block(mixing), pl.BlockSpec((slots, tile), lambda j: (0, j))],
        out_specs=[pl.BlockSpec((BLOCK_TOK, tile), lambda j: (0, j))] * count,
        compiler_params=PARAMS,
        cost_estimate=pl.CostEstimate(
            flops=2 * rows * slots * features,
            bytes_accessed=2 * (rows + slots) * features,
            transcendentals=0,
        ),
    )(mixing, landed)
    return own, parts


def mix_cross_kernel(mixing_a, mixing_b, *refs):
    landed, (keep_a, give_a, keep_b, give_b) = refs[:-4], refs[-4:]
    step = pl.program_id(0)
    half = keep_a.shape[0]
    rows = jnp.concatenate([part[...] for part in landed])

    def store(mixing, keep, give):
        result = jnp.dot(mixing[...], rows, preferred_element_type=F32)
        keep[...] = result[:half]
        give[...] = result[half:].astype(BF16)

    @pl.when(step < TILES // 2)
    def _():
        store(mixing_a, keep_a, give_a)

    @pl.when(step >= TILES // 2)
    def _():
        store(mixing_b, keep_b, give_b)


def mix_cross(mixing_a, mixing_b, landed):
    rows, slots = mixing_a.shape
    features = landed[0].shape[1]
    tile = features // TILES
    shape = (rows // 2, features // 2)
    return pl.pallas_call(
        mix_cross_kernel,
        grid=(TILES,),
        out_shape=[jax.ShapeDtypeStruct(shape, F32), jax.ShapeDtypeStruct(shape, BF16)] * 2,
        in_specs=[whole_block(mixing_a), whole_block(mixing_b)]
        + [pl.BlockSpec((part.shape[0], tile), lambda j: (0, j)) for part in landed],
        out_specs=[in_first_half((rows // 2, tile))] * 2 + [in_second_half((rows // 2, tile))] * 2,
        compiler_params=PARAMS,
        cost_estimate=pl.CostEstimate(
            flops=2 * rows * slots * features,
            bytes_accessed=2 * (rows + slots) * features,
            transcendentals=0,
        ),
    )(mixing_a, mixing_b, *landed)


def expert_kernel(count, first_tiles, nodes, tie, *refs):
    parts, (gate_ref, up_ref, down_ref) = refs[:count], refs[count : count + 3]
    outs, (joined, hidden) = refs[count + 3 : -2], refs[-2:]
    step = pl.program_id(0)
    x_ref = parts[0] if count == 1 and not nodes else joined

    if x_ref is joined:

        @pl.when(step == 0)
        def _():
            pieces = [parts[0][n, 0] for n in range(nodes)] or [part[...] for part in parts]
            joined[...] = jnp.concatenate(pieces)

    @pl.when(step < first_tiles)
    def _():
        x = x_ref[...]
        gate_pre = jnp.dot(x, gate_ref[...], preferred_element_type=F32)
        up_pre = jnp.dot(x, up_ref[...], preferred_element_type=F32)
        hidden[step] = (gate_pre / (1 + jnp.exp(-gate_pre)) * up_pre).astype(BF16)

    @pl.when(step >= first_tiles)
    def _():
        rows = jnp.concatenate([hidden[i] for i in range(first_tiles)], axis=1)
        result = jnp.dot(rows, down_ref[...], preferred_element_type=F32)
        result = result.astype(BF16)
        at = 0
        for out in outs:
            out[...] = result[at : at + out.shape[0]]
            at += out.shape[0]


def expert(parts, tie, gate_weight, up_weight, down_weight, block=None, sizes=None):
    sizes = sizes or [part.shape[0] for part in parts]
    specs = [whole_block(part) for part in parts]
    nodes = 0
    if block is not None:
        nodes, _, size, features = parts[0].shape
        sizes = [nodes * size]
        specs = [pl.BlockSpec((nodes, 1, size, features), lambda i: (0, block, 0, 0))]
    rows = sum(sizes)
    features, hidden = gate_weight.shape
    tile = 256
    first_tiles = hidden // tile
    out_tile = features // TILES

    def first(i):
        return jnp.minimum(i, first_tiles - 1)

    def second(i):
        return jnp.maximum(i - first_tiles, 0)

    return pl.pallas_call(
        functools.partial(expert_kernel, len(parts), first_tiles, nodes),
        grid=(first_tiles + TILES,),
        out_shape=[jax.ShapeDtypeStruct((size, features), BF16) for size in sizes],
        in_specs=[pl.BlockSpec(memory_space=pltpu.SMEM)]
        + specs
        + [
            pl.BlockSpec((features, tile), lambda i: (0, first(i))),
            pl.BlockSpec((features, tile), lambda i: (0, first(i))),
            pl.BlockSpec((hidden, out_tile), lambda i: (0, second(i))),
        ],
        out_specs=[
            pl.BlockSpec((size, out_tile), lambda i: (0, second(i))) for size in sizes
        ],
        scratch_shapes=[
            pltpu.VMEM((rows if nodes or len(parts) > 1 else 16, features), BF16),
            pltpu.VMEM((first_tiles, rows, tile), BF16),
        ],
        compiler_params=PARAMS,
        cost_estimate=pl.CostEstimate(
            flops=6 * rows * features * hidden,
            bytes_accessed=6 * features * hidden + 4 * rows * features,
            transcendentals=rows * hidden,
        ),
    )(tie, *parts, gate_weight, up_weight, down_weight)


def prepare_kernel(tokens, gain, routes, gates, placement, *outs):
    experts = placement.shape[0]
    features = tokens.shape[1]
    chosen = gates[...] / jnp.sum(gates[...], axis=0, keepdims=True)
    columns = jnp.concatenate([routes[...].astype(F32), chosen]).T
    count = routes.shape[0]
    lanes = outs[0].shape[1] - features
    lane = lax.broadcasted_iota(I32, (1, lanes), 1)
    named = jnp.full((1, lanes), -1.0, F32)
    for e in range(experts):
        named = jnp.where(lane == e, placement[e].astype(F32), named)
    start = 0
    for out in outs:
        rows = out.shape[0]
        at = slice(start, start + rows)
        start += rows
        values = tokens[at].astype(F32)
        rescale = lax.rsqrt(jnp.mean(values * values, axis=-1, keepdims=True) + EPSILON)
        for c in range(features // LANES):
            to = slice(c * LANES, (c + 1) * LANES)
            out[:, to] = (values[:, to] * rescale * gain[c : c + 1].astype(F32)).astype(BF16)
        table = jnp.zeros((rows, lanes), F32)
        for k in range(count):
            held = columns[at, k : k + 1] == named
            table = jnp.where(held, columns[at, count + k : count + k + 1], table)
        out[:, features:] = table.astype(BF16)


def prepare(tokens, norm_gain, routes, route_gates, placement, sizes):
    features = tokens.shape[1]
    width = features + -(-placement.shape[0] // LANES) * LANES
    vmem = pl.BlockSpec(memory_space=pltpu.VMEM)
    return pl.pallas_call(
        prepare_kernel,
        out_shape=[jax.ShapeDtypeStruct((size, width), BF16) for size in sizes],
        in_specs=[vmem] * 4 + [pl.BlockSpec(memory_space=pltpu.SMEM)],
        compiler_params=PARAMS,
    )(tokens, norm_gain.reshape(-1, LANES), routes.T, route_gates.T, placement)


def to_experts(rows):
    return lax.all_to_all(rows, "node", 0, 0, tiled=True)


def total(own, parts):
    for part in parts:
        own = own + part.astype(F32)
    return own.astype(BF16)


def body(tokens, norm_gain, routes, route_gates, placement, gate_weight, up_weight, down_weight):
    nodes, peers = lax.axis_size("node"), lax.axis_size("local")
    node, local = lax.axis_index("node"), lax.axis_index("local")
    experts = placement.shape[0]
    features = tokens.shape[1]
    capacity = BLOCK_TOK * routes.shape[1] // experts * 3 // 2
    slots = experts * capacity
    half = features // 2
    weights = (gate_weight[0], up_weight[0], down_weight[0])
    sizes = [BLOCK_TOK, 2 * BLOCK_TOK, BLOCK_TOK]
    sent0, sent12, sent3 = prepare(tokens, norm_gain, routes, route_gates, placement, sizes)

    bits_a, bits_b = bit_order(nodes, False), bit_order(nodes, True)
    ids = jnp.stack([node, local]).astype(I32)
    near = ids, peers, capacity, features
    cuts = [slots // peers * k for k in range(peers + 1)]

    near0 = swaps([sent0] * peers, "local", 1, peers)
    pair = jnp.concatenate([sent3, swap(sent3, "node", bits_a[0])])
    rows_a = gather_doubling(pair[:, :half], "node", bits_a[1:-1])
    rows_b = gather_doubling(pair[:, half:], "node", bits_b[1:-1])
    sent12, rows_a, rows_b = fence([sent12, rows_a, rows_b], near0)
    rows_a = [rows_a, swap(rows_a, "node", bits_a[-1])]
    rows_b = [rows_b, swap(rows_b, "node", bits_b[-1])]
    chain = chain_step([sent12, sent12], "local", 1)
    outbound0, mixing0 = pick([sent0] + near0, *near, chain_in=False, chain_out=False)

    outbound0, *last_rows = fence([outbound0, rows_a[1], rows_b[1]], chain)
    arrived0 = to_experts(outbound0)
    parts12 = [sent12] + chain
    for step in range(2, peers):
        chain = chain_step(chain, "local", step)
        parts12 += chain
    outbound3, mixing3a, mixing3b = pick_cross(
        [rows_a[0], last_rows[0]],
        [rows_b[0], last_rows[1]],
        gathered_from(bits_a),
        gathered_from(bits_b),
        *near,
        cuts,
    )
    outbound12, mixing1, mixing2 = pick(parts12, *near, chain_in=True, chain_out=False)

    own3, *outbound3 = outbound3
    outbound12, *outbound3 = fence([outbound12] + outbound3, [arrived0])
    arrived12 = to_experts(outbound12)
    arrived3 = swaps([None] + outbound3, "local", 1, peers)
    (out0,) = expert([arrived0.reshape(slots, features)], ids, *weights)

    out0, tie = fence([out0, ids], [arrived12] + arrived3)
    landed0 = to_experts(out0)
    size = slots // peers
    sizes = [size] * (peers - 2) + [size * 2 // 3, size // 3] * 2
    last2, last1 = peers - 2, peers - 1
    out3 = list(expert([own3] + arrived3, tie, *weights, sizes=sizes))
    landed3 = out3[:1] + swaps(out3, "local", 1, last1)
    (tie,) = fence([tie], out3[:1])
    (out1,) = expert([arrived12], tie, *weights, block=0)

    (mixing0,) = fence([mixing0], [out1] + landed3[1:])
    out1, part2, part3, tie = fence([out1] + out3[-3:-1] + [tie], [landed0] + landed3[1:])
    landed1 = to_experts(out1)
    landed3 += [swap(part2, "local", last2), swap(part3, "local", last1)]
    own0, parts0 = mix(mixing0, landed0)
    parts0 = swaps([None] + parts0, "local", 1, peers)
    (out2,) = expert([arrived12], tie, *weights, block=1)

    out2, part3 = fence([out2, out3[-1]], [landed1] + landed3[-2:])
    landed2 = to_experts(out2)
    landed3.append(swap(part3, "local", last1))
    own1, parts1 = mix(mixing1, landed1)
    parts1 = swaps([None] + parts1, "local", 1, peers)
    cross = mix_cross(mixing3a, mixing3b, landed3)

    own2, parts2 = mix(mixing2, landed2)
    cross = fence(list(cross), parts2[:1])
    parts2 = swaps([None] + parts2, "local", 1, peers)
    sums3 = halve(*cross[:2], "node", bits_a[-1]), halve(*cross[2:], "node", bits_b[-1])
    piece0, piece1 = total(own0, parts0), total(own1, parts1)
    piece3 = [sum_halving(s, "node", bits[:-1]) for s, bits in zip(sums3, (bits_a, bits_b))]
    piece3 = jnp.concatenate(piece3, axis=1)
    piece2 = total(own2, parts2)
    return jnp.concatenate([piece0, piece1, piece2, piece3], axis=0)


def solution(mesh):
    rows = P(AXES, None)
    stacked = P(AXES, None, None)
    in_specs = (rows, P(), rows, rows, P(), stacked, stacked, stacked)
    return jax.shard_map(body, mesh=mesh, in_specs=in_specs, out_specs=rows, check_vma=False)
```

```python
import functools

import jax
import jax.numpy as jnp
import numpy as np
from jax import lax
from jax.experimental import pallas as pl
from jax.experimental.pallas import tpu as pltpu
from jax.sharding import PartitionSpec as P

BLOCK_TOK = 32
EPSILON = 1e-06
AXES = ("node", "local")
LANES = 128
TILES = 4
BF16, F32, I32 = jnp.bfloat16, jnp.float32, jnp.int32
ANYWHERE = pl.BlockSpec(memory_space=pl.ANY)
PARAMS = pltpu.CompilerParams(vmem_limit_bytes=60 * 2**20)


def fence(arrays, after):
    token = sum(a.reshape(-1, a.shape[-1])[:16, :LANES].astype(F32) for a in after)

    def kernel(*refs):
        pass

    return list(pl.pallas_call(
        kernel,
        out_shape=[jax.ShapeDtypeStruct(a.shape, a.dtype) for a in arrays],
        in_specs=[ANYWHERE] * (len(arrays) + 1),
        out_specs=[ANYWHERE] * len(arrays),
        input_output_aliases={i: i for i in range(len(arrays))},
    )(*arrays, token))


def swap(array, axis, bits):
    size = lax.axis_size(axis)
    return lax.ppermute(array, axis, [(i, i ^ bits) for i in range(size)])


def swaps(parts, axis, first, last):
    return [swap(parts[k], axis, k) for k in range(first, last)]


def bit_order(size, last_first):
    bits = [1 << i for i in range(size.bit_length() - 1)]
    return bits[:1] + bits[:0:-1] if last_first else bits


def chain_step(arrays, axis, step):
    size = lax.axis_size(axis)
    rightward = [(i, i + 1) for i in range(step - 1, size - 1)]
    leftward = [(size - 1 - i, size - 2 - i) for i in range(step - 1, size - 1)]
    return [lax.ppermute(a, axis, way) for a, way in zip(arrays, (rightward, leftward))]


def chain_offsets(size):
    return [0] + [offset for d in range(1, size) for offset in (-d, d)]


def gather_doubling(array, axis, bits):
    for bit in bits:
        array = jnp.concatenate([array, swap(array, axis, bit)])
    return array


def gathered_from(bits):
    found = [0]
    for bit in bits:
        found += [k ^ bit for k in found]
    return found


def halve(keep, give, axis, bit):
    return keep + swap(give.astype(BF16), axis, bit).astype(F32)


def sum_halving(array, axis, bits):
    for bit in bits[::-1]:
        array = halve(*jnp.split(array, 2), axis, bit)
    return array.astype(BF16)


def below(rows):
    at = np.arange(rows)
    same = at[:, None] // BLOCK_TOK == at[None, :] // BLOCK_TOK
    return (same & (at[None, :] < at[:, None])).astype(BF16)


def choose(table, lane, row_group, slot_group, turn, before):
    select = lax.broadcasted_iota(I32, (table.shape[1], lane.shape[1]), 0) == lane
    weight = jnp.dot(table, select.astype(BF16), preferred_element_type=F32)
    mask = jnp.where((weight > 0) & (row_group == slot_group), 1.0, 0.0)
    rank = jnp.dot(before, mask.astype(BF16), preferred_element_type=F32)
    place = jnp.where(rank == turn, mask, 0.0)
    return place.astype(BF16), (place * weight).astype(BF16)


def gather_rows(place, rows):
    return lax.dot_general(
        place, rows, (((0,), (0,)), ((), ())), preferred_element_type=F32
    ).astype(BF16)


def bits_of(labels, local, peers, chained):
    if not chained:
        return labels
    source = labels + local
    return jnp.where((source >= 0) & (source < peers), source ^ local, -1)


def pick_kernel(count, blocks, peers, chain_in, chain_out, ids, *refs):
    parts, refs = refs[:count], refs[count:]
    tables, refs = refs[:count], refs[count:]
    lane, slot_group, turn, before, in_column, in_row, out_column, out = refs[:8]
    mixings, places = refs[8 : 8 + blocks], refs[8 + blocks :]

    def rows_of(refs, block):
        return jnp.concatenate([r[block * BLOCK_TOK : (block + 1) * BLOCK_TOK] for r in refs])

    @pl.when(pl.program_id(0) == 0)
    def _():
        local = ids[1]
        row_group = bits_of(in_column[...], local, peers, chain_in)
        for block, (mixing, place) in enumerate(zip(mixings, places)):
            place[...], weights = choose(
                rows_of(tables, block),
                lane[...] + local,
                row_group,
                slot_group[...],
                turn[...],
                before[...],
            )
            if chain_in != chain_out:
                shape = mixing.shape[0], weights.shape[0]
                same = bits_of(out_column[...], local, peers, chain_out) == bits_of(
                    in_row[...], local, peers, chain_in
                )
                row = lax.broadcasted_iota(I32, shape, 0) & (BLOCK_TOK - 1)
                column = lax.broadcasted_iota(I32, shape, 1) & (BLOCK_TOK - 1)
                order = jnp.where(same & (row == column), 1.0, 0.0).astype(BF16)
                weights = jnp.dot(order, weights, preferred_element_type=F32).astype(BF16)
            mixing[...] = weights

    for block, place in enumerate(places):
        rows = lax.dot_general(
            place[...],
            rows_of(parts, block),
            (((0,), (0,)), ((), ())),
            preferred_element_type=F32,
        )
        nodes, _, size, tile = out.shape
        out[:, block] = rows.reshape(nodes, size, tile).astype(BF16)


def whole_block(array):
    return pl.BlockSpec(array.shape, lambda j: (0,) * array.ndim)


def by_token(labels):
    return np.repeat(np.array(labels, np.int32), BLOCK_TOK)


def pick(parts, ids, peers, capacity, features, chain_in, chain_out):
    nodes = lax.axis_size("node")
    held = parts[0].shape[0]
    blocks = held // BLOCK_TOK
    slots = nodes * peers * capacity
    slot = np.arange(slots, dtype=np.int32)[None, :]
    labels = chain_offsets(peers), list(range(peers))
    in_labels, out_labels = by_token(labels[not chain_in]), by_token(labels[not chain_out])
    rows, tile = len(in_labels), features // TILES
    small = (
        slot // (capacity * peers) * peers,
        slot // capacity % peers,
        (slot % capacity).astype(np.float32),
        below(rows),
        in_labels[:, None],
        in_labels[None, :],
        out_labels[:, None],
    )
    return pl.pallas_call(
        functools.partial(pick_kernel, len(parts), blocks, peers, chain_in, chain_out),
        grid=(TILES,),
        out_shape=[
            jax.ShapeDtypeStruct((nodes, blocks, peers * capacity, features), BF16),
        ]
        + [jax.ShapeDtypeStruct((len(out_labels), slots), BF16)] * blocks,
        in_specs=[pl.BlockSpec(memory_space=pltpu.SMEM)]
        + [pl.BlockSpec((held, tile), lambda j: (0, j))] * len(parts)
        + [pl.BlockSpec((held, LANES), lambda j: (0, features // LANES))] * len(parts)
        + [whole_block(a) for a in small],
        out_specs=[
            pl.BlockSpec((nodes, blocks, peers * capacity, tile), lambda j: (0, 0, 0, j)),
        ]
        + [pl.BlockSpec((len(out_labels), slots), lambda j: (0, 0))] * blocks,
        scratch_shapes=[pltpu.VMEM((rows, slots), BF16)] * blocks,
        compiler_params=PARAMS,
        cost_estimate=pl.CostEstimate(
            flops=2 * blocks * rows * slots * features,
            bytes_accessed=2 * blocks * (rows + slots) * features,
            transcendentals=0,
        ),
    )(ids, *parts, *parts, *small)


def pick_cross_kernel(order, cuts, peers, ids, a0, a1, b0, b1, t0, t1, *refs):
    peer, group_a, group_b, slot_group, turn, before = refs[:6]
    outs, (mixing_a, mixing_b, place_a, place_b) = refs[6:-4], refs[-4:]
    step = pl.program_id(0)

    @pl.when(step == 0)
    def _():
        known = jnp.concatenate([t0[...], t1[...]])
        lane = (peer[...] ^ ids[1]) + ids[0] * peers
        common = slot_group[...], turn[...], before[...]
        place_b[...], mixing_b[...] = choose(known, lane, group_b[...], *common)
        back = [order.index(k) * BLOCK_TOK for k in range(len(order))]
        known = jnp.concatenate([known[at : at + BLOCK_TOK] for at in back])
        place_a[...], mixing_a[...] = choose(known, lane, group_a[...], *common)

    def store(place, first_rows, last_rows):
        result = gather_rows(place[...], jnp.concatenate([first_rows[...], last_rows[...]]))
        for out, first, last in zip(outs, cuts[:-1], cuts[1:]):
            out[...] = result[first:last]

    @pl.when(step < TILES // 2)
    def _():
        store(place_a, a0, a1)

    @pl.when(step >= TILES // 2)
    def _():
        store(place_b, b0, b1)


def in_first_half(shape):
    return pl.BlockSpec(shape, lambda j: (0, jnp.minimum(j, TILES // 2 - 1)))


def in_second_half(shape):
    return pl.BlockSpec(shape, lambda j: (0, jnp.maximum(j - TILES // 2, 0)))


def pick_cross(rows_a, rows_b, order_a, order_b, ids, peers, capacity, features, cuts):
    part = rows_a[0].shape[0]
    rows = 2 * part
    nodes = rows // BLOCK_TOK
    slots = cuts[-1]
    slot = np.arange(slots, dtype=np.int32)[None, :]
    tile = features // TILES
    small = (
        slot // (capacity * nodes),
        by_token(order_a)[:, None],
        by_token(order_b)[:, None],
        slot // capacity % nodes,
        (slot % capacity).astype(np.float32),
        below(rows),
    )
    sizes = [last - first for first, last in zip(cuts[:-1], cuts[1:])]
    results = pl.pallas_call(
        functools.partial(pick_cross_kernel, order_b, cuts, peers),
        grid=(TILES,),
        out_shape=[jax.ShapeDtypeStruct((size, features), BF16) for size in sizes]
        + [jax.ShapeDtypeStruct((rows, slots), BF16)] * 2,
        in_specs=[pl.BlockSpec(memory_space=pltpu.SMEM)]
        + [in_first_half((part, tile))] * 2
        + [in_second_half((part, tile))] * 2
        + [pl.BlockSpec((part, LANES), lambda j: (0, features // 2 // LANES))] * 2
        + [whole_block(a) for a in small],
        out_specs=[pl.BlockSpec((size, tile), lambda j: (0, j)) for size in sizes]
        + [pl.BlockSpec((rows, slots), lambda j: (0, 0))] * 2,
        scratch_shapes=[pltpu.VMEM((rows, slots), BF16)] * 2,
        compiler_params=PARAMS,
        cost_estimate=pl.CostEstimate(
            flops=2 * rows * slots * features,
            bytes_accessed=2 * (rows + slots) * features,
            transcendentals=0,
        ),
    )(ids, *rows_a, *rows_b, *rows_b, *small)
    return list(results[:-2]), results[-2], results[-1]


def mix_kernel(mixing, landed, own, *outs):
    result = jnp.dot(mixing[...], landed[...], preferred_element_type=F32)
    own[...] = result[:BLOCK_TOK]
    for k, out in enumerate(outs):
        out[...] = result[(k + 1) * BLOCK_TOK : (k + 2) * BLOCK_TOK].astype(BF16)


def mix(mixing, landed):
    rows, slots = mixing.shape
    features = landed.shape[1]
    tile = features // TILES
    count = rows // BLOCK_TOK
    own, *parts = pl.pallas_call(
        mix_kernel,
        grid=(TILES,),
        out_shape=[jax.ShapeDtypeStruct((BLOCK_TOK, features), F32)]
        + [jax.ShapeDtypeStruct((BLOCK_TOK, features), BF16)] * (count - 1),
        in_specs=[whole_block(mixing), pl.BlockSpec((slots, tile), lambda j: (0, j))],
        out_specs=[pl.BlockSpec((BLOCK_TOK, tile), lambda j: (0, j))] * count,
        compiler_params=PARAMS,
        cost_estimate=pl.CostEstimate(
            flops=2 * rows * slots * features,
            bytes_accessed=2 * (rows + slots) * features,
            transcendentals=0,
        ),
    )(mixing, landed)
    return own, parts


def mix_cross_kernel(mixing_a, mixing_b, *refs):
    landed, (keep_a, give_a, keep_b, give_b) = refs[:-4], refs[-4:]
    step = pl.program_id(0)
    half = keep_a.shape[0]
    rows = jnp.concatenate([part[...] for part in landed])

    def store(mixing, keep, give):
        result = jnp.dot(mixing[...], rows, preferred_element_type=F32)
        keep[...] = result[:half]
        give[...] = result[half:].astype(BF16)

    @pl.when(step < TILES // 2)
    def _():
        store(mixing_a, keep_a, give_a)

    @pl.when(step >= TILES // 2)
    def _():
        store(mixing_b, keep_b, give_b)


def mix_cross(mixing_a, mixing_b, landed):
    rows, slots = mixing_a.shape
    features = landed[0].shape[1]
    tile = features // TILES
    shape = (rows // 2, features // 2)
    return pl.pallas_call(
        mix_cross_kernel,
        grid=(TILES,),
        out_shape=[jax.ShapeDtypeStruct(shape, F32), jax.ShapeDtypeStruct(shape, BF16)] * 2,
        in_specs=[whole_block(mixing_a), whole_block(mixing_b)]
        + [pl.BlockSpec((part.shape[0], tile), lambda j: (0, j)) for part in landed],
        out_specs=[in_first_half((rows // 2, tile))] * 2 + [in_second_half((rows // 2, tile))] * 2,
        compiler_params=PARAMS,
        cost_estimate=pl.CostEstimate(
            flops=2 * rows * slots * features,
            bytes_accessed=2 * (rows + slots) * features,
            transcendentals=0,
        ),
    )(mixing_a, mixing_b, *landed)


def expert_kernel(count, first_tiles, nodes, tie, *refs):
    parts, (gate_ref, up_ref, down_ref) = refs[:count], refs[count : count + 3]
    outs, (joined, hidden) = refs[count + 3 : -2], refs[-2:]
    step = pl.program_id(0)
    x_ref = parts[0] if count == 1 and not nodes else joined

    if x_ref is joined:

        @pl.when(step == 0)
        def _():
            pieces = [parts[0][n, 0] for n in range(nodes)] or [part[...] for part in parts]
            joined[...] = jnp.concatenate(pieces)

    @pl.when(step < first_tiles)
    def _():
        x = x_ref[...]
        gate_pre = jnp.dot(x, gate_ref[...], preferred_element_type=F32)
        up_pre = jnp.dot(x, up_ref[...], preferred_element_type=F32)
        hidden[step] = (gate_pre / (1 + jnp.exp(-gate_pre)) * up_pre).astype(BF16)

    @pl.when(step >= first_tiles)
    def _():
        rows = jnp.concatenate([hidden[i] for i in range(first_tiles)], axis=1)
        result = jnp.dot(rows, down_ref[...], preferred_element_type=F32)
        result = result.astype(BF16)
        at = 0
        for out in outs:
            out[...] = result[at : at + out.shape[0]]
            at += out.shape[0]


def expert(parts, tie, gate_weight, up_weight, down_weight, block=None, sizes=None):
    sizes = sizes or [part.shape[0] for part in parts]
    specs = [whole_block(part) for part in parts]
    nodes = 0
    if block is not None:
        nodes, _, size, features = parts[0].shape
        sizes = [nodes * size]
        specs = [pl.BlockSpec((nodes, 1, size, features), lambda i: (0, block, 0, 0))]
    rows = sum(sizes)
    features, hidden = gate_weight.shape
    tile = 256
    first_tiles = hidden // tile
    out_tile = features // TILES

    def first(i):
        return jnp.minimum(i, first_tiles - 1)

    def second(i):
        return jnp.maximum(i - first_tiles, 0)

    return pl.pallas_call(
        functools.partial(expert_kernel, len(parts), first_tiles, nodes),
        grid=(first_tiles + TILES,),
        out_shape=[jax.ShapeDtypeStruct((size, features), BF16) for size in sizes],
        in_specs=[pl.BlockSpec(memory_space=pltpu.SMEM)]
        + specs
        + [
            pl.BlockSpec((features, tile), lambda i: (0, first(i))),
            pl.BlockSpec((features, tile), lambda i: (0, first(i))),
            pl.BlockSpec((hidden, out_tile), lambda i: (0, second(i))),
        ],
        out_specs=[
            pl.BlockSpec((size, out_tile), lambda i: (0, second(i))) for size in sizes
        ],
        scratch_shapes=[
            pltpu.VMEM((rows if nodes or len(parts) > 1 else 16, features), BF16),
            pltpu.VMEM((first_tiles, rows, tile), BF16),
        ],
        compiler_params=PARAMS,
        cost_estimate=pl.CostEstimate(
            flops=6 * rows * features * hidden,
            bytes_accessed=6 * features * hidden + 4 * rows * features,
            transcendentals=rows * hidden,
        ),
    )(tie, *parts, gate_weight, up_weight, down_weight)


def prepare_kernel(tokens, gain, routes, gates, placement, *outs):
    experts = placement.shape[0]
    features = tokens.shape[1]
    chosen = gates[...] / jnp.sum(gates[...], axis=0, keepdims=True)
    columns = jnp.concatenate([routes[...].astype(F32), chosen]).T
    count = routes.shape[0]
    lanes = outs[0].shape[1] - features
    lane = lax.broadcasted_iota(I32, (1, lanes), 1)
    named = jnp.full((1, lanes), -1.0, F32)
    for e in range(experts):
        named = jnp.where(lane == e, placement[e].astype(F32), named)
    start = 0
    for out in outs:
        rows = out.shape[0]
        at = slice(start, start + rows)
        start += rows
        values = tokens[at].astype(F32)
        rescale = lax.rsqrt(jnp.mean(values * values, axis=-1, keepdims=True) + EPSILON)
        for c in range(features // LANES):
            to = slice(c * LANES, (c + 1) * LANES)
            out[:, to] = (values[:, to] * rescale * gain[c : c + 1].astype(F32)).astype(BF16)
        table = jnp.zeros((rows, lanes), F32)
        for k in range(count):
            held = columns[at, k : k + 1] == named
            table = jnp.where(held, columns[at, count + k : count + k + 1], table)
        out[:, features:] = table.astype(BF16)


def prepare(tokens, norm_gain, routes, route_gates, placement, sizes):
    features = tokens.shape[1]
    width = features + -(-placement.shape[0] // LANES) * LANES
    vmem = pl.BlockSpec(memory_space=pltpu.VMEM)
    return pl.pallas_call(
        prepare_kernel,
        out_shape=[jax.ShapeDtypeStruct((size, width), BF16) for size in sizes],
        in_specs=[vmem] * 4 + [pl.BlockSpec(memory_space=pltpu.SMEM)],
        compiler_params=PARAMS,
    )(tokens, norm_gain.reshape(-1, LANES), routes.T, route_gates.T, placement)


def to_experts(rows):
    return lax.all_to_all(rows, "node", 0, 0, tiled=True)


def total(own, parts):
    for part in parts:
        own = own + part.astype(F32)
    return own.astype(BF16)


def body(tokens, norm_gain, routes, route_gates, placement, gate_weight, up_weight, down_weight):
    nodes, peers = lax.axis_size("node"), lax.axis_size("local")
    node, local = lax.axis_index("node"), lax.axis_index("local")
    experts = placement.shape[0]
    features = tokens.shape[1]
    capacity = BLOCK_TOK * routes.shape[1] // experts * 3 // 2
    slots = experts * capacity
    half = features // 2
    weights = (gate_weight[0], up_weight[0], down_weight[0])
    sizes = [BLOCK_TOK, 2 * BLOCK_TOK, BLOCK_TOK]
    sent0, sent12, sent3 = prepare(tokens, norm_gain, routes, route_gates, placement, sizes)

    bits_a, bits_b = bit_order(nodes, False), bit_order(nodes, True)
    ids = jnp.stack([node, local]).astype(I32)
    near = ids, peers, capacity, features
    cuts = [slots // peers * k for k in range(peers + 1)]

    near0 = swaps([sent0] * peers, "local", 1, peers)
    pair = jnp.concatenate([sent3, swap(sent3, "node", bits_a[0])])
    rows_a = gather_doubling(pair[:, :half], "node", bits_a[1:-1])
    rows_b = gather_doubling(pair[:, half:], "node", bits_b[1:-1])
    sent12, rows_a, rows_b = fence([sent12, rows_a, rows_b], near0)
    rows_a = [rows_a, swap(rows_a, "node", bits_a[-1])]
    rows_b = [rows_b, swap(rows_b, "node", bits_b[-1])]
    chain = chain_step([sent12, sent12], "local", 1)
    outbound0, mixing0 = pick([sent0] + near0, *near, chain_in=False, chain_out=False)

    outbound0, *last_rows = fence([outbound0, rows_a[1], rows_b[1]], chain)
    arrived0 = to_experts(outbound0)
    parts12 = [sent12] + chain
    for step in range(2, peers):
        chain = chain_step(chain, "local", step)
        parts12 += chain
    outbound3, mixing3a, mixing3b = pick_cross(
        [rows_a[0], last_rows[0]],
        [rows_b[0], last_rows[1]],
        gathered_from(bits_a),
        gathered_from(bits_b),
        *near,
        cuts,
    )
    outbound12, mixing1, mixing2 = pick(parts12, *near, chain_in=True, chain_out=False)

    own3, *outbound3 = outbound3
    outbound12, *outbound3 = fence([outbound12] + outbound3, [arrived0])
    arrived12 = to_experts(outbound12)
    arrived3 = swaps([None] + outbound3, "local", 1, peers)
    (out0,) = expert([arrived0.reshape(slots, features)], ids, *weights)

    out0, tie = fence([out0, ids], [arrived12] + arrived3)
    landed0 = to_experts(out0)
    size = slots // peers
    sizes = [size] * (peers - 2) + [size * 2 // 3, size // 3] * 2
    last2, last1 = peers - 2, peers - 1
    out3 = list(expert([own3] + arrived3, tie, *weights, sizes=sizes))
    landed3 = out3[:1] + swaps(out3, "local", 1, last1)
    (tie,) = fence([tie], out3[:1])
    (out1,) = expert([arrived12], tie, *weights, block=0)

    out1, part2, part3, tie = fence([out1] + out3[-3:-1] + [tie], [landed0] + landed3[1:])
    landed1 = to_experts(out1)
    landed3 += [swap(part2, "local", last2), swap(part3, "local", last1)]
    (out2,) = expert([arrived12], tie, *weights, block=1)
    (mixing0,) = fence([mixing0], [out2])
    own0, parts0 = mix(mixing0, landed0)
    parts0 = swaps([None] + parts0, "local", 1, peers)

    out2, part3 = fence([out2, out3[-1]], [landed1, own0] + landed3[-2:])
    landed2 = to_experts(out2)
    landed3.append(swap(part3, "local", last1))
    own1, parts1 = mix(mixing1, landed1)
    parts1 = swaps([None] + parts1, "local", 1, peers)
    cross = mix_cross(mixing3a, mixing3b, landed3)

    own2, parts2 = mix(mixing2, landed2)
    own0, own1, *cross = fence([own0, own1] + list(cross), parts2[:1])
    parts2 = swaps([None] + parts2, "local", 1, peers)
    sums3 = halve(*cross[:2], "node", bits_a[-1]), halve(*cross[2:], "node", bits_b[-1])
    piece0, piece1 = total(own0, parts0), total(own1, parts1)
    piece3 = [sum_halving(s, "node", bits[:-1]) for s, bits in zip(sums3, (bits_a, bits_b))]
    piece3 = jnp.concatenate(piece3, axis=1)
    piece2 = total(own2, parts2)
    return jnp.concatenate([piece0, piece1, piece2, piece3], axis=0)


def solution(mesh):
    rows = P(AXES, None)
    stacked = P(AXES, None, None)
    in_specs = (rows, P(), rows, rows, P(), stacked, stacked, stacked)
    return jax.shard_map(body, mesh=mesh, in_specs=in_specs, out_specs=rows, check_vma=False)
```

```python
import functools

import jax
import jax.numpy as jnp
import numpy as np
from jax import lax
from jax.experimental import pallas as pl
from jax.experimental.pallas import tpu as pltpu
from jax.sharding import PartitionSpec as P

BLOCK_TOK = 32
EPSILON = 1e-06
AXES = ("node", "local")
LANES = 128
TILES = 4
BF16, F32, I32 = jnp.bfloat16, jnp.float32, jnp.int32
ANYWHERE = pl.BlockSpec(memory_space=pl.ANY)
PARAMS = pltpu.CompilerParams(vmem_limit_bytes=60 * 2**20)


def fence(arrays, after):
    token = sum(a.reshape(-1, a.shape[-1])[:16, :LANES].astype(F32) for a in after)

    def kernel(*refs):
        pass

    return list(pl.pallas_call(
        kernel,
        out_shape=[jax.ShapeDtypeStruct(a.shape, a.dtype) for a in arrays],
        in_specs=[ANYWHERE] * (len(arrays) + 1),
        out_specs=[ANYWHERE] * len(arrays),
        input_output_aliases={i: i for i in range(len(arrays))},
    )(*arrays, token))


def swap(array, axis, bits):
    size = lax.axis_size(axis)
    return lax.ppermute(array, axis, [(i, i ^ bits) for i in range(size)])


def swaps(parts, axis, first, last):
    return [swap(parts[k], axis, k) for k in range(first, last)]


def bit_order(size, last_first):
    bits = [1 << i for i in range(size.bit_length() - 1)]
    return bits[:1] + bits[:0:-1] if last_first else bits


def chain_step(arrays, axis, step):
    size = lax.axis_size(axis)
    rightward = [(i, i + 1) for i in range(step - 1, size - 1)]
    leftward = [(size - 1 - i, size - 2 - i) for i in range(step - 1, size - 1)]
    return [lax.ppermute(a, axis, way) for a, way in zip(arrays, (rightward, leftward))]


def chain_offsets(size):
    return [0] + [offset for d in range(1, size) for offset in (-d, d)]


def gather_doubling(array, axis, bits):
    for bit in bits:
        array = jnp.concatenate([array, swap(array, axis, bit)])
    return array


def gathered_from(bits):
    found = [0]
    for bit in bits:
        found += [k ^ bit for k in found]
    return found


def halve(keep, give, axis, bit):
    return keep + swap(give.astype(BF16), axis, bit).astype(F32)


def sum_halving(array, axis, bits):
    for bit in bits[::-1]:
        array = halve(*jnp.split(array, 2), axis, bit)
    return array.astype(BF16)


def below(rows):
    at = np.arange(rows)
    same = at[:, None] // BLOCK_TOK == at[None, :] // BLOCK_TOK
    return (same & (at[None, :] < at[:, None])).astype(BF16)


def choose(table, lane, row_group, slot_group, turn, before):
    select = lax.broadcasted_iota(I32, (table.shape[1], lane.shape[1]), 0) == lane
    weight = jnp.dot(table, select.astype(BF16), preferred_element_type=F32)
    mask = jnp.where((weight > 0) & (row_group == slot_group), 1.0, 0.0)
    rank = jnp.dot(before, mask.astype(BF16), preferred_element_type=F32)
    place = jnp.where(rank == turn, mask, 0.0)
    return place.astype(BF16), (place * weight).astype(BF16)


def gather_rows(place, rows):
    return lax.dot_general(
        place, rows, (((0,), (0,)), ((), ())), preferred_element_type=F32
    ).astype(BF16)


def bits_of(labels, local, peers, chained):
    if not chained:
        return labels
    source = labels + local
    return jnp.where((source >= 0) & (source < peers), source ^ local, -1)


def pick_kernel(count, blocks, peers, chain_in, chain_out, ids, *refs):
    parts, refs = refs[:count], refs[count:]
    tables, refs = refs[:count], refs[count:]
    lane, slot_group, turn, before, in_column, in_row, out_column, out = refs[:8]
    mixings, places = refs[8 : 8 + blocks], refs[8 + blocks :]

    def rows_of(refs, block):
        return jnp.concatenate([r[block * BLOCK_TOK : (block + 1) * BLOCK_TOK] for r in refs])

    @pl.when(pl.program_id(0) == 0)
    def _():
        local = ids[1]
        row_group = bits_of(in_column[...], local, peers, chain_in)
        for block, (mixing, place) in enumerate(zip(mixings, places)):
            place[...], weights = choose(
                rows_of(tables, block),
                lane[...] + local,
                row_group,
                slot_group[...],
                turn[...],
                before[...],
            )
            if chain_in != chain_out:
                shape = mixing.shape[0], weights.shape[0]
                same = bits_of(out_column[...], local, peers, chain_out) == bits_of(
                    in_row[...], local, peers, chain_in
                )
                row = lax.broadcasted_iota(I32, shape, 0) & (BLOCK_TOK - 1)
                column = lax.broadcasted_iota(I32, shape, 1) & (BLOCK_TOK - 1)
                order = jnp.where(same & (row == column), 1.0, 0.0).astype(BF16)
                weights = jnp.dot(order, weights, preferred_element_type=F32).astype(BF16)
            mixing[...] = weights

    for block, place in enumerate(places):
        rows = lax.dot_general(
            place[...],
            rows_of(parts, block),
            (((0,), (0,)), ((), ())),
            preferred_element_type=F32,
        )
        nodes, _, size, tile = out.shape
        out[:, block] = rows.reshape(nodes, size, tile).astype(BF16)


def whole_block(array):
    return pl.BlockSpec(array.shape, lambda j: (0,) * array.ndim)


def by_token(labels):
    return np.repeat(np.array(labels, np.int32), BLOCK_TOK)


def pick(parts, ids, peers, capacity, features, chain_in, chain_out):
    nodes = lax.axis_size("node")
    held = parts[0].shape[0]
    blocks = held // BLOCK_TOK
    slots = nodes * peers * capacity
    slot = np.arange(slots, dtype=np.int32)[None, :]
    labels = chain_offsets(peers), list(range(peers))
    in_labels, out_labels = by_token(labels[not chain_in]), by_token(labels[not chain_out])
    rows, tile = len(in_labels), features // TILES
    small = (
        slot // (capacity * peers) * peers,
        slot // capacity % peers,
        (slot % capacity).astype(np.float32),
        below(rows),
        in_labels[:, None],
        in_labels[None, :],
        out_labels[:, None],
    )
    return pl.pallas_call(
        functools.partial(pick_kernel, len(parts), blocks, peers, chain_in, chain_out),
        grid=(TILES,),
        out_shape=[
            jax.ShapeDtypeStruct((nodes, blocks, peers * capacity, features), BF16),
        ]
        + [jax.ShapeDtypeStruct((len(out_labels), slots), BF16)] * blocks,
        in_specs=[pl.BlockSpec(memory_space=pltpu.SMEM)]
        + [pl.BlockSpec((held, tile), lambda j: (0, j))] * len(parts)
        + [pl.BlockSpec((held, LANES), lambda j: (0, features // LANES))] * len(parts)
        + [whole_block(a) for a in small],
        out_specs=[
            pl.BlockSpec((nodes, blocks, peers * capacity, tile), lambda j: (0, 0, 0, j)),
        ]
        + [pl.BlockSpec((len(out_labels), slots), lambda j: (0, 0))] * blocks,
        scratch_shapes=[pltpu.VMEM((rows, slots), BF16)] * blocks,
        compiler_params=PARAMS,
        cost_estimate=pl.CostEstimate(
            flops=2 * blocks * rows * slots * features,
            bytes_accessed=2 * blocks * (rows + slots) * features,
            transcendentals=0,
        ),
    )(ids, *parts, *parts, *small)


def pick_cross_kernel(order, cuts, peers, ids, a0, a1, b0, b1, t0, t1, *refs):
    peer, group_a, group_b, slot_group, turn, before = refs[:6]
    outs, (mixing_a, mixing_b, place_a, place_b) = refs[6:-4], refs[-4:]
    step = pl.program_id(0)

    @pl.when(step == 0)
    def _():
        known = jnp.concatenate([t0[...], t1[...]])
        lane = (peer[...] ^ ids[1]) + ids[0] * peers
        common = slot_group[...], turn[...], before[...]
        place_b[...], mixing_b[...] = choose(known, lane, group_b[...], *common)
        back = [order.index(k) * BLOCK_TOK for k in range(len(order))]
        known = jnp.concatenate([known[at : at + BLOCK_TOK] for at in back])
        place_a[...], mixing_a[...] = choose(known, lane, group_a[...], *common)

    def store(place, first_rows, last_rows):
        result = gather_rows(place[...], jnp.concatenate([first_rows[...], last_rows[...]]))
        for out, first, last in zip(outs, cuts[:-1], cuts[1:]):
            out[...] = result[first:last]

    @pl.when(step < TILES // 2)
    def _():
        store(place_a, a0, a1)

    @pl.when(step >= TILES // 2)
    def _():
        store(place_b, b0, b1)


def in_first_half(shape):
    return pl.BlockSpec(shape, lambda j: (0, jnp.minimum(j, TILES // 2 - 1)))


def in_second_half(shape):
    return pl.BlockSpec(shape, lambda j: (0, jnp.maximum(j - TILES // 2, 0)))


def pick_cross(rows_a, rows_b, order_a, order_b, ids, peers, capacity, features, cuts):
    part = rows_a[0].shape[0]
    rows = 2 * part
    nodes = rows // BLOCK_TOK
    slots = cuts[-1]
    slot = np.arange(slots, dtype=np.int32)[None, :]
    tile = features // TILES
    small = (
        slot // (capacity * nodes),
        by_token(order_a)[:, None],
        by_token(order_b)[:, None],
        slot // capacity % nodes,
        (slot % capacity).astype(np.float32),
        below(rows),
    )
    sizes = [last - first for first, last in zip(cuts[:-1], cuts[1:])]
    results = pl.pallas_call(
        functools.partial(pick_cross_kernel, order_b, cuts, peers),
        grid=(TILES,),
        out_shape=[jax.ShapeDtypeStruct((size, features), BF16) for size in sizes]
        + [jax.ShapeDtypeStruct((rows, slots), BF16)] * 2,
        in_specs=[pl.BlockSpec(memory_space=pltpu.SMEM)]
        + [in_first_half((part, tile))] * 2
        + [in_second_half((part, tile))] * 2
        + [pl.BlockSpec((part, LANES), lambda j: (0, features // 2 // LANES))] * 2
        + [whole_block(a) for a in small],
        out_specs=[pl.BlockSpec((size, tile), lambda j: (0, j)) for size in sizes]
        + [pl.BlockSpec((rows, slots), lambda j: (0, 0))] * 2,
        scratch_shapes=[pltpu.VMEM((rows, slots), BF16)] * 2,
        compiler_params=PARAMS,
        cost_estimate=pl.CostEstimate(
            flops=2 * rows * slots * features,
            bytes_accessed=2 * (rows + slots) * features,
            transcendentals=0,
        ),
    )(ids, *rows_a, *rows_b, *rows_b, *small)
    return list(results[:-2]), results[-2], results[-1]


def mix_kernel(mixing, landed, own, *outs):
    result = jnp.dot(mixing[...], landed[...], preferred_element_type=F32)
    own[...] = result[:BLOCK_TOK]
    for k, out in enumerate(outs):
        out[...] = result[(k + 1) * BLOCK_TOK : (k + 2) * BLOCK_TOK].astype(BF16)


def mix(mixing, landed):
    rows, slots = mixing.shape
    features = landed.shape[1]
    tile = features // TILES
    count = rows // BLOCK_TOK
    own, *parts = pl.pallas_call(
        mix_kernel,
        grid=(TILES,),
        out_shape=[jax.ShapeDtypeStruct((BLOCK_TOK, features), F32)]
        + [jax.ShapeDtypeStruct((BLOCK_TOK, features), BF16)] * (count - 1),
        in_specs=[whole_block(mixing), pl.BlockSpec((slots, tile), lambda j: (0, j))],
        out_specs=[pl.BlockSpec((BLOCK_TOK, tile), lambda j: (0, j))] * count,
        compiler_params=PARAMS,
        cost_estimate=pl.CostEstimate(
            flops=2 * rows * slots * features,
            bytes_accessed=2 * (rows + slots) * features,
            transcendentals=0,
        ),
    )(mixing, landed)
    return own, parts


def mix_cross_kernel(mixing_a, mixing_b, *refs):
    landed, (keep_a, give_a, keep_b, give_b) = refs[:-4], refs[-4:]
    step = pl.program_id(0)
    half = keep_a.shape[0]
    rows = jnp.concatenate([part[...] for part in landed])

    def store(mixing, keep, give):
        result = jnp.dot(mixing[...], rows, preferred_element_type=F32)
        keep[...] = result[:half]
        give[...] = result[half:].astype(BF16)

    @pl.when(step < TILES // 2)
    def _():
        store(mixing_a, keep_a, give_a)

    @pl.when(step >= TILES // 2)
    def _():
        store(mixing_b, keep_b, give_b)


def mix_cross(mixing_a, mixing_b, landed):
    rows, slots = mixing_a.shape
    features = landed[0].shape[1]
    tile = features // TILES
    shape = (rows // 2, features // 2)
    return pl.pallas_call(
        mix_cross_kernel,
        grid=(TILES,),
        out_shape=[jax.ShapeDtypeStruct(shape, F32), jax.ShapeDtypeStruct(shape, BF16)] * 2,
        in_specs=[whole_block(mixing_a), whole_block(mixing_b)]
        + [pl.BlockSpec((part.shape[0], tile), lambda j: (0, j)) for part in landed],
        out_specs=[in_first_half((rows // 2, tile))] * 2 + [in_second_half((rows // 2, tile))] * 2,
        compiler_params=PARAMS,
        cost_estimate=pl.CostEstimate(
            flops=2 * rows * slots * features,
            bytes_accessed=2 * (rows + slots) * features,
            transcendentals=0,
        ),
    )(mixing_a, mixing_b, *landed)


def expert_kernel(count, first_tiles, nodes, tie, *refs):
    parts, (gate_ref, up_ref, down_ref) = refs[:count], refs[count : count + 3]
    outs, (joined, hidden) = refs[count + 3 : -2], refs[-2:]
    step = pl.program_id(0)
    x_ref = parts[0] if count == 1 and not nodes else joined

    if x_ref is joined:

        @pl.when(step == 0)
        def _():
            pieces = [parts[0][n, 0] for n in range(nodes)] or [part[...] for part in parts]
            joined[...] = jnp.concatenate(pieces)

    @pl.when(step < first_tiles)
    def _():
        x = x_ref[...]
        gate_pre = jnp.dot(x, gate_ref[...], preferred_element_type=F32)
        up_pre = jnp.dot(x, up_ref[...], preferred_element_type=F32)
        hidden[step] = (gate_pre / (1 + jnp.exp(-gate_pre)) * up_pre).astype(BF16)

    @pl.when(step >= first_tiles)
    def _():
        rows = jnp.concatenate([hidden[i] for i in range(first_tiles)], axis=1)
        result = jnp.dot(rows, down_ref[...], preferred_element_type=F32)
        result = result.astype(BF16)
        at = 0
        for out in outs:
            out[...] = result[at : at + out.shape[0]]
            at += out.shape[0]


def expert(parts, tie, gate_weight, up_weight, down_weight, block=None, sizes=None):
    sizes = sizes or [part.shape[0] for part in parts]
    specs = [whole_block(part) for part in parts]
    nodes = 0
    if block is not None:
        nodes, _, size, features = parts[0].shape
        sizes = [nodes * size]
        specs = [pl.BlockSpec((nodes, 1, size, features), lambda i: (0, block, 0, 0))]
    rows = sum(sizes)
    features, hidden = gate_weight.shape
    tile = 256
    first_tiles = hidden // tile
    out_tile = features // TILES

    def first(i):
        return jnp.minimum(i, first_tiles - 1)

    def second(i):
        return jnp.maximum(i - first_tiles, 0)

    return pl.pallas_call(
        functools.partial(expert_kernel, len(parts), first_tiles, nodes),
        grid=(first_tiles + TILES,),
        out_shape=[jax.ShapeDtypeStruct((size, features), BF16) for size in sizes],
        in_specs=[pl.BlockSpec(memory_space=pltpu.SMEM)]
        + specs
        + [
            pl.BlockSpec((features, tile), lambda i: (0, first(i))),
            pl.BlockSpec((features, tile), lambda i: (0, first(i))),
            pl.BlockSpec((hidden, out_tile), lambda i: (0, second(i))),
        ],
        out_specs=[
            pl.BlockSpec((size, out_tile), lambda i: (0, second(i))) for size in sizes
        ],
        scratch_shapes=[
            pltpu.VMEM((rows if nodes or len(parts) > 1 else 16, features), BF16),
            pltpu.VMEM((first_tiles, rows, tile), BF16),
        ],
        compiler_params=PARAMS,
        cost_estimate=pl.CostEstimate(
            flops=6 * rows * features * hidden,
            bytes_accessed=6 * features * hidden + 4 * rows * features,
            transcendentals=rows * hidden,
        ),
    )(tie, *parts, gate_weight, up_weight, down_weight)


def prepare_kernel(tokens, gain, routes, gates, placement, *outs):
    experts = placement.shape[0]
    features = tokens.shape[1]
    chosen = gates[...] / jnp.sum(gates[...], axis=0, keepdims=True)
    columns = jnp.concatenate([routes[...].astype(F32), chosen]).T
    count = routes.shape[0]
    lanes = outs[0].shape[1] - features
    lane = lax.broadcasted_iota(I32, (1, lanes), 1)
    named = jnp.full((1, lanes), -1.0, F32)
    for e in range(experts):
        named = jnp.where(lane == e, placement[e].astype(F32), named)
    start = 0
    for out in outs:
        rows = out.shape[0]
        at = slice(start, start + rows)
        start += rows
        values = tokens[at].astype(F32)
        rescale = lax.rsqrt(jnp.mean(values * values, axis=-1, keepdims=True) + EPSILON)
        for c in range(features // LANES):
            to = slice(c * LANES, (c + 1) * LANES)
            out[:, to] = (values[:, to] * rescale * gain[c : c + 1].astype(F32)).astype(BF16)
        table = jnp.zeros((rows, lanes), F32)
        for k in range(count):
            held = columns[at, k : k + 1] == named
            table = jnp.where(held, columns[at, count + k : count + k + 1], table)
        out[:, features:] = table.astype(BF16)


def prepare(tokens, norm_gain, routes, route_gates, placement, sizes):
    features = tokens.shape[1]
    width = features + -(-placement.shape[0] // LANES) * LANES
    vmem = pl.BlockSpec(memory_space=pltpu.VMEM)
    return pl.pallas_call(
        prepare_kernel,
        out_shape=[jax.ShapeDtypeStruct((size, width), BF16) for size in sizes],
        in_specs=[vmem] * 4 + [pl.BlockSpec(memory_space=pltpu.SMEM)],
        compiler_params=PARAMS,
    )(tokens, norm_gain.reshape(-1, LANES), routes.T, route_gates.T, placement)


def to_experts(rows):
    return lax.all_to_all(rows, "node", 0, 0, tiled=True)


def total(own, parts):
    for part in parts:
        own = own + part.astype(F32)
    return own.astype(BF16)


def body(tokens, norm_gain, routes, route_gates, placement, gate_weight, up_weight, down_weight):
    nodes, peers = lax.axis_size("node"), lax.axis_size("local")
    node, local = lax.axis_index("node"), lax.axis_index("local")
    experts = placement.shape[0]
    features = tokens.shape[1]
    capacity = BLOCK_TOK * routes.shape[1] // experts * 3 // 2
    slots = experts * capacity
    half = features // 2
    weights = (gate_weight[0], up_weight[0], down_weight[0])
    sizes = [BLOCK_TOK, 2 * BLOCK_TOK, BLOCK_TOK]
    sent0, sent12, sent3 = prepare(tokens, norm_gain, routes, route_gates, placement, sizes)

    bits_a, bits_b = bit_order(nodes, False), bit_order(nodes, True)
    ids = jnp.stack([node, local]).astype(I32)
    near = ids, peers, capacity, features
    cuts = [slots // peers * k for k in range(peers + 1)]

    near0 = swaps([sent0] * peers, "local", 1, peers)
    pair = jnp.concatenate([sent3, swap(sent3, "node", bits_a[0])])
    rows_a = gather_doubling(pair[:, :half], "node", bits_a[1:-1])
    rows_b = gather_doubling(pair[:, half:], "node", bits_b[1:-1])
    sent12, rows_a, rows_b = fence([sent12, rows_a, rows_b], near0)
    rows_a = [rows_a, swap(rows_a, "node", bits_a[-1])]
    rows_b = [rows_b, swap(rows_b, "node", bits_b[-1])]
    chain = chain_step([sent12, sent12], "local", 1)
    outbound0, mixing0 = pick([sent0] + near0, *near, chain_in=False, chain_out=False)

    outbound0, *last_rows = fence([outbound0, rows_a[1], rows_b[1]], chain)
    arrived0 = to_experts(outbound0)
    parts12 = [sent12] + chain
    for step in range(2, peers):
        chain = chain_step(chain, "local", step)
        parts12 += chain
    outbound3, mixing3a, mixing3b = pick_cross(
        [rows_a[0], last_rows[0]],
        [rows_b[0], last_rows[1]],
        gathered_from(bits_a),
        gathered_from(bits_b),
        *near,
        cuts,
    )
    outbound12, mixing1, mixing2 = pick(parts12, *near, chain_in=True, chain_out=False)

    own3, *outbound3 = outbound3
    outbound12, *outbound3 = fence([outbound12] + outbound3, [arrived0])
    arrived12 = to_experts(outbound12)
    arrived3 = swaps([None] + outbound3, "local", 1, peers)
    (out0,) = expert([arrived0.reshape(slots, features)], ids, *weights)

    out0, tie = fence([out0, ids], [arrived12] + arrived3)
    landed0 = to_experts(out0)
    size = slots // peers
    sizes = [size] * (peers - 2) + [size // 2] * 4
    last2, last1 = peers - 2, peers - 1
    out3 = list(expert([own3] + arrived3, tie, *weights, sizes=sizes))
    landed3 = out3[:1] + swaps(out3, "local", 1, last1)
    (tie,) = fence([tie], out3[:1])
    (out1,) = expert([arrived12], tie, *weights, block=0)

    out1, part2, part3, tie = fence([out1] + out3[-3:-1] + [tie], [landed0] + landed3[1:])
    landed1 = to_experts(out1)
    landed3 += [swap(part2, "local", last2), swap(part3, "local", last1)]
    (out2,) = expert([arrived12], tie, *weights, block=1)
    (mixing0,) = fence([mixing0], [out2])
    own0, parts0 = mix(mixing0, landed0)
    parts0 = swaps([None] + parts0, "local", 1, peers)

    out2, part3 = fence([out2, out3[-1]], [landed1, own0] + landed3[-2:])
    landed2 = to_experts(out2)
    landed3.append(swap(part3, "local", last1))
    own1, parts1 = mix(mixing1, landed1)
    parts1 = swaps([None] + parts1, "local", 1, peers)
    cross = mix_cross(mixing3a, mixing3b, landed3)

    own2, parts2 = mix(mixing2, landed2)
    own1, *cross = fence([own1] + list(cross), parts2[:1])
    parts2 = swaps([None] + parts2, "local", 1, peers)
    sums3 = halve(*cross[:2], "node", bits_a[-1]), halve(*cross[2:], "node", bits_b[-1])
    (own2,) = fence([own2], [sums3[0]])
    piece0, piece1 = total(own0, parts0), total(own1, parts1)
    piece3 = [sum_halving(s, "node", bits[:-1]) for s, bits in zip(sums3, (bits_a, bits_b))]
    piece3 = jnp.concatenate(piece3, axis=1)
    piece2 = total(own2, parts2)
    return jnp.concatenate([piece0, piece1, piece2, piece3], axis=0)


def solution(mesh):
    rows = P(AXES, None)
    stacked = P(AXES, None, None)
    in_specs = (rows, P(), rows, rows, P(), stacked, stacked, stacked)
    return jax.shard_map(body, mesh=mesh, in_specs=in_specs, out_specs=rows, check_vma=False)
```

```python
import functools

import jax
import jax.numpy as jnp
import numpy as np
from jax import lax
from jax.experimental import pallas as pl
from jax.experimental.pallas import tpu as pltpu
from jax.sharding import PartitionSpec as P

BLOCK_TOK = 32
EPSILON = 1e-06
AXES = ("node", "local")
LANES = 128
TILES = 4
BF16, F32, I32 = jnp.bfloat16, jnp.float32, jnp.int32
ANYWHERE = pl.BlockSpec(memory_space=pl.ANY)
PARAMS = pltpu.CompilerParams(vmem_limit_bytes=60 * 2**20)


def fence(arrays, after):
    token = sum(a.reshape(-1, a.shape[-1])[:16, :LANES].astype(F32) for a in after)

    def kernel(*refs):
        pass

    return list(pl.pallas_call(
        kernel,
        out_shape=[jax.ShapeDtypeStruct(a.shape, a.dtype) for a in arrays],
        in_specs=[ANYWHERE] * (len(arrays) + 1),
        out_specs=[ANYWHERE] * len(arrays),
        input_output_aliases={i: i for i in range(len(arrays))},
    )(*arrays, token))


def swap(array, axis, bits):
    size = lax.axis_size(axis)
    return lax.ppermute(array, axis, [(i, i ^ bits) for i in range(size)])


def swaps(parts, axis, first, last):
    return [swap(parts[k], axis, k) for k in range(first, last)]


def bit_order(size, last_first):
    bits = [1 << i for i in range(size.bit_length() - 1)]
    return bits[:1] + bits[:0:-1] if last_first else bits


def chain_step(arrays, axis, step):
    size = lax.axis_size(axis)
    rightward = [(i, i + 1) for i in range(step - 1, size - 1)]
    leftward = [(size - 1 - i, size - 2 - i) for i in range(step - 1, size - 1)]
    return [lax.ppermute(a, axis, way) for a, way in zip(arrays, (rightward, leftward))]


def chain_offsets(size):
    return [0] + [offset for d in range(1, size) for offset in (-d, d)]


def gather_doubling(array, axis, bits):
    for bit in bits:
        array = jnp.concatenate([array, swap(array, axis, bit)])
    return array


def gathered_from(bits):
    found = [0]
    for bit in bits:
        found += [k ^ bit for k in found]
    return found


def halve(keep, give, axis, bit):
    return keep + swap(give.astype(BF16), axis, bit).astype(F32)


def sum_halving(array, axis, bits):
    for bit in bits[::-1]:
        array = halve(*jnp.split(array, 2), axis, bit)
    return array.astype(BF16)


def below(rows):
    at = np.arange(rows)
    same = at[:, None] // BLOCK_TOK == at[None, :] // BLOCK_TOK
    return (same & (at[None, :] < at[:, None])).astype(BF16)


def choose(table, lane, row_group, slot_group, turn, before):
    select = lax.broadcasted_iota(I32, (table.shape[1], lane.shape[1]), 0) == lane
    weight = jnp.dot(table, select.astype(BF16), preferred_element_type=F32)
    mask = jnp.where((weight > 0) & (row_group == slot_group), 1.0, 0.0)
    rank = jnp.dot(before, mask.astype(BF16), preferred_element_type=F32)
    place = jnp.where(rank == turn, mask, 0.0)
    return place.astype(BF16), (place * weight).astype(BF16)


def gather_rows(place, rows):
    return lax.dot_general(
        place, rows, (((0,), (0,)), ((), ())), preferred_element_type=F32
    ).astype(BF16)


def bits_of(labels, local, peers, chained):
    if not chained:
        return labels
    source = labels + local
    return jnp.where((source >= 0) & (source < peers), source ^ local, -1)


def pick_kernel(count, blocks, peers, chain_in, chain_out, ids, *refs):
    parts, refs = refs[:count], refs[count:]
    tables, refs = refs[:count], refs[count:]
    lane, slot_group, turn, before, in_column, in_row, out_column, out = refs[:8]
    mixings, places = refs[8 : 8 + blocks], refs[8 + blocks :]

    def rows_of(refs, block):
        return jnp.concatenate([r[block * BLOCK_TOK : (block + 1) * BLOCK_TOK] for r in refs])

    @pl.when(pl.program_id(0) == 0)
    def _():
        local = ids[1]
        row_group = bits_of(in_column[...], local, peers, chain_in)
        for block, (mixing, place) in enumerate(zip(mixings, places)):
            place[...], weights = choose(
                rows_of(tables, block),
                lane[...] + local,
                row_group,
                slot_group[...],
                turn[...],
                before[...],
            )
            if chain_in != chain_out:
                shape = mixing.shape[0], weights.shape[0]
                same = bits_of(out_column[...], local, peers, chain_out) == bits_of(
                    in_row[...], local, peers, chain_in
                )
                row = lax.broadcasted_iota(I32, shape, 0) & (BLOCK_TOK - 1)
                column = lax.broadcasted_iota(I32, shape, 1) & (BLOCK_TOK - 1)
                order = jnp.where(same & (row == column), 1.0, 0.0).astype(BF16)
                weights = jnp.dot(order, weights, preferred_element_type=F32).astype(BF16)
            mixing[...] = weights

    for block, place in enumerate(places):
        rows = lax.dot_general(
            place[...],
            rows_of(parts, block),
            (((0,), (0,)), ((), ())),
            preferred_element_type=F32,
        )
        nodes, _, size, tile = out.shape
        out[:, block] = rows.reshape(nodes, size, tile).astype(BF16)


def whole_block(array):
    return pl.BlockSpec(array.shape, lambda j: (0,) * array.ndim)


def by_token(labels):
    return np.repeat(np.array(labels, np.int32), BLOCK_TOK)


def pick(parts, ids, peers, capacity, features, chain_in, chain_out):
    nodes = lax.axis_size("node")
    held = parts[0].shape[0]
    blocks = held // BLOCK_TOK
    slots = nodes * peers * capacity
    slot = np.arange(slots, dtype=np.int32)[None, :]
    labels = chain_offsets(peers), list(range(peers))
    in_labels, out_labels = by_token(labels[not chain_in]), by_token(labels[not chain_out])
    rows, tile = len(in_labels), features // TILES
    small = (
        slot // (capacity * peers) * peers,
        slot // capacity % peers,
        (slot % capacity).astype(np.float32),
        below(rows),
        in_labels[:, None],
        in_labels[None, :],
        out_labels[:, None],
    )
    return pl.pallas_call(
        functools.partial(pick_kernel, len(parts), blocks, peers, chain_in, chain_out),
        grid=(TILES,),
        out_shape=[
            jax.ShapeDtypeStruct((nodes, blocks, peers * capacity, features), BF16),
        ]
        + [jax.ShapeDtypeStruct((len(out_labels), slots), BF16)] * blocks,
        in_specs=[pl.BlockSpec(memory_space=pltpu.SMEM)]
        + [pl.BlockSpec((held, tile), lambda j: (0, j))] * len(parts)
        + [pl.BlockSpec((held, LANES), lambda j: (0, features // LANES))] * len(parts)
        + [whole_block(a) for a in small],
        out_specs=[
            pl.BlockSpec((nodes, blocks, peers * capacity, tile), lambda j: (0, 0, 0, j)),
        ]
        + [pl.BlockSpec((len(out_labels), slots), lambda j: (0, 0))] * blocks,
        scratch_shapes=[pltpu.VMEM((rows, slots), BF16)] * blocks,
        compiler_params=PARAMS,
        cost_estimate=pl.CostEstimate(
            flops=2 * blocks * rows * slots * features,
            bytes_accessed=2 * blocks * (rows + slots) * features,
            transcendentals=0,
        ),
    )(ids, *parts, *parts, *small)


def pick_cross_kernel(order, cuts, peers, ids, a0, a1, b0, b1, t0, t1, *refs):
    peer, group_a, group_b, slot_group, turn, before = refs[:6]
    outs, (mixing_a, mixing_b, place_a, place_b) = refs[6:-4], refs[-4:]
    step = pl.program_id(0)

    @pl.when(step == 0)
    def _():
        known = jnp.concatenate([t0[...], t1[...]])
        lane = (peer[...] ^ ids[1]) + ids[0] * peers
        common = slot_group[...], turn[...], before[...]
        place_b[...], mixing_b[...] = choose(known, lane, group_b[...], *common)
        back = [order.index(k) * BLOCK_TOK for k in range(len(order))]
        known = jnp.concatenate([known[at : at + BLOCK_TOK] for at in back])
        place_a[...], mixing_a[...] = choose(known, lane, group_a[...], *common)

    def store(place, first_rows, last_rows):
        result = gather_rows(place[...], jnp.concatenate([first_rows[...], last_rows[...]]))
        for out, first, last in zip(outs, cuts[:-1], cuts[1:]):
            out[...] = result[first:last]

    @pl.when(step < TILES // 2)
    def _():
        store(place_a, a0, a1)

    @pl.when(step >= TILES // 2)
    def _():
        store(place_b, b0, b1)


def in_first_half(shape):
    return pl.BlockSpec(shape, lambda j: (0, jnp.minimum(j, TILES // 2 - 1)))


def in_second_half(shape):
    return pl.BlockSpec(shape, lambda j: (0, jnp.maximum(j - TILES // 2, 0)))


def pick_cross(rows_a, rows_b, order_a, order_b, ids, peers, capacity, features, cuts):
    part = rows_a[0].shape[0]
    rows = 2 * part
    nodes = rows // BLOCK_TOK
    slots = cuts[-1]
    slot = np.arange(slots, dtype=np.int32)[None, :]
    tile = features // TILES
    small = (
        slot // (capacity * nodes),
        by_token(order_a)[:, None],
        by_token(order_b)[:, None],
        slot // capacity % nodes,
        (slot % capacity).astype(np.float32),
        below(rows),
    )
    sizes = [last - first for first, last in zip(cuts[:-1], cuts[1:])]
    results = pl.pallas_call(
        functools.partial(pick_cross_kernel, order_b, cuts, peers),
        grid=(TILES,),
        out_shape=[jax.ShapeDtypeStruct((size, features), BF16) for size in sizes]
        + [jax.ShapeDtypeStruct((rows, slots), BF16)] * 2,
        in_specs=[pl.BlockSpec(memory_space=pltpu.SMEM)]
        + [in_first_half((part, tile))] * 2
        + [in_second_half((part, tile))] * 2
        + [pl.BlockSpec((part, LANES), lambda j: (0, features // 2 // LANES))] * 2
        + [whole_block(a) for a in small],
        out_specs=[pl.BlockSpec((size, tile), lambda j: (0, j)) for size in sizes]
        + [pl.BlockSpec((rows, slots), lambda j: (0, 0))] * 2,
        scratch_shapes=[pltpu.VMEM((rows, slots), BF16)] * 2,
        compiler_params=PARAMS,
        cost_estimate=pl.CostEstimate(
            flops=2 * rows * slots * features,
            bytes_accessed=2 * (rows + slots) * features,
            transcendentals=0,
        ),
    )(ids, *rows_a, *rows_b, *rows_b, *small)
    return list(results[:-2]), results[-2], results[-1]


def mix_kernel(mixing, landed, own, *outs):
    result = jnp.dot(mixing[...], landed[...], preferred_element_type=F32)
    own[...] = result[:BLOCK_TOK]
    for k, out in enumerate(outs):
        out[...] = result[(k + 1) * BLOCK_TOK : (k + 2) * BLOCK_TOK].astype(BF16)


def mix(mixing, landed):
    rows, slots = mixing.shape
    features = landed.shape[1]
    tile = features // TILES
    count = rows // BLOCK_TOK
    own, *parts = pl.pallas_call(
        mix_kernel,
        grid=(TILES,),
        out_shape=[jax.ShapeDtypeStruct((BLOCK_TOK, features), F32)]
        + [jax.ShapeDtypeStruct((BLOCK_TOK, features), BF16)] * (count - 1),
        in_specs=[whole_block(mixing), pl.BlockSpec((slots, tile), lambda j: (0, j))],
        out_specs=[pl.BlockSpec((BLOCK_TOK, tile), lambda j: (0, j))] * count,
        compiler_params=PARAMS,
        cost_estimate=pl.CostEstimate(
            flops=2 * rows * slots * features,
            bytes_accessed=2 * (rows + slots) * features,
            transcendentals=0,
        ),
    )(mixing, landed)
    return own, parts


def mix_cross_kernel(mixing_a, mixing_b, *refs):
    landed, (keep_a, give_a, keep_b, give_b) = refs[:-4], refs[-4:]
    step = pl.program_id(0)
    half = keep_a.shape[0]
    rows = jnp.concatenate([part[...] for part in landed])

    def store(mixing, keep, give):
        result = jnp.dot(mixing[...], rows, preferred_element_type=F32)
        keep[...] = result[:half]
        give[...] = result[half:].astype(BF16)

    @pl.when(step < TILES // 2)
    def _():
        store(mixing_a, keep_a, give_a)

    @pl.when(step >= TILES // 2)
    def _():
        store(mixing_b, keep_b, give_b)


def mix_cross(mixing_a, mixing_b, landed):
    rows, slots = mixing_a.shape
    features = landed[0].shape[1]
    tile = features // TILES
    shape = (rows // 2, features // 2)
    return pl.pallas_call(
        mix_cross_kernel,
        grid=(TILES,),
        out_shape=[jax.ShapeDtypeStruct(shape, F32), jax.ShapeDtypeStruct(shape, BF16)] * 2,
        in_specs=[whole_block(mixing_a), whole_block(mixing_b)]
        + [pl.BlockSpec((part.shape[0], tile), lambda j: (0, j)) for part in landed],
        out_specs=[in_first_half((rows // 2, tile))] * 2 + [in_second_half((rows // 2, tile))] * 2,
        compiler_params=PARAMS,
        cost_estimate=pl.CostEstimate(
            flops=2 * rows * slots * features,
            bytes_accessed=2 * (rows + slots) * features,
            transcendentals=0,
        ),
    )(mixing_a, mixing_b, *landed)


def expert_kernel(count, first_tiles, nodes, tie, *refs):
    parts, (gate_ref, up_ref, down_ref) = refs[:count], refs[count : count + 3]
    outs, (joined, hidden) = refs[count + 3 : -2], refs[-2:]
    step = pl.program_id(0)
    x_ref = parts[0] if count == 1 and not nodes else joined

    if x_ref is joined:

        @pl.when(step == 0)
        def _():
            pieces = [parts[0][n, 0] for n in range(nodes)] or [part[...] for part in parts]
            joined[...] = jnp.concatenate(pieces)

    @pl.when(step < first_tiles)
    def _():
        x = x_ref[...]
        gate_pre = jnp.dot(x, gate_ref[...], preferred_element_type=F32)
        up_pre = jnp.dot(x, up_ref[...], preferred_element_type=F32)
        hidden[step] = (gate_pre / (1 + jnp.exp(-gate_pre)) * up_pre).astype(BF16)

    @pl.when(step >= first_tiles)
    def _():
        rows = jnp.concatenate([hidden[i] for i in range(first_tiles)], axis=1)
        result = jnp.dot(rows, down_ref[...], preferred_element_type=F32)
        result = result.astype(BF16)
        at = 0
        for out in outs:
            out[...] = result[at : at + out.shape[0]]
            at += out.shape[0]


def expert(parts, tie, gate_weight, up_weight, down_weight, block=None, sizes=None):
    sizes = sizes or [part.shape[0] for part in parts]
    specs = [whole_block(part) for part in parts]
    nodes = 0
    if block is not None:
        nodes, _, size, features = parts[0].shape
        sizes = [nodes * size]
        specs = [pl.BlockSpec((nodes, 1, size, features), lambda i: (0, block, 0, 0))]
    rows = sum(sizes)
    features, hidden = gate_weight.shape
    tile = 256
    first_tiles = hidden // tile
    out_tile = features // TILES

    def first(i):
        return jnp.minimum(i, first_tiles - 1)

    def second(i):
        return jnp.maximum(i - first_tiles, 0)

    return pl.pallas_call(
        functools.partial(expert_kernel, len(parts), first_tiles, nodes),
        grid=(first_tiles + TILES,),
        out_shape=[jax.ShapeDtypeStruct((size, features), BF16) for size in sizes],
        in_specs=[pl.BlockSpec(memory_space=pltpu.SMEM)]
        + specs
        + [
            pl.BlockSpec((features, tile), lambda i: (0, first(i))),
            pl.BlockSpec((features, tile), lambda i: (0, first(i))),
            pl.BlockSpec((hidden, out_tile), lambda i: (0, second(i))),
        ],
        out_specs=[
            pl.BlockSpec((size, out_tile), lambda i: (0, second(i))) for size in sizes
        ],
        scratch_shapes=[
            pltpu.VMEM((rows if nodes or len(parts) > 1 else 16, features), BF16),
            pltpu.VMEM((first_tiles, rows, tile), BF16),
        ],
        compiler_params=PARAMS,
        cost_estimate=pl.CostEstimate(
            flops=6 * rows * features * hidden,
            bytes_accessed=6 * features * hidden + 4 * rows * features,
            transcendentals=rows * hidden,
        ),
    )(tie, *parts, gate_weight, up_weight, down_weight)


def prepare_kernel(tokens, gain, routes, gates, placement, *outs):
    experts = placement.shape[0]
    features = tokens.shape[1]
    chosen = gates[...] / jnp.sum(gates[...], axis=0, keepdims=True)
    columns = jnp.concatenate([routes[...].astype(F32), chosen]).T
    count = routes.shape[0]
    lanes = outs[0].shape[1] - features
    lane = lax.broadcasted_iota(I32, (1, lanes), 1)
    named = jnp.full((1, lanes), -1.0, F32)
    for e in range(experts):
        named = jnp.where(lane == e, placement[e].astype(F32), named)
    start = 0
    for out in outs:
        rows = out.shape[0]
        at = slice(start, start + rows)
        start += rows
        values = tokens[at].astype(F32)
        rescale = lax.rsqrt(jnp.mean(values * values, axis=-1, keepdims=True) + EPSILON)
        for c in range(features // LANES):
            to = slice(c * LANES, (c + 1) * LANES)
            out[:, to] = (values[:, to] * rescale * gain[c : c + 1].astype(F32)).astype(BF16)
        table = jnp.zeros((rows, lanes), F32)
        for k in range(count):
            held = columns[at, k : k + 1] == named
            table = jnp.where(held, columns[at, count + k : count + k + 1], table)
        out[:, features:] = table.astype(BF16)


def prepare(tokens, norm_gain, routes, route_gates, placement, sizes):
    features = tokens.shape[1]
    width = features + -(-placement.shape[0] // LANES) * LANES
    vmem = pl.BlockSpec(memory_space=pltpu.VMEM)
    return pl.pallas_call(
        prepare_kernel,
        out_shape=[jax.ShapeDtypeStruct((size, width), BF16) for size in sizes],
        in_specs=[vmem] * 4 + [pl.BlockSpec(memory_space=pltpu.SMEM)],
        compiler_params=PARAMS,
    )(tokens, norm_gain.reshape(-1, LANES), routes.T, route_gates.T, placement)


def to_experts(rows):
    return lax.all_to_all(rows, "node", 0, 0, tiled=True)


def total(own, parts):
    for part in parts:
        own = own + part.astype(F32)
    return own.astype(BF16)


def body(tokens, norm_gain, routes, route_gates, placement, gate_weight, up_weight, down_weight):
    nodes, peers = lax.axis_size("node"), lax.axis_size("local")
    node, local = lax.axis_index("node"), lax.axis_index("local")
    experts = placement.shape[0]
    features = tokens.shape[1]
    capacity = BLOCK_TOK * routes.shape[1] // experts * 3 // 2
    slots = experts * capacity
    half = features // 2
    weights = (gate_weight[0], up_weight[0], down_weight[0])
    sizes = [BLOCK_TOK, 2 * BLOCK_TOK, BLOCK_TOK]
    sent0, sent12, sent3 = prepare(tokens, norm_gain, routes, route_gates, placement, sizes)

    bits_a, bits_b = bit_order(nodes, False), bit_order(nodes, True)
    ids = jnp.stack([node, local]).astype(I32)
    near = ids, peers, capacity, features
    cuts = [slots // peers * k for k in range(peers + 1)]

    near0 = swaps([sent0] * peers, "local", 1, peers)
    pair = jnp.concatenate([sent3, swap(sent3, "node", bits_a[0])])
    rows_a = gather_doubling(pair[:, :half], "node", bits_a[1:-1])
    rows_b = gather_doubling(pair[:, half:], "node", bits_b[1:-1])
    sent12, rows_a, rows_b = fence([sent12, rows_a, rows_b], near0)
    rows_a = [rows_a, swap(rows_a, "node", bits_a[-1])]
    rows_b = [rows_b, swap(rows_b, "node", bits_b[-1])]
    chain = chain_step([sent12, sent12], "local", 1)
    outbound0, mixing0 = pick([sent0] + near0, *near, chain_in=False, chain_out=False)

    outbound0, *last_rows = fence([outbound0, rows_a[1], rows_b[1]], chain)
    arrived0 = to_experts(outbound0)
    parts12 = [sent12] + chain
    for step in range(2, peers):
        chain = chain_step(chain, "local", step)
        parts12 += chain
    outbound3, mixing3a, mixing3b = pick_cross(
        [rows_a[0], last_rows[0]],
        [rows_b[0], last_rows[1]],
        gathered_from(bits_a),
        gathered_from(bits_b),
        *near,
        cuts,
    )
    outbound12, mixing1, mixing2 = pick(parts12, *near, chain_in=True, chain_out=False)

    own3, *outbound3 = outbound3
    outbound12, *outbound3 = fence([outbound12] + outbound3, [arrived0])
    arrived12 = to_experts(outbound12)
    arrived3 = swaps([None] + outbound3, "local", 1, peers)
    (out0,) = expert([arrived0.reshape(slots, features)], ids, *weights)

    out0, tie = fence([out0, ids], [arrived12] + arrived3)
    landed0 = to_experts(out0)
    size = slots // peers
    sizes = [size] * (peers - 2) + [size // 2] * 4
    last2, last1 = peers - 2, peers - 1
    out3 = list(expert([own3] + arrived3, tie, *weights, sizes=sizes))
    landed3 = out3[:1] + swaps(out3, "local", 1, last1)
    (tie,) = fence([tie], out3[:1])
    (out1,) = expert([arrived12], tie, *weights, block=0)

    out1, part2, part3, tie = fence([out1] + out3[-3:-1] + [tie], [landed0] + landed3[1:])
    landed1 = to_experts(out1)
    landed3 += [swap(part2, "local", last2), swap(part3, "local", last1)]
    (out2,) = expert([arrived12], tie, *weights, block=1)
    (mixing0,) = fence([mixing0], [out2])
    own0, parts0 = mix(mixing0, landed0)
    parts0 = swaps([None] + parts0, "local", 1, peers)

    out2, part3 = fence([out2, out3[-1]], [landed1, own0] + landed3[-2:])
    landed2 = to_experts(out2)
    landed3.append(swap(part3, "local", last1))
    own1, parts1 = mix(mixing1, landed1)
    (own0,) = fence([own0], parts1[:1])
    parts1 = swaps([None] + parts1, "local", 1, peers)
    cross = mix_cross(mixing3a, mixing3b, landed3)

    own2, parts2 = mix(mixing2, landed2)
    own1, *cross = fence([own1] + list(cross), parts2[:1])
    parts2 = swaps([None] + parts2, "local", 1, peers)
    sums3 = halve(*cross[:2], "node", bits_a[-1]), halve(*cross[2:], "node", bits_b[-1])
    (own2,) = fence([own2], [sums3[0]])
    piece0, piece1 = total(own0, parts0), total(own1, parts1)
    piece3 = [sum_halving(s, "node", bits[:-1]) for s, bits in zip(sums3, (bits_a, bits_b))]
    piece3 = jnp.concatenate(piece3, axis=1)
    piece2 = total(own2, parts2)
    return jnp.concatenate([piece0, piece1, piece2, piece3], axis=0)


def solution(mesh):
    rows = P(AXES, None)
    stacked = P(AXES, None, None)
    in_specs = (rows, P(), rows, rows, P(), stacked, stacked, stacked)
    return jax.shard_map(body, mesh=mesh, in_specs=in_specs, out_specs=rows, check_vma=False)
```

```python
import functools

import jax
import jax.numpy as jnp
import numpy as np
from jax import lax
from jax.experimental import pallas as pl
from jax.experimental.pallas import tpu as pltpu
from jax.sharding import PartitionSpec as P

BLOCK_TOK = 32
EPSILON = 1e-06
AXES = ("node", "local")
LANES = 128
TILES = 4
BF16, F32, I32 = jnp.bfloat16, jnp.float32, jnp.int32
ANYWHERE = pl.BlockSpec(memory_space=pl.ANY)
PARAMS = pltpu.CompilerParams(vmem_limit_bytes=60 * 2**20)


def fence(arrays, after):
    token = sum(a.reshape(-1, a.shape[-1])[:16, :LANES].astype(F32) for a in after)

    def kernel(*refs):
        pass

    return list(pl.pallas_call(
        kernel,
        out_shape=[jax.ShapeDtypeStruct(a.shape, a.dtype) for a in arrays],
        in_specs=[ANYWHERE] * (len(arrays) + 1),
        out_specs=[ANYWHERE] * len(arrays),
        input_output_aliases={i: i for i in range(len(arrays))},
    )(*arrays, token))


def swap(array, axis, bits):
    size = lax.axis_size(axis)
    return lax.ppermute(array, axis, [(i, i ^ bits) for i in range(size)])


def swaps(parts, axis, first, last):
    return [swap(parts[k], axis, k) for k in range(first, last)]


def bit_order(size, last_first):
    bits = [1 << i for i in range(size.bit_length() - 1)]
    return bits[:1] + bits[:0:-1] if last_first else bits


def chain_step(arrays, axis, step):
    size = lax.axis_size(axis)
    rightward = [(i, i + 1) for i in range(step - 1, size - 1)]
    leftward = [(size - 1 - i, size - 2 - i) for i in range(step - 1, size - 1)]
    return [lax.ppermute(a, axis, way) for a, way in zip(arrays, (rightward, leftward))]


def chain_offsets(size):
    return [0] + [offset for d in range(1, size) for offset in (-d, d)]


def gather_doubling(array, axis, bits):
    for bit in bits:
        array = jnp.concatenate([array, swap(array, axis, bit)])
    return array


def gathered_from(bits):
    found = [0]
    for bit in bits:
        found += [k ^ bit for k in found]
    return found


def halve(keep, give, axis, bit):
    return keep + swap(give.astype(BF16), axis, bit).astype(F32)


def sum_halving(array, axis, bits):
    for bit in bits[::-1]:
        array = halve(*jnp.split(array, 2), axis, bit)
    return array.astype(BF16)


def below(rows):
    at = np.arange(rows)
    same = at[:, None] // BLOCK_TOK == at[None, :] // BLOCK_TOK
    return (same & (at[None, :] < at[:, None])).astype(BF16)


def choose(table, lane, row_group, slot_group, turn, before):
    select = lax.broadcasted_iota(I32, (table.shape[1], lane.shape[1]), 0) == lane
    weight = jnp.dot(table, select.astype(BF16), preferred_element_type=F32)
    mask = jnp.where((weight > 0) & (row_group == slot_group), 1.0, 0.0)
    rank = jnp.dot(before, mask.astype(BF16), preferred_element_type=F32)
    place = jnp.where(rank == turn, mask, 0.0)
    return place.astype(BF16), (place * weight).astype(BF16)


def gather_rows(place, rows):
    return lax.dot_general(
        place, rows, (((0,), (0,)), ((), ())), preferred_element_type=F32
    ).astype(BF16)


def bits_of(labels, local, peers, chained):
    if not chained:
        return labels
    source = labels + local
    return jnp.where((source >= 0) & (source < peers), source ^ local, -1)


def pick_kernel(count, blocks, peers, chain_in, chain_out, ids, *refs):
    parts, refs = refs[:count], refs[count:]
    tables, refs = refs[:count], refs[count:]
    lane, slot_group, turn, before, in_column, in_row, out_column, out = refs[:8]
    mixings, places = refs[8 : 8 + blocks], refs[8 + blocks :]

    def rows_of(refs, block):
        return jnp.concatenate([r[block * BLOCK_TOK : (block + 1) * BLOCK_TOK] for r in refs])

    @pl.when(pl.program_id(0) == 0)
    def _():
        local = ids[1]
        row_group = bits_of(in_column[...], local, peers, chain_in)
        for block, (mixing, place) in enumerate(zip(mixings, places)):
            place[...], weights = choose(
                rows_of(tables, block),
                lane[...] + local,
                row_group,
                slot_group[...],
                turn[...],
                before[...],
            )
            if chain_in != chain_out:
                shape = mixing.shape[0], weights.shape[0]
                same = bits_of(out_column[...], local, peers, chain_out) == bits_of(
                    in_row[...], local, peers, chain_in
                )
                row = lax.broadcasted_iota(I32, shape, 0) & (BLOCK_TOK - 1)
                column = lax.broadcasted_iota(I32, shape, 1) & (BLOCK_TOK - 1)
                order = jnp.where(same & (row == column), 1.0, 0.0).astype(BF16)
                weights = jnp.dot(order, weights, preferred_element_type=F32).astype(BF16)
            mixing[...] = weights

    for block, place in enumerate(places):
        rows = lax.dot_general(
            place[...],
            rows_of(parts, block),
            (((0,), (0,)), ((), ())),
            preferred_element_type=F32,
        )
        nodes, _, size, tile = out.shape
        out[:, block] = rows.reshape(nodes, size, tile).astype(BF16)


def whole_block(array):
    return pl.BlockSpec(array.shape, lambda j: (0,) * array.ndim)


def by_token(labels):
    return np.repeat(np.array(labels, np.int32), BLOCK_TOK)


def pick(parts, ids, peers, capacity, features, chain_in, chain_out):
    nodes = lax.axis_size("node")
    held = parts[0].shape[0]
    blocks = held // BLOCK_TOK
    slots = nodes * peers * capacity
    slot = np.arange(slots, dtype=np.int32)[None, :]
    labels = chain_offsets(peers), list(range(peers))
    in_labels, out_labels = by_token(labels[not chain_in]), by_token(labels[not chain_out])
    rows, tile = len(in_labels), features // TILES
    small = (
        slot // (capacity * peers) * peers,
        slot // capacity % peers,
        (slot % capacity).astype(np.float32),
        below(rows),
        in_labels[:, None],
        in_labels[None, :],
        out_labels[:, None],
    )
    return pl.pallas_call(
        functools.partial(pick_kernel, len(parts), blocks, peers, chain_in, chain_out),
        grid=(TILES,),
        out_shape=[
            jax.ShapeDtypeStruct((nodes, blocks, peers * capacity, features), BF16),
        ]
        + [jax.ShapeDtypeStruct((len(out_labels), slots), BF16)] * blocks,
        in_specs=[pl.BlockSpec(memory_space=pltpu.SMEM)]
        + [pl.BlockSpec((held, tile), lambda j: (0, j))] * len(parts)
        + [pl.BlockSpec((held, LANES), lambda j: (0, features // LANES))] * len(parts)
        + [whole_block(a) for a in small],
        out_specs=[
            pl.BlockSpec((nodes, blocks, peers * capacity, tile), lambda j: (0, 0, 0, j)),
        ]
        + [pl.BlockSpec((len(out_labels), slots), lambda j: (0, 0))] * blocks,
        scratch_shapes=[pltpu.VMEM((rows, slots), BF16)] * blocks,
        compiler_params=PARAMS,
        cost_estimate=pl.CostEstimate(
            flops=2 * blocks * rows * slots * features,
            bytes_accessed=2 * blocks * (rows + slots) * features,
            transcendentals=0,
        ),
    )(ids, *parts, *parts, *small)


def pick_cross_kernel(order, cuts, peers, ids, a0, a1, b0, b1, t0, t1, *refs):
    peer, group_a, group_b, slot_group, turn, before = refs[:6]
    outs, (mixing_a, mixing_b, place_a, place_b) = refs[6:-4], refs[-4:]
    step = pl.program_id(0)

    @pl.when(step == 0)
    def _():
        known = jnp.concatenate([t0[...], t1[...]])
        lane = (peer[...] ^ ids[1]) + ids[0] * peers
        common = slot_group[...], turn[...], before[...]
        place_b[...], mixing_b[...] = choose(known, lane, group_b[...], *common)
        back = [order.index(k) * BLOCK_TOK for k in range(len(order))]
        known = jnp.concatenate([known[at : at + BLOCK_TOK] for at in back])
        place_a[...], mixing_a[...] = choose(known, lane, group_a[...], *common)

    def store(place, first_rows, last_rows):
        result = gather_rows(place[...], jnp.concatenate([first_rows[...], last_rows[...]]))
        for out, first, last in zip(outs, cuts[:-1], cuts[1:]):
            out[...] = result[first:last]

    @pl.when(step < TILES // 2)
    def _():
        store(place_a, a0, a1)

    @pl.when(step >= TILES // 2)
    def _():
        store(place_b, b0, b1)


def in_first_half(shape):
    return pl.BlockSpec(shape, lambda j: (0, jnp.minimum(j, TILES // 2 - 1)))


def in_second_half(shape):
    return pl.BlockSpec(shape, lambda j: (0, jnp.maximum(j - TILES // 2, 0)))


def pick_cross(rows_a, rows_b, order_a, order_b, ids, peers, capacity, features, cuts):
    part = rows_a[0].shape[0]
    rows = 2 * part
    nodes = rows // BLOCK_TOK
    slots = cuts[-1]
    slot = np.arange(slots, dtype=np.int32)[None, :]
    tile = features // TILES
    small = (
        slot // (capacity * nodes),
        by_token(order_a)[:, None],
        by_token(order_b)[:, None],
        slot // capacity % nodes,
        (slot % capacity).astype(np.float32),
        below(rows),
    )
    sizes = [last - first for first, last in zip(cuts[:-1], cuts[1:])]
    results = pl.pallas_call(
        functools.partial(pick_cross_kernel, order_b, cuts, peers),
        grid=(TILES,),
        out_shape=[jax.ShapeDtypeStruct((size, features), BF16) for size in sizes]
        + [jax.ShapeDtypeStruct((rows, slots), BF16)] * 2,
        in_specs=[pl.BlockSpec(memory_space=pltpu.SMEM)]
        + [in_first_half((part, tile))] * 2
        + [in_second_half((part, tile))] * 2
        + [pl.BlockSpec((part, LANES), lambda j: (0, features // 2 // LANES))] * 2
        + [whole_block(a) for a in small],
        out_specs=[pl.BlockSpec((size, tile), lambda j: (0, j)) for size in sizes]
        + [pl.BlockSpec((rows, slots), lambda j: (0, 0))] * 2,
        scratch_shapes=[pltpu.VMEM((rows, slots), BF16)] * 2,
        compiler_params=PARAMS,
        cost_estimate=pl.CostEstimate(
            flops=2 * rows * slots * features,
            bytes_accessed=2 * (rows + slots) * features,
            transcendentals=0,
        ),
    )(ids, *rows_a, *rows_b, *rows_b, *small)
    return list(results[:-2]), results[-2], results[-1]


def mix_kernel(mixing, landed, own, *outs):
    result = jnp.dot(mixing[...], landed[...], preferred_element_type=F32)
    own[...] = result[:BLOCK_TOK]
    for k, out in enumerate(outs):
        out[...] = result[(k + 1) * BLOCK_TOK : (k + 2) * BLOCK_TOK].astype(BF16)


def mix(mixing, landed):
    rows, slots = mixing.shape
    features = landed.shape[1]
    tile = features // TILES
    count = rows // BLOCK_TOK
    own, *parts = pl.pallas_call(
        mix_kernel,
        grid=(TILES,),
        out_shape=[jax.ShapeDtypeStruct((BLOCK_TOK, features), F32)]
        + [jax.ShapeDtypeStruct((BLOCK_TOK, features), BF16)] * (count - 1),
        in_specs=[whole_block(mixing), pl.BlockSpec((slots, tile), lambda j: (0, j))],
        out_specs=[pl.BlockSpec((BLOCK_TOK, tile), lambda j: (0, j))] * count,
        compiler_params=PARAMS,
        cost_estimate=pl.CostEstimate(
            flops=2 * rows * slots * features,
            bytes_accessed=2 * (rows + slots) * features,
            transcendentals=0,
        ),
    )(mixing, landed)
    return own, parts


def mix_cross_kernel(mixing_a, mixing_b, *refs):
    landed, (keep_a, give_a, keep_b, give_b) = refs[:-4], refs[-4:]
    step = pl.program_id(0)
    half = keep_a.shape[0]
    rows = jnp.concatenate([part[...] for part in landed])

    def store(mixing, keep, give):
        result = jnp.dot(mixing[...], rows, preferred_element_type=F32)
        keep[...] = result[:half]
        give[...] = result[half:].astype(BF16)

    @pl.when(step < TILES // 2)
    def _():
        store(mixing_a, keep_a, give_a)

    @pl.when(step >= TILES // 2)
    def _():
        store(mixing_b, keep_b, give_b)


def mix_cross(mixing_a, mixing_b, landed):
    rows, slots = mixing_a.shape
    features = landed[0].shape[1]
    tile = features // TILES
    shape = (rows // 2, features // 2)
    return pl.pallas_call(
        mix_cross_kernel,
        grid=(TILES,),
        out_shape=[jax.ShapeDtypeStruct(shape, F32), jax.ShapeDtypeStruct(shape, BF16)] * 2,
        in_specs=[whole_block(mixing_a), whole_block(mixing_b)]
        + [pl.BlockSpec((part.shape[0], tile), lambda j: (0, j)) for part in landed],
        out_specs=[in_first_half((rows // 2, tile))] * 2 + [in_second_half((rows // 2, tile))] * 2,
        compiler_params=PARAMS,
        cost_estimate=pl.CostEstimate(
            flops=2 * rows * slots * features,
            bytes_accessed=2 * (rows + slots) * features,
            transcendentals=0,
        ),
    )(mixing_a, mixing_b, *landed)


def expert_kernel(count, first_tiles, nodes, tie, *refs):
    parts, (gate_ref, up_ref, down_ref) = refs[:count], refs[count : count + 3]
    outs, (joined, hidden) = refs[count + 3 : -2], refs[-2:]
    step = pl.program_id(0)
    x_ref = parts[0] if count == 1 and not nodes else joined

    if x_ref is joined:

        @pl.when(step == 0)
        def _():
            pieces = [parts[0][n, 0] for n in range(nodes)] or [part[...] for part in parts]
            joined[...] = jnp.concatenate(pieces)

    @pl.when(step < first_tiles)
    def _():
        x = x_ref[...]
        gate_pre = jnp.dot(x, gate_ref[...], preferred_element_type=F32)
        up_pre = jnp.dot(x, up_ref[...], preferred_element_type=F32)
        hidden[step] = (gate_pre / (1 + jnp.exp(-gate_pre)) * up_pre).astype(BF16)

    @pl.when(step >= first_tiles)
    def _():
        rows = jnp.concatenate([hidden[i] for i in range(first_tiles)], axis=1)
        result = jnp.dot(rows, down_ref[...], preferred_element_type=F32)
        result = result.astype(BF16)
        at = 0
        for out in outs:
            out[...] = result[at : at + out.shape[0]]
            at += out.shape[0]


def expert(parts, tie, gate_weight, up_weight, down_weight, block=None, sizes=None):
    sizes = sizes or [part.shape[0] for part in parts]
    specs = [whole_block(part) for part in parts]
    nodes = 0
    if block is not None:
        nodes, _, size, features = parts[0].shape
        sizes = [nodes * size]
        specs = [pl.BlockSpec((nodes, 1, size, features), lambda i: (0, block, 0, 0))]
    rows = sum(sizes)
    features, hidden = gate_weight.shape
    tile = 256
    first_tiles = hidden // tile
    out_tile = features // TILES

    def first(i):
        return jnp.minimum(i, first_tiles - 1)

    def second(i):
        return jnp.maximum(i - first_tiles, 0)

    return pl.pallas_call(
        functools.partial(expert_kernel, len(parts), first_tiles, nodes),
        grid=(first_tiles + TILES,),
        out_shape=[jax.ShapeDtypeStruct((size, features), BF16) for size in sizes],
        in_specs=[pl.BlockSpec(memory_space=pltpu.SMEM)]
        + specs
        + [
            pl.BlockSpec((features, tile), lambda i: (0, first(i))),
            pl.BlockSpec((features, tile), lambda i: (0, first(i))),
            pl.BlockSpec((hidden, out_tile), lambda i: (0, second(i))),
        ],
        out_specs=[
            pl.BlockSpec((size, out_tile), lambda i: (0, second(i))) for size in sizes
        ],
        scratch_shapes=[
            pltpu.VMEM((rows if nodes or len(parts) > 1 else 16, features), BF16),
            pltpu.VMEM((first_tiles, rows, tile), BF16),
        ],
        compiler_params=PARAMS,
        cost_estimate=pl.CostEstimate(
            flops=6 * rows * features * hidden,
            bytes_accessed=6 * features * hidden + 4 * rows * features,
            transcendentals=rows * hidden,
        ),
    )(tie, *parts, gate_weight, up_weight, down_weight)


def prepare_kernel(tokens, gain, routes, gates, placement, *outs):
    experts = placement.shape[0]
    features = tokens.shape[1]
    chosen = gates[...] / jnp.sum(gates[...], axis=0, keepdims=True)
    columns = jnp.concatenate([routes[...].astype(F32), chosen]).T
    count = routes.shape[0]
    lanes = outs[0].shape[1] - features
    lane = lax.broadcasted_iota(I32, (1, lanes), 1)
    named = jnp.full((1, lanes), -1.0, F32)
    for e in range(experts):
        named = jnp.where(lane == e, placement[e].astype(F32), named)
    start = 0
    for out in outs:
        rows = out.shape[0]
        at = slice(start, start + rows)
        start += rows
        values = tokens[at].astype(F32)
        rescale = lax.rsqrt(jnp.mean(values * values, axis=-1, keepdims=True) + EPSILON)
        for c in range(features // LANES):
            to = slice(c * LANES, (c + 1) * LANES)
            out[:, to] = (values[:, to] * rescale * gain[c : c + 1].astype(F32)).astype(BF16)
        table = jnp.zeros((rows, lanes), F32)
        for k in range(count):
            held = columns[at, k : k + 1] == named
            table = jnp.where(held, columns[at, count + k : count + k + 1], table)
        out[:, features:] = table.astype(BF16)


def prepare(tokens, norm_gain, routes, route_gates, placement, sizes):
    features = tokens.shape[1]
    width = features + -(-placement.shape[0] // LANES) * LANES
    vmem = pl.BlockSpec(memory_space=pltpu.VMEM)
    return pl.pallas_call(
        prepare_kernel,
        out_shape=[jax.ShapeDtypeStruct((size, width), BF16) for size in sizes],
        in_specs=[vmem] * 4 + [pl.BlockSpec(memory_space=pltpu.SMEM)],
        compiler_params=PARAMS,
    )(tokens, norm_gain.reshape(-1, LANES), routes.T, route_gates.T, placement)


def to_experts(rows):
    return lax.all_to_all(rows, "node", 0, 0, tiled=True)


def total(own, parts):
    for part in parts:
        own = own + part.astype(F32)
    return own.astype(BF16)


def body(tokens, norm_gain, routes, route_gates, placement, gate_weight, up_weight, down_weight):
    nodes, peers = lax.axis_size("node"), lax.axis_size("local")
    node, local = lax.axis_index("node"), lax.axis_index("local")
    experts = placement.shape[0]
    features = tokens.shape[1]
    capacity = BLOCK_TOK * routes.shape[1] // experts * 3 // 2
    slots = experts * capacity
    half = features // 2
    weights = (gate_weight[0], up_weight[0], down_weight[0])
    sizes = [BLOCK_TOK, 2 * BLOCK_TOK, BLOCK_TOK]
    sent0, sent12, sent3 = prepare(tokens, norm_gain, routes, route_gates, placement, sizes)

    bits_a, bits_b = bit_order(nodes, False), bit_order(nodes, True)
    ids = jnp.stack([node, local]).astype(I32)
    near = ids, peers, capacity, features
    cuts = [slots // peers * k for k in range(peers + 1)]

    near0 = swaps([sent0] * peers, "local", 1, peers)
    pair = jnp.concatenate([sent3, swap(sent3, "node", bits_a[0])])
    rows_a = gather_doubling(pair[:, :half], "node", bits_a[1:-1])
    rows_b = gather_doubling(pair[:, half:], "node", bits_b[1:-1])
    sent12, rows_a, rows_b = fence([sent12, rows_a, rows_b], near0)
    rows_a = [rows_a, swap(rows_a, "node", bits_a[-1])]
    rows_b = [rows_b, swap(rows_b, "node", bits_b[-1])]
    chain = chain_step([sent12, sent12], "local", 1)
    outbound0, mixing0 = pick([sent0] + near0, *near, chain_in=False, chain_out=False)

    outbound0, *last_rows = fence([outbound0, rows_a[1], rows_b[1]], chain)
    arrived0 = to_experts(outbound0)
    parts12 = [sent12] + chain
    for step in range(2, peers):
        chain = chain_step(chain, "local", step)
        parts12 += chain
    outbound3, mixing3a, mixing3b = pick_cross(
        [rows_a[0], last_rows[0]],
        [rows_b[0], last_rows[1]],
        gathered_from(bits_a),
        gathered_from(bits_b),
        *near,
        cuts,
    )
    outbound12, mixing1, mixing2 = pick(parts12, *near, chain_in=True, chain_out=False)

    own3, *outbound3 = outbound3
    outbound12, *outbound3 = fence([outbound12] + outbound3, [arrived0])
    arrived12 = to_experts(outbound12)
    arrived3 = swaps([None] + outbound3, "local", 1, peers)
    (out0,) = expert([arrived0.reshape(slots, features)], ids, *weights)

    out0, tie = fence([out0, ids], [arrived12] + arrived3)
    landed0 = to_experts(out0)
    size = slots // peers
    sizes = [size] * (peers - 2) + [size // 2] * 4
    last2, last1 = peers - 2, peers - 1
    out3 = list(expert([own3] + arrived3, tie, *weights, sizes=sizes))
    landed3 = out3[:1] + swaps(out3, "local", 1, last1)
    (tie,) = fence([tie], out3[:1])
    (out1,) = expert([arrived12], tie, *weights, block=0)

    out1, part2, part3, tie = fence([out1] + out3[-3:-1] + [tie], [landed0] + landed3[1:])
    landed1 = to_experts(out1)
    landed3 += [swap(part2, "local", last2), swap(part3, "local", last1)]
    (out2,) = expert([arrived12], tie, *weights, block=1)
    (mixing0,) = fence([mixing0], [out2])
    own0, parts0 = mix(mixing0, landed0)
    parts0 = swaps([None] + parts0, "local", 1, peers)

    out2, part3 = fence([out2, out3[-1]], [landed1, own0] + landed3[-2:])
    landed2 = to_experts(out2)
    landed3.append(swap(part3, "local", last1))
    own1, parts1 = mix(mixing1, landed1)
    parts1 = swaps([None] + parts1, "local", 1, peers)
    cross = mix_cross(mixing3a, mixing3b, landed3)

    own2, parts2 = mix(mixing2, landed2)
    own0, own1, *cross = fence([own0, own1] + list(cross), parts2[:1])
    parts2 = swaps([None] + parts2, "local", 1, peers)
    sums3 = halve(*cross[:2], "node", bits_a[-1]), halve(*cross[2:], "node", bits_b[-1])
    (own2,) = fence([own2], [sums3[0]])
    piece0, piece1 = total(own0, parts0), total(own1, parts1)
    piece3 = [sum_halving(s, "node", bits[:-1]) for s, bits in zip(sums3, (bits_a, bits_b))]
    piece3 = jnp.concatenate(piece3, axis=1)
    piece2 = total(own2, parts2)
    return jnp.concatenate([piece0, piece1, piece2, piece3], axis=0)


def solution(mesh):
    rows = P(AXES, None)
    stacked = P(AXES, None, None)
    in_specs = (rows, P(), rows, rows, P(), stacked, stacked, stacked)
    return jax.shard_map(body, mesh=mesh, in_specs=in_specs, out_specs=rows, check_vma=False)
```

```python
import functools

import jax
import jax.numpy as jnp
import numpy as np
from jax import lax
from jax.experimental import pallas as pl
from jax.experimental.pallas import tpu as pltpu
from jax.sharding import PartitionSpec as P

BLOCK_TOK = 32
EPSILON = 1e-06
AXES = ("node", "local")
LANES = 128
TILES = 4
BF16, F32, I32 = jnp.bfloat16, jnp.float32, jnp.int32
ANYWHERE = pl.BlockSpec(memory_space=pl.ANY)
PARAMS = pltpu.CompilerParams(vmem_limit_bytes=60 * 2**20)


def fence(arrays, after):
    token = sum(a.reshape(-1, a.shape[-1])[:16, :LANES].astype(F32) for a in after)

    def kernel(*refs):
        pass

    return list(pl.pallas_call(
        kernel,
        out_shape=[jax.ShapeDtypeStruct(a.shape, a.dtype) for a in arrays],
        in_specs=[ANYWHERE] * (len(arrays) + 1),
        out_specs=[ANYWHERE] * len(arrays),
        input_output_aliases={i: i for i in range(len(arrays))},
    )(*arrays, token))


def swap(array, axis, bits):
    size = lax.axis_size(axis)
    return lax.ppermute(array, axis, [(i, i ^ bits) for i in range(size)])


def swaps(parts, axis, first, last):
    return [swap(parts[k], axis, k) for k in range(first, last)]


def bit_order(size, last_first):
    bits = [1 << i for i in range(size.bit_length() - 1)]
    return bits[:1] + bits[:0:-1] if last_first else bits


def chain_step(arrays, axis, step):
    size = lax.axis_size(axis)
    rightward = [(i, i + 1) for i in range(step - 1, size - 1)]
    leftward = [(size - 1 - i, size - 2 - i) for i in range(step - 1, size - 1)]
    return [lax.ppermute(a, axis, way) for a, way in zip(arrays, (rightward, leftward))]


def chain_offsets(size):
    return [0] + [offset for d in range(1, size) for offset in (-d, d)]


def gather_doubling(array, axis, bits):
    for bit in bits:
        array = jnp.concatenate([array, swap(array, axis, bit)])
    return array


def gathered_from(bits):
    found = [0]
    for bit in bits:
        found += [k ^ bit for k in found]
    return found


def halve(keep, give, axis, bit):
    return keep + swap(give.astype(BF16), axis, bit).astype(F32)


def sum_halving(array, axis, bits):
    for bit in bits[::-1]:
        array = halve(*jnp.split(array, 2), axis, bit)
    return array.astype(BF16)


def below(rows):
    at = np.arange(rows)
    same = at[:, None] // BLOCK_TOK == at[None, :] // BLOCK_TOK
    return (same & (at[None, :] < at[:, None])).astype(BF16)


def choose(table, lane, row_group, slot_group, turn, before):
    select = lax.broadcasted_iota(I32, (table.shape[1], lane.shape[1]), 0) == lane
    weight = jnp.dot(table, select.astype(BF16), preferred_element_type=F32)
    mask = jnp.where((weight > 0) & (row_group == slot_group), 1.0, 0.0)
    rank = jnp.dot(before, mask.astype(BF16), preferred_element_type=F32)
    place = jnp.where(rank == turn, mask, 0.0)
    return place.astype(BF16), (place * weight).astype(BF16)


def gather_rows(place, rows):
    return lax.dot_general(
        place, rows, (((0,), (0,)), ((), ())), preferred_element_type=F32
    ).astype(BF16)


def bits_of(labels, local, peers, chained):
    if not chained:
        return labels
    source = labels + local
    return jnp.where((source >= 0) & (source < peers), source ^ local, -1)


def pick_kernel(count, blocks, peers, chain_in, chain_out, ids, *refs):
    parts, refs = refs[:count], refs[count:]
    tables, refs = refs[:count], refs[count:]
    lane, slot_group, turn, before, in_column, in_row, out_column, out = refs[:8]
    mixings, places = refs[8 : 8 + blocks], refs[8 + blocks :]

    def rows_of(refs, block):
        return jnp.concatenate([r[block * BLOCK_TOK : (block + 1) * BLOCK_TOK] for r in refs])

    @pl.when(pl.program_id(0) == 0)
    def _():
        local = ids[1]
        row_group = bits_of(in_column[...], local, peers, chain_in)
        for block, (mixing, place) in enumerate(zip(mixings, places)):
            place[...], weights = choose(
                rows_of(tables, block),
                lane[...] + local,
                row_group,
                slot_group[...],
                turn[...],
                before[...],
            )
            if chain_in != chain_out:
                shape = mixing.shape[0], weights.shape[0]
                same = bits_of(out_column[...], local, peers, chain_out) == bits_of(
                    in_row[...], local, peers, chain_in
                )
                row = lax.broadcasted_iota(I32, shape, 0) & (BLOCK_TOK - 1)
                column = lax.broadcasted_iota(I32, shape, 1) & (BLOCK_TOK - 1)
                order = jnp.where(same & (row == column), 1.0, 0.0).astype(BF16)
                weights = jnp.dot(order, weights, preferred_element_type=F32).astype(BF16)
            mixing[...] = weights

    for block, place in enumerate(places):
        rows = lax.dot_general(
            place[...],
            rows_of(parts, block),
            (((0,), (0,)), ((), ())),
            preferred_element_type=F32,
        )
        nodes, _, size, tile = out.shape
        out[:, block] = rows.reshape(nodes, size, tile).astype(BF16)


def whole_block(array):
    return pl.BlockSpec(array.shape, lambda j: (0,) * array.ndim)


def by_token(labels):
    return np.repeat(np.array(labels, np.int32), BLOCK_TOK)


def pick(parts, ids, peers, capacity, features, chain_in, chain_out):
    nodes = lax.axis_size("node")
    held = parts[0].shape[0]
    blocks = held // BLOCK_TOK
    slots = nodes * peers * capacity
    slot = np.arange(slots, dtype=np.int32)[None, :]
    labels = chain_offsets(peers), list(range(peers))
    in_labels, out_labels = by_token(labels[not chain_in]), by_token(labels[not chain_out])
    rows, tile = len(in_labels), features // TILES
    small = (
        slot // (capacity * peers) * peers,
        slot // capacity % peers,
        (slot % capacity).astype(np.float32),
        below(rows),
        in_labels[:, None],
        in_labels[None, :],
        out_labels[:, None],
    )
    return pl.pallas_call(
        functools.partial(pick_kernel, len(parts), blocks, peers, chain_in, chain_out),
        grid=(TILES,),
        out_shape=[
            jax.ShapeDtypeStruct((nodes, blocks, peers * capacity, features), BF16),
        ]
        + [jax.ShapeDtypeStruct((len(out_labels), slots), BF16)] * blocks,
        in_specs=[pl.BlockSpec(memory_space=pltpu.SMEM)]
        + [pl.BlockSpec((held, tile), lambda j: (0, j))] * len(parts)
        + [pl.BlockSpec((held, LANES), lambda j: (0, features // LANES))] * len(parts)
        + [whole_block(a) for a in small],
        out_specs=[
            pl.BlockSpec((nodes, blocks, peers * capacity, tile), lambda j: (0, 0, 0, j)),
        ]
        + [pl.BlockSpec((len(out_labels), slots), lambda j: (0, 0))] * blocks,
        scratch_shapes=[pltpu.VMEM((rows, slots), BF16)] * blocks,
        compiler_params=PARAMS,
        cost_estimate=pl.CostEstimate(
            flops=2 * blocks * rows * slots * features,
            bytes_accessed=2 * blocks * (rows + slots) * features,
            transcendentals=0,
        ),
    )(ids, *parts, *parts, *small)


def pick_cross_kernel(order, cuts, peers, ids, a0, a1, b0, b1, t0, t1, *refs):
    peer, group_a, group_b, slot_group, turn, before = refs[:6]
    outs, (mixing_a, mixing_b, place_a, place_b) = refs[6:-4], refs[-4:]
    step = pl.program_id(0)

    @pl.when(step == 0)
    def _():
        known = jnp.concatenate([t0[...], t1[...]])
        lane = (peer[...] ^ ids[1]) + ids[0] * peers
        common = slot_group[...], turn[...], before[...]
        place_b[...], mixing_b[...] = choose(known, lane, group_b[...], *common)
        back = [order.index(k) * BLOCK_TOK for k in range(len(order))]
        known = jnp.concatenate([known[at : at + BLOCK_TOK] for at in back])
        place_a[...], mixing_a[...] = choose(known, lane, group_a[...], *common)

    def store(place, first_rows, last_rows):
        result = gather_rows(place[...], jnp.concatenate([first_rows[...], last_rows[...]]))
        for out, first, last in zip(outs, cuts[:-1], cuts[1:]):
            out[...] = result[first:last]

    @pl.when(step < TILES // 2)
    def _():
        store(place_a, a0, a1)

    @pl.when(step >= TILES // 2)
    def _():
        store(place_b, b0, b1)


def in_first_half(shape):
    return pl.BlockSpec(shape, lambda j: (0, jnp.minimum(j, TILES // 2 - 1)))


def in_second_half(shape):
    return pl.BlockSpec(shape, lambda j: (0, jnp.maximum(j - TILES // 2, 0)))


def pick_cross(rows_a, rows_b, order_a, order_b, ids, peers, capacity, features, cuts):
    part = rows_a[0].shape[0]
    rows = 2 * part
    nodes = rows // BLOCK_TOK
    slots = cuts[-1]
    slot = np.arange(slots, dtype=np.int32)[None, :]
    tile = features // TILES
    small = (
        slot // (capacity * nodes),
        by_token(order_a)[:, None],
        by_token(order_b)[:, None],
        slot // capacity % nodes,
        (slot % capacity).astype(np.float32),
        below(rows),
    )
    sizes = [last - first for first, last in zip(cuts[:-1], cuts[1:])]
    results = pl.pallas_call(
        functools.partial(pick_cross_kernel, order_b, cuts, peers),
        grid=(TILES,),
        out_shape=[jax.ShapeDtypeStruct((size, features), BF16) for size in sizes]
        + [jax.ShapeDtypeStruct((rows, slots), BF16)] * 2,
        in_specs=[pl.BlockSpec(memory_space=pltpu.SMEM)]
        + [in_first_half((part, tile))] * 2
        + [in_second_half((part, tile))] * 2
        + [pl.BlockSpec((part, LANES), lambda j: (0, features // 2 // LANES))] * 2
        + [whole_block(a) for a in small],
        out_specs=[pl.BlockSpec((size, tile), lambda j: (0, j)) for size in sizes]
        + [pl.BlockSpec((rows, slots), lambda j: (0, 0))] * 2,
        scratch_shapes=[pltpu.VMEM((rows, slots), BF16)] * 2,
        compiler_params=PARAMS,
        cost_estimate=pl.CostEstimate(
            flops=2 * rows * slots * features,
            bytes_accessed=2 * (rows + slots) * features,
            transcendentals=0,
        ),
    )(ids, *rows_a, *rows_b, *rows_b, *small)
    return list(results[:-2]), results[-2], results[-1]


def mix_kernel(mixing, landed, own, *outs):
    result = jnp.dot(mixing[...], landed[...], preferred_element_type=F32)
    own[...] = result[:BLOCK_TOK]
    for k, out in enumerate(outs):
        out[...] = result[(k + 1) * BLOCK_TOK : (k + 2) * BLOCK_TOK].astype(BF16)


def mix(mixing, landed):
    rows, slots = mixing.shape
    features = landed.shape[1]
    tile = features // TILES
    count = rows // BLOCK_TOK
    own, *parts = pl.pallas_call(
        mix_kernel,
        grid=(TILES,),
        out_shape=[jax.ShapeDtypeStruct((BLOCK_TOK, features), F32)]
        + [jax.ShapeDtypeStruct((BLOCK_TOK, features), BF16)] * (count - 1),
        in_specs=[whole_block(mixing), pl.BlockSpec((slots, tile), lambda j: (0, j))],
        out_specs=[pl.BlockSpec((BLOCK_TOK, tile), lambda j: (0, j))] * count,
        compiler_params=PARAMS,
        cost_estimate=pl.CostEstimate(
            flops=2 * rows * slots * features,
            bytes_accessed=2 * (rows + slots) * features,
            transcendentals=0,
        ),
    )(mixing, landed)
    return own, parts


def mix_cross_kernel(mixing_a, mixing_b, *refs):
    landed, (keep_a, give_a, keep_b, give_b) = refs[:-4], refs[-4:]
    step = pl.program_id(0)
    half = keep_a.shape[0]
    rows = jnp.concatenate([part[...] for part in landed])

    def store(mixing, keep, give):
        result = jnp.dot(mixing[...], rows, preferred_element_type=F32)
        keep[...] = result[:half]
        give[...] = result[half:].astype(BF16)

    @pl.when(step < TILES // 2)
    def _():
        store(mixing_a, keep_a, give_a)

    @pl.when(step >= TILES // 2)
    def _():
        store(mixing_b, keep_b, give_b)


def mix_cross(mixing_a, mixing_b, landed):
    rows, slots = mixing_a.shape
    features = landed[0].shape[1]
    tile = features // TILES
    shape = (rows // 2, features // 2)
    return pl.pallas_call(
        mix_cross_kernel,
        grid=(TILES,),
        out_shape=[jax.ShapeDtypeStruct(shape, F32), jax.ShapeDtypeStruct(shape, BF16)] * 2,
        in_specs=[whole_block(mixing_a), whole_block(mixing_b)]
        + [pl.BlockSpec((part.shape[0], tile), lambda j: (0, j)) for part in landed],
        out_specs=[in_first_half((rows // 2, tile))] * 2 + [in_second_half((rows // 2, tile))] * 2,
        compiler_params=PARAMS,
        cost_estimate=pl.CostEstimate(
            flops=2 * rows * slots * features,
            bytes_accessed=2 * (rows + slots) * features,
            transcendentals=0,
        ),
    )(mixing_a, mixing_b, *landed)


def expert_kernel(count, first_tiles, nodes, tie, *refs):
    parts, (gate_ref, up_ref, down_ref) = refs[:count], refs[count : count + 3]
    outs, (joined, hidden) = refs[count + 3 : -2], refs[-2:]
    step = pl.program_id(0)
    x_ref = parts[0] if count == 1 and not nodes else joined

    if x_ref is joined:

        @pl.when(step == 0)
        def _():
            pieces = [parts[0][n, 0] for n in range(nodes)] or [part[...] for part in parts]
            joined[...] = jnp.concatenate(pieces)

    @pl.when(step < first_tiles)
    def _():
        x = x_ref[...]
        gate_pre = jnp.dot(x, gate_ref[...], preferred_element_type=F32)
        up_pre = jnp.dot(x, up_ref[...], preferred_element_type=F32)
        hidden[step] = (gate_pre / (1 + jnp.exp(-gate_pre)) * up_pre).astype(BF16)

    @pl.when(step >= first_tiles)
    def _():
        rows = jnp.concatenate([hidden[i] for i in range(first_tiles)], axis=1)
        result = jnp.dot(rows, down_ref[...], preferred_element_type=F32)
        result = result.astype(BF16)
        at = 0
        for out in outs:
            out[...] = result[at : at + out.shape[0]]
            at += out.shape[0]


def expert(parts, tie, gate_weight, up_weight, down_weight, block=None, sizes=None):
    sizes = sizes or [part.shape[0] for part in parts]
    specs = [whole_block(part) for part in parts]
    nodes = 0
    if block is not None:
        nodes, _, size, features = parts[0].shape
        sizes = [nodes * size]
        specs = [pl.BlockSpec((nodes, 1, size, features), lambda i: (0, block, 0, 0))]
    rows = sum(sizes)
    features, hidden = gate_weight.shape
    tile = 256
    first_tiles = hidden // tile
    out_tile = features // TILES

    def first(i):
        return jnp.minimum(i, first_tiles - 1)

    def second(i):
        return jnp.maximum(i - first_tiles, 0)

    return pl.pallas_call(
        functools.partial(expert_kernel, len(parts), first_tiles, nodes),
        grid=(first_tiles + TILES,),
        out_shape=[jax.ShapeDtypeStruct((size, features), BF16) for size in sizes],
        in_specs=[pl.BlockSpec(memory_space=pltpu.SMEM)]
        + specs
        + [
            pl.BlockSpec((features, tile), lambda i: (0, first(i))),
            pl.BlockSpec((features, tile), lambda i: (0, first(i))),
            pl.BlockSpec((hidden, out_tile), lambda i: (0, second(i))),
        ],
        out_specs=[
            pl.BlockSpec((size, out_tile), lambda i: (0, second(i))) for size in sizes
        ],
        scratch_shapes=[
            pltpu.VMEM((rows if nodes or len(parts) > 1 else 16, features), BF16),
            pltpu.VMEM((first_tiles, rows, tile), BF16),
        ],
        compiler_params=PARAMS,
        cost_estimate=pl.CostEstimate(
            flops=6 * rows * features * hidden,
            bytes_accessed=6 * features * hidden + 4 * rows * features,
            transcendentals=rows * hidden,
        ),
    )(tie, *parts, gate_weight, up_weight, down_weight)


def prepare_kernel(tokens, gain, routes, gates, placement, *outs):
    experts = placement.shape[0]
    features = tokens.shape[1]
    chosen = gates[...] / jnp.sum(gates[...], axis=0, keepdims=True)
    columns = jnp.concatenate([routes[...].astype(F32), chosen]).T
    count = routes.shape[0]
    lanes = outs[0].shape[1] - features
    lane = lax.broadcasted_iota(I32, (1, lanes), 1)
    named = jnp.full((1, lanes), -1.0, F32)
    for e in range(experts):
        named = jnp.where(lane == e, placement[e].astype(F32), named)
    start = 0
    for out in outs:
        rows = out.shape[0]
        at = slice(start, start + rows)
        start += rows
        values = tokens[at].astype(F32)
        rescale = lax.rsqrt(jnp.mean(values * values, axis=-1, keepdims=True) + EPSILON)
        for c in range(features // LANES):
            to = slice(c * LANES, (c + 1) * LANES)
            out[:, to] = (values[:, to] * rescale * gain[c : c + 1].astype(F32)).astype(BF16)
        table = jnp.zeros((rows, lanes), F32)
        for k in range(count):
            held = columns[at, k : k + 1] == named
            table = jnp.where(held, columns[at, count + k : count + k + 1], table)
        out[:, features:] = table.astype(BF16)


def prepare(tokens, norm_gain, routes, route_gates, placement, sizes):
    features = tokens.shape[1]
    width = features + -(-placement.shape[0] // LANES) * LANES
    vmem = pl.BlockSpec(memory_space=pltpu.VMEM)
    return pl.pallas_call(
        prepare_kernel,
        out_shape=[jax.ShapeDtypeStruct((size, width), BF16) for size in sizes],
        in_specs=[vmem] * 4 + [pl.BlockSpec(memory_space=pltpu.SMEM)],
        compiler_params=PARAMS,
    )(tokens, norm_gain.reshape(-1, LANES), routes.T, route_gates.T, placement)


def to_experts(rows):
    return lax.all_to_all(rows, "node", 0, 0, tiled=True)


def total(own, parts):
    for part in parts:
        own = own + part.astype(F32)
    return own.astype(BF16)


def body(tokens, norm_gain, routes, route_gates, placement, gate_weight, up_weight, down_weight):
    nodes, peers = lax.axis_size("node"), lax.axis_size("local")
    node, local = lax.axis_index("node"), lax.axis_index("local")
    experts = placement.shape[0]
    features = tokens.shape[1]
    capacity = BLOCK_TOK * routes.shape[1] // experts * 3 // 2
    slots = experts * capacity
    half = features // 2
    weights = (gate_weight[0], up_weight[0], down_weight[0])
    sizes = [BLOCK_TOK, 2 * BLOCK_TOK, BLOCK_TOK]
    sent0, sent12, sent3 = prepare(tokens, norm_gain, routes, route_gates, placement, sizes)

    bits_a, bits_b = bit_order(nodes, False), bit_order(nodes, True)
    ids = jnp.stack([node, local]).astype(I32)
    near = ids, peers, capacity, features
    cuts = [slots // peers * k for k in range(peers + 1)]

    near0 = swaps([sent0] * peers, "local", 1, peers)
    pair = jnp.concatenate([sent3, swap(sent3, "node", bits_a[0])])
    rows_a = gather_doubling(pair[:, :half], "node", bits_a[1:-1])
    rows_b = gather_doubling(pair[:, half:], "node", bits_b[1:-1])
    sent12, rows_a, rows_b = fence([sent12, rows_a, rows_b], near0)
    rows_a = [rows_a, swap(rows_a, "node", bits_a[-1])]
    rows_b = [rows_b, swap(rows_b, "node", bits_b[-1])]
    chain = chain_step([sent12, sent12], "local", 1)
    outbound0, mixing0 = pick([sent0] + near0, *near, chain_in=False, chain_out=False)

    outbound0, *last_rows = fence([outbound0, rows_a[1], rows_b[1]], chain)
    arrived0 = to_experts(outbound0)
    parts12 = [sent12] + chain
    for step in range(2, peers):
        chain = chain_step(chain, "local", step)
        parts12 += chain
    outbound3, mixing3a, mixing3b = pick_cross(
        [rows_a[0], last_rows[0]],
        [rows_b[0], last_rows[1]],
        gathered_from(bits_a),
        gathered_from(bits_b),
        *near,
        cuts,
    )
    outbound12, mixing1, mixing2 = pick(parts12, *near, chain_in=True, chain_out=False)

    own3, *outbound3 = outbound3
    outbound12, *outbound3 = fence([outbound12] + outbound3, [arrived0])
    arrived12 = to_experts(outbound12)
    arrived3 = swaps([None] + outbound3, "local", 1, peers)
    (out0,) = expert([arrived0.reshape(slots, features)], ids, *weights)

    out0, tie = fence([out0, ids], [arrived12] + arrived3)
    landed0 = to_experts(out0)
    size = slots // peers
    sizes = [size] * (peers - 2) + [size * 2 // 3, size // 3, size - 16, 16]
    last2, last1 = peers - 2, peers - 1
    out3 = list(expert([own3] + arrived3, tie, *weights, sizes=sizes))
    landed3 = out3[:1] + swaps(out3, "local", 1, last1)
    (tie,) = fence([tie], out3[:1])
    (out1,) = expert([arrived12], tie, *weights, block=0)

    out1, part2, part3, tie = fence([out1] + out3[-3:-1] + [tie], [landed0] + landed3[1:])
    landed1 = to_experts(out1)
    landed3 += [swap(part2, "local", last2), swap(part3, "local", last1)]
    (out2,) = expert([arrived12], tie, *weights, block=1)
    (mixing0,) = fence([mixing0], [out2])
    own0, parts0 = mix(mixing0, landed0)
    parts0 = swaps([None] + parts0, "local", 1, peers)

    out2, part3 = fence([out2, out3[-1]], [landed1, own0] + landed3[-2:])
    landed2 = to_experts(out2)
    landed3.append(swap(part3, "local", last1))
    own1, parts1 = mix(mixing1, landed1)
    parts1 = swaps([None] + parts1, "local", 1, peers)
    cross = mix_cross(mixing3a, mixing3b, landed3)

    own2, parts2 = mix(mixing2, landed2)
    own0, own1, *cross = fence([own0, own1] + list(cross), parts2[:1])
    parts2 = swaps([None] + parts2, "local", 1, peers)
    sums3 = halve(*cross[:2], "node", bits_a[-1]), halve(*cross[2:], "node", bits_b[-1])
    piece0, piece1 = total(own0, parts0), total(own1, parts1)
    piece3 = [sum_halving(s, "node", bits[:-1]) for s, bits in zip(sums3, (bits_a, bits_b))]
    piece3 = jnp.concatenate(piece3, axis=1)
    piece2 = total(own2, parts2)
    return jnp.concatenate([piece0, piece1, piece2, piece3], axis=0)


def solution(mesh):
    rows = P(AXES, None)
    stacked = P(AXES, None, None)
    in_specs = (rows, P(), rows, rows, P(), stacked, stacked, stacked)
    return jax.shard_map(body, mesh=mesh, in_specs=in_specs, out_specs=rows, check_vma=False)
```
